32 devices in a mesh: pipe: 2 (over x), dp: 16 (over z, y, core).
Axes of the slice: x: 2, y: 2, z: 4, core: 2. Of those that a mesh axis runs over, the one named last changes fastest.
Arguments:
- frames: bfloat16 [2, 16, 384, 512], P(None, 'dp'), may hold values from -6 to 6
- cotangent: bfloat16 [2, 16, 384, 512], P(None, 'dp'), may hold values from -6 to 6
- lengths: int32 [2, 16], P(None, 'dp'), may hold values from 96 to 384, as said below
- stream_flags: int32 [2, 16], P(None, 'dp'), may hold values 0 or 1
- span_sizes: int32 [2, 16], P(None, 'dp'), may hold values from 24 to 96
- early_gain: bfloat16 [2, 512], P('pipe', 'dp'), may hold values from 0.25 to 1.75
- early_up: bfloat16 [2, 512, 2048], P('pipe', 'dp'), may hold values from -0.25 to 0.25
- early_down: bfloat16 [2, 2048, 512], P('pipe', None, 'dp'), may hold values from -0.125 to 0.125
- attend_gain: bfloat16 [2, 512], P('pipe', 'dp'), may hold values from 0.25 to 1.75
- attend_proj: bfloat16 [2, 512, 1536], P('pipe', 'dp'), may hold values from -0.25 to 0.25
- attend_out: bfloat16 [2, 512, 512], P('pipe', 'dp'), may hold values from -2 to 2
- convolve_gain: bfloat16 [2, 512], P('pipe', 'dp'), may hold values from 0.25 to 1.75
- convolve_in: bfloat16 [2, 512, 1024], P('pipe', 'dp'), may hold values from -0.25 to 0.25
- convolve_depth: bfloat16 [2, 15, 512], P('pipe', None, 'dp'), may hold values from -1.5 to 1.5
- convolve_norm: bfloat16 [2, 512], P('pipe', 'dp'), may hold values from 0.25 to 1.75
- convolve_out: bfloat16 [2, 512, 512], P('pipe', 'dp'), may hold values from -0.25 to 0.25
- late_gain: bfloat16 [2, 512], P('pipe', 'dp'), may hold values from 0.25 to 1.75
- late_up: bfloat16 [2, 512, 2048], P('pipe', 'dp'), may hold values from -0.25 to 0.25
- late_down: bfloat16 [2, 2048, 512], P('pipe', None, 'dp'), may hold values from -0.125 to 0.125
- final_gain: bfloat16 [2, 512], P('pipe', 'dp'), may hold values from 0.25 to 1.75
Outputs:
- layer_outputs: bfloat16 [2, 2, 16, 384, 512], P('pipe', None, 'dp')
- input_grads: bfloat16 [2, 2, 16, 384, 512], P('pipe', None, 'dp')
- grad_early_gain: float32 [2, 512], P('pipe', 'dp')
- grad_early_up: float32 [2, 512, 2048], P('pipe', 'dp')
- grad_early_down: float32 [2, 2048, 512], P('pipe', None, 'dp')
- grad_attend_gain: float32 [2, 512], P('pipe', 'dp')
- grad_attend_proj: float32 [2, 512, 1536], P('pipe', 'dp')
- grad_attend_out: float32 [2, 512, 512], P('pipe', 'dp')
- grad_convolve_gain: float32 [2, 512], P('pipe', 'dp')
- grad_convolve_in: float32 [2, 512, 1024], P('pipe', 'dp')
- grad_convolve_depth: float32 [2, 15, 512], P('pipe', None, 'dp')
- grad_convolve_norm: float32 [2, 512], P('pipe', 'dp')
- grad_convolve_out: float32 [2, 512, 512], P('pipe', 'dp')
- grad_late_gain: float32 [2, 512], P('pipe', 'dp')
- grad_late_up: float32 [2, 512, 2048], P('pipe', 'dp')
- grad_late_down: float32 [2, 2048, 512], P('pipe', None, 'dp')
- grad_final_gain: float32 [2, 512], P('pipe', 'dp')
The draws below stay inside these ranges and needn't reach their ends.
Inputs may be any that keep to these rules, and one draw needn't show every extreme that they name: micro-batch 0 holds lengths from 96 to 192, the others from 192 to 384; the shortest length, 96, and the longest, 384, occur in every draw.
All inputs are finite; a program needn't handle non-finite values. No bound on the sum of `stream_flags` on one device may be relied on, other than what follows from the above.
Results may differ from the reference program's by a relative error of at most 0.023.
Values may be sent and summed in bfloat16 or wider, within the bound.
A program may use at most 256 MiB of HBM per device.

```python
import math
import jax
import jax.numpy as jnp
from jax import lax

D = 512
FF = 2048
HEADS = 8
KERNEL = 15
MB = 2
LEN = 384
UTT = 16


def draw_lengths(key, part):
    shorter = jax.random.randint(jax.random.fold_in(key, 11), (1, UTT), LEN // 4, LEN // 2 + 1)
    longer = jax.random.randint(jax.random.fold_in(key, 12), (MB - 1, UTT), LEN // 2, LEN + 1)
    joined = jnp.concatenate([shorter, longer], axis=0)
    joined = joined.at[0, 0].set(LEN // 4)
    joined = joined.at[MB - 1, UTT - 1].set(LEN)
    return joined.astype(jnp.int32)


def with_ends(entries, rng, smallest, top_value):
    longest = entries.shape.index(max(entries.shape))
    spots = []
    for shift in (0, 1):
        where = [jax.random.randint(jax.random.fold_in(rng, axis), (), 0, length) for axis, length in enumerate(entries.shape)]
        where[longest] = (where[longest] + shift) % entries.shape[longest]
        spots.append(tuple(where))
    return entries.at[spots[0]].set(smallest).at[spots[1]].set(top_value)


def level_of(key, extent, cuts, low, largest):
    def one(position, blocks):
        draws = jax.random.uniform(jax.random.fold_in(jax.random.fold_in(key, 6), position), (blocks,), jnp.float32, low / len(cuts), largest / len(cuts))
        return jnp.repeat(jnp.exp(draws), extent[position] // blocks).reshape((-1,) + (1,) * (len(extent) - position - 1))

    gain = one(*cuts[0])
    for cut in cuts[1:]:
        gain = gain * one(*cut)
    return gain


def bell_draw(key, shape, deviation, most, pieces=(), kind=jnp.bfloat16):
    drawn = deviation * jax.random.normal(key, shape, jnp.float32)
    if pieces:
        drawn = drawn * level_of(key, shape, pieces, -0.22, 0.18)
    return jnp.clip(drawn, -most, most).astype(kind)


def setup_inputs(seed: int = 0) -> dict:
    streams_of = jax.random.split(jax.random.key(seed), 21)
    frames = bell_draw(streams_of[0], (MB, UTT, LEN, D), 1.0, 6.0, ((1, 16),))
    cotangent = bell_draw(streams_of[1], (MB, UTT, LEN, D), 1.0, 6.0, ((1, 16),))
    lengths = draw_lengths(jax.random.fold_in(streams_of[20], 71), 0)
    stream_flags = with_ends((jax.random.randint(streams_of[3], (MB, UTT), 0, 2) < 1).astype(jnp.int32), jax.random.fold_in(streams_of[3], 1), 0, 1)
    span_sizes = with_ends(jax.random.randint(streams_of[4], (MB, UTT), max(LEN // 16, 2), LEN // 4 + 1), jax.random.fold_in(streams_of[4], 1), max(LEN // 16, 2), (LEN // 4 + 1) - 1).astype(jnp.int32)
    early_gain = jnp.clip(1.0 + 0.15 * jax.random.normal(streams_of[5], (2, D), jnp.float32), 0.25, 1.75).astype(jnp.bfloat16)
    early_up = bell_draw(streams_of[6], (2, D, FF), D ** -0.5, 0.25, ((0, 2), (1, 16)))
    early_down = bell_draw(streams_of[7], (2, FF, D), FF ** -0.5, 0.125, ((0, 2), (2, 16)))
    attend_gain = jnp.clip(1.0 + 0.15 * jax.random.normal(streams_of[8], (2, D), jnp.float32), 0.25, 1.75).astype(jnp.bfloat16)
    attend_proj = bell_draw(streams_of[9], (2, D, 3 * D), D ** -0.5, 0.25, ((0, 2), (1, 16)))
    attend_out = bell_draw(streams_of[10], (2, D, D), (D // 64) ** -0.5, 2.0, ((0, 2), (1, 16)))
    convolve_gain = jnp.clip(1.0 + 0.15 * jax.random.normal(streams_of[11], (2, D), jnp.float32), 0.25, 1.75).astype(jnp.bfloat16)
    convolve_in = bell_draw(streams_of[12], (2, D, 2 * D), D ** -0.5, 0.25, ((0, 2), (1, 16)))
    convolve_depth = bell_draw(streams_of[13], (2, KERNEL, D), KERNEL ** -0.5, 1.5, ((0, 2), (2, 16)))
    convolve_norm = jnp.clip(1.0 + 0.15 * jax.random.normal(streams_of[14], (2, D), jnp.float32), 0.25, 1.75).astype(jnp.bfloat16)
    convolve_out = bell_draw(streams_of[15], (2, D, D), D ** -0.5, 0.25, ((0, 2), (1, 16)))
    late_gain = jnp.clip(1.0 + 0.15 * jax.random.normal(streams_of[16], (2, D), jnp.float32), 0.25, 1.75).astype(jnp.bfloat16)
    late_up = bell_draw(streams_of[17], (2, D, FF), D ** -0.5, 0.25, ((0, 2), (1, 16)))
    late_down = bell_draw(streams_of[18], (2, FF, D), FF ** -0.5, 0.125, ((0, 2), (2, 16)))
    final_gain = jnp.clip(1.0 + 0.15 * jax.random.normal(streams_of[19], (2, D), jnp.float32), 0.25, 1.75).astype(jnp.bfloat16)
    return dict(frames=frames, cotangent=cotangent, lengths=lengths, stream_flags=stream_flags, span_sizes=span_sizes, early_gain=early_gain, early_up=early_up, early_down=early_down, attend_gain=attend_gain, attend_proj=attend_proj, attend_out=attend_out, convolve_gain=convolve_gain, convolve_in=convolve_in, convolve_depth=convolve_depth, convolve_norm=convolve_norm, convolve_out=convolve_out, late_gain=late_gain, late_up=late_up, late_down=late_down, final_gain=final_gain)


@jax.custom_vjp
def low(v):
    return lax.optimization_barrier(v.astype(jnp.bfloat16)).astype(jnp.float32)

@jax.custom_vjp
def low_back(v):
    return v

def low_keep(v):
    return (low(v), None)

def low_pass(kept, grad):
    return (grad,)

def back_keep(v):
    return (v, None)

def back_low(kept, grad):
    return (low(grad),)
low.defvjp(low_keep, low_pass)
low_back.defvjp(back_keep, back_low)
EPSILON = 1e-05
HIGHEST = lax.Precision.HIGHEST

def layer_norm(values, scales):
    center = values - lax.optimization_barrier(jnp.mean(values, axis=-1, keepdims=True))
    spread = lax.optimization_barrier(jnp.mean(center * center, axis=-1, keepdims=True))
    return center * lax.rsqrt(spread + EPSILON) * scales

def rotary_tables(frame_count, head_size):
    half_size = head_size // 2
    rates = jnp.exp(jnp.arange(half_size).astype(jnp.float32) * (-2.0 * math.log(10000.0) / head_size))
    phases = jnp.arange(frame_count).astype(jnp.float32)[:, None] * rates[None, :]
    return (jnp.cos(phases)[:, None, :], jnp.sin(phases)[:, None, :])

def rotate(values, cosine, sine_table):
    half_size = values.shape[-1] // 2
    front = values[..., :half_size]
    behind = values[..., half_size:]
    return jnp.concatenate([front * cosine - behind * sine_table, front * sine_table + behind * cosine], axis=-1)

def matmul(left, right):
    return jnp.dot(left, right, precision=HIGHEST)

def feed_forward(stream, scales, up_matrix, down_matrix):
    normed = low(layer_norm(stream, scales))
    inner = low_back(matmul(normed, up_matrix))
    hidden = low(jax.nn.silu(inner))
    return low_back(matmul(hidden, down_matrix))

def conformer_layer(stream, weights, length, stream_flag, span_size):
    early_gain, early_up, early_down, attend_gain, attend_proj, attend_out, convolve_gain, convolve_in, convolve_depth, convolve_norm, convolve_out, late_gain, late_up, late_down, final_gain = weights
    frame_count, channels = stream.shape
    head_size = channels // HEADS
    stream = stream + 0.5 * feed_forward(stream, early_gain, early_up, early_down)
    normed = low(layer_norm(stream, attend_gain))
    projected = low_back(matmul(normed, attend_proj)).reshape(frame_count, 3, HEADS, head_size)
    cosine, sine_table = rotary_tables(frame_count, head_size)
    queries = low(rotate(projected[:, 0], cosine, sine_table))
    key_rows = low(rotate(projected[:, 1], cosine, sine_table))
    value_rows = low(projected[:, 2])
    scores = low_back(jnp.einsum('ihd,jhd->hij', queries, key_rows, precision=HIGHEST) * head_size ** (-0.5))
    places = jnp.arange(frame_count).astype(jnp.int32)
    visible = (places[None, :] < length) & ((stream_flag == 0) | (places[None, :] // span_size <= places[:, None] // span_size))
    scores = jnp.where(visible[None], scores, -1e+30)
    powers = jnp.exp(scores - lax.optimization_barrier(jnp.max(scores, axis=-1, keepdims=True)))
    soft_weights = powers / lax.optimization_barrier(jnp.sum(powers, axis=-1, keepdims=True))
    context = jnp.einsum('hij,jhd->ihd', low(soft_weights), value_rows, precision=HIGHEST)
    context = low(low_back(context)).reshape(frame_count, channels)
    stream = stream + low_back(matmul(context, attend_out))
    live_rows = (places < length).astype(stream.dtype)[:, None]
    normed = low(layer_norm(stream, convolve_gain))
    gates = low_back(matmul(normed, convolve_in))
    glu_out = gates[:, :channels] * jax.nn.sigmoid(gates[:, channels:]) * live_rows
    tap_index = jnp.arange(KERNEL).astype(jnp.int32)
    tap_live = ((stream_flag == 0) | (tap_index <= KERNEL // 2)).astype(stream.dtype)[:, None]
    depth_taps = convolve_depth * tap_live
    padded = jnp.pad(glu_out, ((KERNEL // 2, KERNEL // 2), (0, 0)))
    mixed = jnp.zeros_like(glu_out)
    for offset in range(KERNEL):
        mixed = mixed + depth_taps[offset] * padded[offset:offset + frame_count]
    hidden = low(jax.nn.silu(layer_norm(mixed, convolve_norm)))
    stream = stream + low_back(matmul(hidden, convolve_out))
    stream = stream + 0.5 * feed_forward(stream, late_gain, late_up, late_down)
    return layer_norm(stream, final_gain)

def reference(frames, cotangent, lengths, stream_flags, span_sizes, early_gain, early_up, early_down, attend_gain, attend_proj, attend_out, convolve_gain, convolve_in, convolve_depth, convolve_norm, convolve_out, late_gain, late_up, late_down, final_gain):
    stacked = tuple((piece.astype(jnp.float32) for piece in (early_gain, early_up, early_down, attend_gain, attend_proj, attend_out, convolve_gain, convolve_in, convolve_depth, convolve_norm, convolve_out, late_gain, late_up, late_down, final_gain)))
    first_layer = tuple((piece[0] for piece in stacked))
    second_layer = tuple((piece[1] for piece in stacked))
    micro_count, utter_count, frame_count, channels = frames.shape
    group_size = 8
    groups = micro_count * utter_count // group_size
    inputs_all = frames.astype(jnp.float32).reshape(groups, group_size, frame_count, channels)
    seeds_all = cotangent.astype(jnp.float32).reshape(groups, group_size, frame_count, channels)
    lengths_all = lengths.reshape(groups, group_size)
    flags_all = stream_flags.reshape(groups, group_size)
    spans_all = span_sizes.reshape(groups, group_size)
    first_zero = tuple((jnp.zeros_like(piece) for piece in first_layer))
    second_zero = tuple((jnp.zeros_like(piece) for piece in second_layer))

    def group_step(carry, item):
        first_total, second_total = carry
        group_inputs, group_seeds, group_lengths, group_flags, group_spans = item

        def run_layer(stream, weights):
            return jax.vmap(conformer_layer, in_axes=(0, None, 0, 0, 0))(stream, weights, group_lengths, group_flags, group_spans)
        middle, first_back = jax.vjp(run_layer, group_inputs, first_layer)
        middle = low(middle)
        result, second_back = jax.vjp(run_layer, middle, second_layer)
        middle_grad, second_grads = second_back(group_seeds)
        middle_grad = low(middle_grad)
        input_grad, first_grads = first_back(middle_grad)
        first_total = jax.tree.map(jnp.add, first_total, first_grads)
        second_total = jax.tree.map(jnp.add, second_total, second_grads)
        return ((first_total, second_total), (middle, result, input_grad, middle_grad))
    (first_total, second_total), (middles, results, input_all, middle_all) = lax.scan(group_step, (first_zero, second_zero), (inputs_all, seeds_all, lengths_all, flags_all, spans_all))
    shape_out = (micro_count, utter_count, frame_count, channels)
    layer_outputs = jnp.stack([middles.reshape(shape_out), results.reshape(shape_out)]).astype(jnp.bfloat16)
    input_grads = jnp.stack([input_all.reshape(shape_out), middle_all.reshape(shape_out)]).astype(jnp.bfloat16)
    grads = tuple((jnp.stack([one, two]) for one, two in zip(first_total, second_total)))
    return (layer_outputs, input_grads, grads[0], grads[1], grads[2], grads[3], grads[4], grads[5], grads[6], grads[7], grads[8], grads[9], grads[10], grads[11], grads[12], grads[13], grads[14])
```

```python
import functools
import math

import jax
import jax.numpy as jnp
import numpy as np
from jax import lax
from jax.experimental import pallas as pl
from jax.experimental.pallas import tpu as pltpu
from jax.sharding import PartitionSpec as P

HEADS = 8
KERNEL = 15
EPSILON = 1e-05
LOW = jnp.bfloat16
F32 = jnp.float32

EU, ED, PJ, AO, CI, CO, LU, LD, SM = 0, 2048, 4096, 5632, 6144, 7168, 7680, 9728, 11776
COLS = 11904
STEP = 512
G_EARLY, G_ATTEND, G_CONV, G_MIX, G_LATE, G_FINAL, TAPS = 0, 1, 2, 3, 4, 5, 6


def dot(left, right):
    return lax.dot_general(left, right, (((1,), (0,)), ((), ())), preferred_element_type=F32)


def dot_t(left, right):
    return lax.dot_general(left, right, (((1,), (1,)), ((), ())), preferred_element_type=F32)


def sigmoid(values):
    return 0.5 * jnp.tanh(0.5 * values) + 0.5


def norm_hat(values):
    center = values - jnp.mean(values, axis=-1, keepdims=True)
    rate = lax.rsqrt(jnp.mean(center * center, axis=-1, keepdims=True) + EPSILON)
    return center * rate, rate


def norm_grad(grad_hat, hat, rate):
    first = jnp.mean(grad_hat, axis=-1, keepdims=True)
    second = jnp.mean(grad_hat * hat, axis=-1, keepdims=True)
    return rate * (grad_hat - first - hat * second)


class Layer:
    def __init__(self, refs, emit):
        self.__dict__.update(refs)
        self.emit = emit

    def gain(self, l, row):
        return self.sm[l, row : row + 1, :]

    def weight(self, l, column, size=STEP):
        return self.w[l, :, column : column + size]

    def enter(self, l, site, row):
        values = self.stream[...]
        hat, rate = norm_hat(values)
        self.xh[l, site] = hat.astype(LOW)
        self.rate[l, :, site : site + 1] = rate
        return (hat * self.gain(l, row)).astype(LOW)

    def leave(self, l, site, row, grad):
        hat = self.xh[l, site].astype(F32)
        rate = self.rate[l, :, site : site + 1]
        self.smg[l, row : row + 1, :] = jnp.sum(grad * hat, axis=0, keepdims=True)
        return norm_grad(grad * self.gain(l, row), hat, rate)

    def small_forward(self, l):
        block = self.w[l, :, SM : SM + 128].astype(F32)
        self.sm[l] = block.T[:32]

    def small_backward(self, l):
        self.emit(l, SM, self.smg[l].T)

    def feed_forward(self, l, site, row, place, up, down):
        normed = self.enter(l, site, row)
        self.at[l, place] = normed.T
        side = 0 if site == 0 else 1
        total = None
        for j in range(0, 2048, STEP):
            inner = dot(normed, self.weight(l, up + j))
            self.u[l, side, :, j : j + STEP] = inner.astype(LOW)
            hidden = (inner * sigmoid(inner)).astype(LOW)
            term = dot_t(hidden, self.weight(l, down + j))
            total = term if total is None else total + term
        self.stream[...] += 0.5 * total

    def feed_backward(self, l, site, row, place, up, down):
        branch = (0.5 * self.grad[...]).astype(LOW)
        turned = branch.T
        side = 0 if site == 0 else 1
        total = None
        for j in range(0, 2048, STEP):
            hidden_grad = dot(branch, self.weight(l, down + j))
            inner = self.u[l, side, :, j : j + STEP].astype(F32)
            gate = sigmoid(inner)
            hidden = inner * gate
            inner_grad = (hidden_grad * (gate + hidden * (1.0 - gate))).astype(LOW)
            self.emit(l, down + j, dot(turned, hidden.astype(LOW)))
            self.emit(l, up + j, dot(self.at[l, place], inner_grad))
            term = dot_t(inner_grad, self.weight(l, up + j))
            total = term if total is None else total + term
        self.grad[...] += self.leave(l, site, row, total)

    def rotate(self, values, sign):
        cosine, sine = self.cos[...], self.sin[...]
        if sign < 0:
            sine = -sine
        parts = []
        for g in range(0, 512, 256):
            front, behind = values[:, g : g + 128], values[:, g + 128 : g + 256]
            parts += [front * cosine - behind * sine, front * sine + behind * cosine]
        return parts

    def pair_mask(self, j):
        lane = lax.broadcasted_iota(jnp.int32, (1, 256), 1)
        return (lane % 128) // 32 == j

    def head_mask(self, j):
        lane = lax.broadcasted_iota(jnp.int32, (1, 256), 1)
        return lane // 64 == j

    def attend_forward(self, l):
        normed = self.enter(l, 1, G_ATTEND)
        self.at[l, 1] = normed.T
        for which, scale in ((0, 0.125), (1, 1.0)):
            parts = self.rotate(dot(normed, self.weight(l, PJ + 512 * which)), 1)
            for i, part in enumerate(parts):
                self.qkv[l, which, :, 128 * i : 128 * i + 128] = part.astype(LOW) * LOW(scale)
        self.kt[l] = self.qkv[l, 1].T
        value_rows = dot(normed, self.weight(l, PJ + 1024)).astype(LOW)
        self.qkv[l, 2] = value_rows
        self.vt[...] = value_rows.T
        for h in range(HEADS):
            g, j = h // 4 * 256, h % 4
            keys = self.qkv[l, 1, :, g : g + 256]
            keys = jnp.where(self.pair_mask(j), keys, jnp.zeros_like(keys))
            scores = dot_t(keys, self.qkv[l, 0, :, g : g + 256]) + self.bias[...]
            powers = jnp.exp(scores - jnp.max(scores, axis=0, keepdims=True))
            powers = powers * (1.0 / jnp.sum(powers, axis=0, keepdims=True))
            powers = powers.astype(LOW)
            self.pt[l, h] = powers
            self.ot[l, 64 * h : 64 * h + 64, :] = dot(
                self.vt[64 * h : 64 * h + 64, :], powers
            ).astype(LOW)
        self.stream[...] += dot(self.ot[l].T, self.weight(l, AO))

    def attend_backward(self, l):
        branch = self.grad[...].astype(LOW)
        self.emit(l, AO, dot(self.ot[l], branch))
        self.ctx[...] = dot_t(branch, self.weight(l, AO)).astype(LOW)
        key_total, value_total = [], []
        for g in range(0, 512, 256):
            ctx = self.ctx[:, g : g + 256]
            queries = self.qkv[l, 0, :, g : g + 256]
            values = self.qkv[l, 2, :, g : g + 256]
            key_grad = value_grad = None
            for j in range(4):
                h = g // 64 + j
                head = self.head_mask(j)
                soft_grad = dot_t(jnp.where(head, values, jnp.zeros_like(values)), ctx)
                soft_low = self.pt[l, h]
                soft = soft_low.astype(F32)
                delta = jnp.sum(soft_grad * soft, axis=0, keepdims=True)
                score_grad = (soft * (soft_grad - delta)).astype(LOW)
                term = dot(soft_low, jnp.where(head, ctx, jnp.zeros_like(ctx)))
                value_grad = term if value_grad is None else value_grad + term
                term = dot(
                    score_grad, jnp.where(self.pair_mask(j), queries, jnp.zeros_like(queries))
                )
                key_grad = term if key_grad is None else key_grad + term
                front, behind = g + 32 * j, g + 128 + 32 * j
                rows = jnp.concatenate(
                    [self.kt[l, front : front + 32, :], self.kt[l, behind : behind + 32, :]], axis=0
                )
                turned = dot(rows, score_grad)
                self.qt[front : front + 32, :] = turned[:32]
                self.qt[behind : behind + 32, :] = turned[32:]
            key_total.append(key_grad)
            value_total.append(value_grad)
        query_grad = self.qt[...].T * 0.125
        query_grad = jnp.concatenate(self.rotate(query_grad, -1), axis=1).astype(LOW)
        key_grad = jnp.concatenate(key_total, axis=1)
        key_grad = jnp.concatenate(self.rotate(key_grad, -1), axis=1).astype(LOW)
        value_grad = jnp.concatenate(value_total, axis=1).astype(LOW)
        total = None
        for i, part in enumerate((query_grad, key_grad, value_grad)):
            self.emit(l, PJ + 512 * i, dot(self.at[l, 1], part))
            term = dot_t(part, self.weight(l, PJ + 512 * i))
            total = term if total is None else total + term
        self.grad[...] += self.leave(l, 1, G_ATTEND, total)

    def tap(self, l, k):
        row = self.sm[l, TAPS + k : TAPS + k + 1, :]
        return row if k <= KERNEL // 2 else row * self.whole

    def convolve_forward(self, l):
        normed = self.enter(l, 2, G_CONV)
        self.at[l, 2] = normed.T
        first = dot(normed, self.weight(l, CI))
        second = dot(normed, self.weight(l, CI + 512))
        self.gates[l, :, :512] = first.astype(LOW)
        self.gates[l, :, 512:] = second.astype(LOW)
        n = first.shape[0]
        self.pad[0, 8 : n + 8, :] = first * sigmoid(second) * self.live[...]
        mixed = None
        for k in range(KERNEL):
            term = self.tap(l, k) * self.pad[0, k + 1 : k + 1 + n, :]
            mixed = term if mixed is None else mixed + term
        hat, rate = norm_hat(mixed)
        self.xh[l, 5] = hat.astype(LOW)
        self.rate[l, :, 5:6] = rate
        inner = hat * self.gain(l, G_MIX)
        hidden = (inner * sigmoid(inner)).astype(LOW)
        self.wt[l] = hidden.T
        self.stream[...] += dot(hidden, self.weight(l, CO))

    def convolve_backward(self, l):
        branch = self.grad[...].astype(LOW)
        n = branch.shape[0]
        self.emit(l, CO, dot(self.wt[l], branch))
        hidden_grad = dot_t(branch, self.weight(l, CO))
        hat = self.xh[l, 5].astype(F32)
        inner = hat * self.gain(l, G_MIX)
        gate = sigmoid(inner)
        inner_grad = hidden_grad * (gate + inner * gate * (1.0 - gate))
        self.pad[1, 8 : n + 8, :] = self.leave(l, 5, G_MIX, inner_grad)
        first = self.gates[l, :, :512].astype(F32)
        gate = sigmoid(self.gates[l, :, 512:].astype(F32))
        self.pad[0, 8 : n + 8, :] = first * gate * self.live[...]
        mixed_grad = self.pad[1, 8 : n + 8, :]
        total = None
        for k in range(KERNEL):
            row = jnp.sum(mixed_grad * self.pad[0, k + 1 : k + 1 + n, :], axis=0, keepdims=True)
            if k > KERNEL // 2:
                row = row * self.whole
            self.smg[l, TAPS + k : TAPS + k + 1, :] = row
            term = self.tap(l, k) * self.pad[1, 15 - k : 15 - k + n, :]
            total = term if total is None else total + term
        total = total * self.live[...]
        first_grad = (total * gate).astype(LOW)
        second_grad = (total * first * gate * (1.0 - gate)).astype(LOW)
        self.emit(l, CI, dot(self.at[l, 2], first_grad))
        self.emit(l, CI + 512, dot(self.at[l, 2], second_grad))
        total = dot_t(first_grad, self.weight(l, CI))
        total = total + dot_t(second_grad, self.weight(l, CI + 512))
        self.grad[...] += self.leave(l, 2, G_CONV, total)

    def prepare(self, length, flag, span):
        n = self.stream.shape[0]
        key = lax.broadcasted_iota(jnp.int32, (n, n), 0)
        query = lax.broadcasted_iota(jnp.int32, (n, n), 1)
        width = span.astype(F32)
        key_block = jnp.floor((key.astype(F32) + 0.5) / width)
        query_block = jnp.floor((query.astype(F32) + 0.5) / width)
        shown = (key < length) & ((flag == 0) | (key_block <= query_block))
        self.bias[...] = jnp.where(shown, 0.0, -1e30)
        place = lax.broadcasted_iota(jnp.int32, (n, 1), 0)
        self.live[...] = (place < length).astype(F32)
        self.whole = jnp.where(flag == 0, 1.0, 0.0)
        self.pad[...] = jnp.zeros_like(self.pad)
        self.smg[...] = jnp.zeros_like(self.smg)

    def finish_forward(self, l):
        hat, rate = norm_hat(self.stream[...])
        self.xh[l, 4] = hat.astype(LOW)
        self.rate[l, :, 4:5] = rate
        return (hat * self.gain(l, G_FINAL)).astype(LOW)


def act_shapes(n):
    return dict(
        w=pltpu.VMEM((2, 512, COLS), LOW),
        stream=pltpu.VMEM((n, 512), F32),
        grad=pltpu.VMEM((n, 512), F32),
        xh=pltpu.VMEM((2, 6, n, 512), LOW),
        rate=pltpu.VMEM((2, n, 128), F32),
        at=pltpu.VMEM((2, 4, 512, n), LOW),
        u=pltpu.VMEM((2, 2, n, 2048), LOW),
        qkv=pltpu.VMEM((2, 3, n, 512), LOW),
        kt=pltpu.VMEM((2, 512, n), LOW),
        vt=pltpu.VMEM((512, n), LOW),
        qt=pltpu.VMEM((512, n), F32),
        ctx=pltpu.VMEM((n, 512), LOW),
        pt=pltpu.VMEM((2, HEADS, n, n), LOW),
        ot=pltpu.VMEM((2, 512, n), LOW),
        gates=pltpu.VMEM((2, n, 1024), LOW),
        wt=pltpu.VMEM((2, 512, n), LOW),
        pad=pltpu.VMEM((2, n + 16, 512), F32),
        sm=pltpu.VMEM((2, 32, 512), F32),
        smg=pltpu.VMEM((2, 128, 512), F32),
        bias=pltpu.VMEM((n, n), F32),
        live=pltpu.VMEM((n, 1), F32),
    )


def compute_kernel(names, scalars, w_hbm, frames, cotangent, cos, sin, y_out, dx_out, g_out, *scratch):
    refs = dict(zip(names, scratch))
    slots, slot_sem, load_sem = scratch[len(names) :]
    refs.update(cos=cos, sin=sin)
    pending = [None, None]
    count = [0]

    def emit(l, column, value):
        slot = count[0] % 2
        count[0] += 1
        if pending[slot] is not None:
            pending[slot].wait()
        width = value.shape[1]
        slots[slot, :, :width] = value.astype(LOW)
        copy = pltpu.make_async_copy(
            slots.at[slot, :, pl.ds(0, width)],
            g_out.at[l, :, pl.ds(column, width)],
            slot_sem.at[slot],
        )
        copy.start()
        pending[slot] = copy

    run = Layer(refs, emit)
    loads = [pltpu.make_async_copy(w_hbm.at[l], run.w.at[l], load_sem.at[l]) for l in range(2)]
    for load in loads:
        load.start()
    run.prepare(scalars[0], scalars[1], scalars[2])
    run.stream[...] = frames[...].astype(F32)
    for l in range(2):
        loads[l].wait()
        run.small_forward(l)
        run.feed_forward(l, 0, G_EARLY, 0, EU, ED)
        run.attend_forward(l)
        run.convolve_forward(l)
        run.feed_forward(l, 3, G_LATE, 3, LU, LD)
        result = run.finish_forward(l)
        y_out[l] = result
        if l == 0:
            run.stream[...] = result.astype(F32)
    for l in (1, 0):
        start = cotangent[...].astype(F32) if l == 1 else run.grad[...].astype(LOW).astype(F32)
        run.grad[...] = run.leave(l, 4, G_FINAL, start)
        run.feed_backward(l, 3, G_LATE, 3, LU, LD)
        run.convolve_backward(l)
        run.attend_backward(l)
        run.feed_backward(l, 0, G_EARLY, 0, EU, ED)
        run.small_backward(l)
        dx_out[l] = run.grad[...].astype(LOW)
    for copy in pending:
        copy.wait()


def tables(n):
    rates = np.exp(np.arange(32, dtype=np.float64) * (-2.0 * math.log(10000.0) / 64))
    phases = np.arange(n, dtype=np.float64)[:, None] * np.tile(rates, 4)[None, :]
    return np.cos(phases).astype(np.float32), np.sin(phases).astype(np.float32)


def compute(scalars, weights, frames, cotangent):
    n = frames.shape[0]
    shapes = act_shapes(n)
    cosine, sine = tables(n)
    vmem = pl.BlockSpec(memory_space=pltpu.VMEM)
    hbm = pl.BlockSpec(memory_space=pl.ANY)
    return pl.pallas_call(
        functools.partial(compute_kernel, tuple(shapes)),
        out_shape=(
            jax.ShapeDtypeStruct((2, n, 512), LOW),
            jax.ShapeDtypeStruct((2, n, 512), LOW),
            jax.ShapeDtypeStruct((2, 512, COLS), LOW),
        ),
        in_specs=[pl.BlockSpec(memory_space=pltpu.SMEM), hbm, vmem, vmem, vmem, vmem],
        out_specs=(vmem, vmem, hbm),
        scratch_shapes=list(shapes.values())
        + [
            pltpu.VMEM((2, 512, STEP), LOW),
            pltpu.SemaphoreType.DMA((2,)),
            pltpu.SemaphoreType.DMA((2,)),
        ],
        compiler_params=pltpu.CompilerParams(vmem_limit_bytes=62 * 2**20),
        cost_estimate=pl.CostEstimate(
            flops=30 * 10**9, bytes_accessed=60 * 2**20, transcendentals=10**7
        ),
    )(scalars, weights, frames, cotangent, jnp.asarray(cosine), jnp.asarray(sine))


def swap_halves(columns, back=False):
    rows = columns.shape[0]
    shape = (rows, 4, 2, 4, 32) if back else (rows, 4, 4, 2, 32)
    return columns.reshape(shape).swapaxes(2, 3).reshape(rows, 1024)


def pack(shards):
    eg, eu, ed, ag, pj, ao, cg, ci, cd, cn, co, lg, lu, ld, fg = (piece[0] for piece in shards)
    rows = eu.shape[0]
    small = jnp.concatenate(
        [gain[:, None] for gain in (eg, ag, cg, cn, lg, fg)]
        + [cd.T, jnp.zeros((rows, 128 - 6 - KERNEL), LOW)],
        axis=1,
    )
    proj = jnp.concatenate([swap_halves(pj[:, :1024]), pj[:, 1024:]], axis=1)
    return jnp.concatenate([eu, ed.T, proj, ao, ci, co, lu, ld.T, small], axis=1)


def unpack(block):
    proj = block[:, PJ : PJ + 1536]
    proj = jnp.concatenate([swap_halves(proj[:, :1024], True), proj[:, 1024:]], axis=1)
    gains = [block[:, SM + i] for i in range(6)]
    eg, ag, cg, cn, lg, fg = gains
    outs = (
        eg,
        block[:, EU:ED],
        block[:, ED:PJ].T,
        ag,
        proj,
        block[:, AO:CI],
        cg,
        block[:, CI:CO],
        block[:, SM + TAPS : SM + TAPS + KERNEL].T,
        cn,
        block[:, CO:LU],
        lg,
        block[:, LU:LD],
        block[:, LD:SM].T,
        fg,
    )
    return tuple(piece[None] for piece in outs)


def place_pair(own_pair, section):
    own = jnp.where(section == 0, own_pair[0], own_pair[1])
    other = jnp.where(section == 0, own_pair[1], own_pair[0])
    got = lax.ppermute(other, "pipe", [(0, 1), (1, 0)])
    return jnp.where(section == 0, jnp.stack([own, got]), jnp.stack([got, own]))[None, :, None]


def body(frames, cotangent, lengths, stream_flags, span_sizes, *shards):
    section = lax.axis_index("pipe")
    devices = lax.axis_size("dp")

    def mine(block):
        return lax.dynamic_index_in_dim(block, section, 0, keepdims=False)[0]

    scalars = jnp.stack([mine(lengths), mine(stream_flags), mine(span_sizes)])
    packed = pack(shards)
    rows = packed.shape[0]
    full = lax.all_gather(packed, ("pipe", "dp"), axis=0, tiled=True).reshape(2, 512, COLS)
    ys, dxs, grads = compute(scalars, full, mine(frames), mine(cotangent))
    summed = lax.psum_scatter(
        grads.reshape(1024, COLS), ("pipe", "dp"), scatter_dimension=0, tiled=True
    ).astype(F32)
    return (place_pair(ys, section), place_pair(dxs, section)) + unpack(summed)


def solution(mesh):
    gain, matrix, column = P("pipe", "dp"), P("pipe", "dp", None), P("pipe", None, "dp")
    weights = (gain, matrix, column, gain, matrix, matrix, gain, matrix, column, gain, matrix)
    weights = weights + (gain, matrix, column, gain)
    frames, stacked = P(None, "dp", None, None), P("pipe", None, "dp", None, None)
    return jax.shard_map(
        body,
        mesh=mesh,
        in_specs=(frames, frames) + (P(None, "dp"),) * 3 + weights,
        out_specs=(stacked, stacked) + weights,
        check_vma=False,
    )
```

```python
import functools
import math

import jax
import jax.numpy as jnp
import numpy as np
from jax import lax
from jax.experimental import pallas as pl
from jax.experimental.pallas import tpu as pltpu
from jax.sharding import PartitionSpec as P

HEADS = 8
KERNEL = 15
EPSILON = 1e-05
LOW = jnp.bfloat16
F32 = jnp.float32

EU, ED, PJ, AO, CI, CO, LU, LD, SM = 0, 2048, 4096, 5632, 6144, 7168, 7680, 9728, 11776
COLS = 11904
STEP = 512
G_EARLY, G_ATTEND, G_CONV, G_MIX, G_LATE, G_FINAL, TAPS = 0, 1, 2, 3, 4, 5, 6


def dot(left, right):
    return lax.dot_general(left, right, (((1,), (0,)), ((), ())), preferred_element_type=F32)


def dot_t(left, right):
    return lax.dot_general(left, right, (((1,), (1,)), ((), ())), preferred_element_type=F32)


def sigmoid(values):
    return 0.5 * jnp.tanh(0.5 * values) + 0.5


def norm_hat(values):
    center = values - jnp.mean(values, axis=-1, keepdims=True)
    rate = lax.rsqrt(jnp.mean(center * center, axis=-1, keepdims=True) + EPSILON)
    return center * rate, rate


def norm_grad(grad_hat, hat, rate):
    first = jnp.mean(grad_hat, axis=-1, keepdims=True)
    second = jnp.mean(grad_hat * hat, axis=-1, keepdims=True)
    return rate * (grad_hat - first - hat * second)


class Layer:
    def __init__(self, refs, emit, need, poll):
        self.__dict__.update(refs)
        self.emit, self.need, self.poll = emit, need, poll

    def gain(self, l, row):
        return self.sm[l, row : row + 1, :]

    def weight(self, l, column, size=STEP):
        return self.w[:, :, :, :, column : column + size].reshape(512, size)

    def enter(self, l, site, row):
        values = self.stream[...]
        hat, rate = norm_hat(values)
        self.xh[site] = hat.astype(LOW)
        self.rate[l, :, site : site + 1] = rate
        return (hat * self.gain(l, row)).astype(LOW)

    def leave(self, l, site, row, grad):
        hat = self.xh[site].astype(F32)
        rate = self.rate[l, :, site : site + 1]
        self.smg[l, row : row + 1, :] = jnp.sum(grad * hat, axis=0, keepdims=True)
        return norm_grad(grad * self.gain(l, row), hat, rate)

    def small_forward(self, l):
        self.need(l, SM)
        block = self.weight(l, SM, 128).astype(F32)
        self.sm[l] = block.T[:32]

    def small_backward(self, l):
        self.emit(l, SM, self.smg[l].T)

    def feed_forward(self, l, site, row, place, up, down):
        normed = self.enter(l, site, row)
        self.at[place] = normed.T
        side = 0 if site == 0 else 1
        total = None
        for j in range(0, 2048, STEP):
            self.need(l, up + j, down + j)
            inner = dot(normed, self.weight(l, up + j))
            self.u[side, :, j : j + STEP] = inner.astype(LOW)
            hidden = (inner * sigmoid(inner)).astype(LOW)
            term = dot_t(hidden, self.weight(l, down + j))
            total = term if total is None else total + term
        self.stream[...] += 0.5 * total

    def feed_backward(self, l, site, row, place, up, down):
        branch = (0.5 * self.grad[...]).astype(LOW)
        turned = branch.T
        side = 0 if site == 0 else 1
        total = None
        for j in range(0, 2048, STEP):
            hidden_grad = dot(branch, self.weight(l, down + j))
            inner = self.u[side, :, j : j + STEP].astype(F32)
            gate = sigmoid(inner)
            hidden = inner * gate
            inner_grad = (hidden_grad * (gate + hidden * (1.0 - gate))).astype(LOW)
            self.emit(l, down + j, dot(turned, hidden.astype(LOW)))
            self.emit(l, up + j, dot(self.at[place], inner_grad))
            term = dot_t(inner_grad, self.weight(l, up + j))
            total = term if total is None else total + term
        self.grad[...] += self.leave(l, site, row, total)

    def rotate(self, values, sign):
        cosine, sine = self.cos[...], self.sin[...]
        if sign < 0:
            sine = -sine
        parts = []
        for g in range(0, 512, 256):
            front, behind = values[:, g : g + 128], values[:, g + 128 : g + 256]
            parts += [front * cosine - behind * sine, front * sine + behind * cosine]
        return parts

    def pair_mask(self, j):
        lane = lax.broadcasted_iota(jnp.int32, (1, 256), 1)
        return (lane % 128) // 32 == j

    def head_mask(self, j):
        lane = lax.broadcasted_iota(jnp.int32, (1, 256), 1)
        return lane // 64 == j

    def attend_forward(self, l):
        normed = self.enter(l, 1, G_ATTEND)
        self.at[1] = normed.T
        self.need(l, PJ, PJ + 512, PJ + 1024)
        for which, scale in ((0, 0.125), (1, 1.0)):
            parts = self.rotate(dot(normed, self.weight(l, PJ + 512 * which)), 1)
            for i, part in enumerate(parts):
                self.qkv[which, :, 128 * i : 128 * i + 128] = part.astype(LOW) * LOW(scale)
        self.kt[...] = self.qkv[1].T
        value_rows = dot(normed, self.weight(l, PJ + 1024)).astype(LOW)
        self.qkv[2] = value_rows
        self.vt[...] = value_rows.T
        for h in range(HEADS):
            g, j = h // 4 * 256, h % 4
            keys = self.qkv[1, :, g : g + 256]
            keys = jnp.where(self.pair_mask(j), keys, jnp.zeros_like(keys))
            scores = dot_t(keys, self.qkv[0, :, g : g + 256]) + self.bias[...]
            powers = jnp.exp(scores - jnp.max(scores, axis=0, keepdims=True))
            powers = powers * (1.0 / jnp.sum(powers, axis=0, keepdims=True))
            powers = powers.astype(LOW)
            self.pt[h] = powers
            self.ot[64 * h : 64 * h + 64, :] = dot(
                self.vt[64 * h : 64 * h + 64, :], powers
            ).astype(LOW)
            self.poll()
        self.need(l, AO)
        self.stream[...] += dot(self.ot[...].T, self.weight(l, AO))

    def attend_backward(self, l):
        branch = self.grad[...].astype(LOW)
        self.emit(l, AO, dot(self.ot[...], branch))
        self.ctx[...] = dot_t(branch, self.weight(l, AO)).astype(LOW)
        key_total, value_total = [], []
        for g in range(0, 512, 256):
            ctx = self.ctx[:, g : g + 256]
            queries = self.qkv[0, :, g : g + 256]
            values = self.qkv[2, :, g : g + 256]
            key_grad = value_grad = None
            for j in range(4):
                h = g // 64 + j
                head = self.head_mask(j)
                soft_grad = dot_t(jnp.where(head, values, jnp.zeros_like(values)), ctx)
                soft_low = self.pt[h]
                soft = soft_low.astype(F32)
                delta = jnp.sum(soft_grad * soft, axis=0, keepdims=True)
                score_grad = (soft * (soft_grad - delta)).astype(LOW)
                term = dot(soft_low, jnp.where(head, ctx, jnp.zeros_like(ctx)))
                value_grad = term if value_grad is None else value_grad + term
                term = dot(
                    score_grad, jnp.where(self.pair_mask(j), queries, jnp.zeros_like(queries))
                )
                key_grad = term if key_grad is None else key_grad + term
                front, behind = g + 32 * j, g + 128 + 32 * j
                rows = jnp.concatenate(
                    [self.kt[front : front + 32, :], self.kt[behind : behind + 32, :]], axis=0
                )
                turned = dot(rows, score_grad)
                self.qt[front : front + 32, :] = turned[:32]
                self.qt[behind : behind + 32, :] = turned[32:]
                self.poll()
            key_total.append(key_grad)
            value_total.append(value_grad)
        query_grad = self.qt[...].T * 0.125
        query_grad = jnp.concatenate(self.rotate(query_grad, -1), axis=1).astype(LOW)
        key_grad = jnp.concatenate(key_total, axis=1)
        key_grad = jnp.concatenate(self.rotate(key_grad, -1), axis=1).astype(LOW)
        value_grad = jnp.concatenate(value_total, axis=1).astype(LOW)
        total = None
        for i, part in enumerate((query_grad, key_grad, value_grad)):
            self.emit(l, PJ + 512 * i, dot(self.at[1], part))
            term = dot_t(part, self.weight(l, PJ + 512 * i))
            total = term if total is None else total + term
        self.grad[...] += self.leave(l, 1, G_ATTEND, total)

    def tap(self, l, k):
        row = self.sm[l, TAPS + k : TAPS + k + 1, :]
        return row if k <= KERNEL // 2 else row * self.whole

    def convolve_forward(self, l):
        normed = self.enter(l, 2, G_CONV)
        self.at[2] = normed.T
        self.need(l, CI, CI + 512, CO)
        first = dot(normed, self.weight(l, CI))
        second = dot(normed, self.weight(l, CI + 512))
        self.gates[:, :512] = first.astype(LOW)
        self.gates[:, 512:] = second.astype(LOW)
        n = first.shape[0]
        self.pad[0, 8 : n + 8, :] = first * sigmoid(second) * self.live[...]
        mixed = None
        for k in range(KERNEL):
            term = self.tap(l, k) * self.pad[0, k + 1 : k + 1 + n, :]
            mixed = term if mixed is None else mixed + term
        hat, rate = norm_hat(mixed)
        self.xh[5] = hat.astype(LOW)
        self.rate[l, :, 5:6] = rate
        inner = hat * self.gain(l, G_MIX)
        hidden = (inner * sigmoid(inner)).astype(LOW)
        self.wt[...] = hidden.T
        self.stream[...] += dot(hidden, self.weight(l, CO))

    def convolve_backward(self, l):
        branch = self.grad[...].astype(LOW)
        n = branch.shape[0]
        self.emit(l, CO, dot(self.wt[...], branch))
        hidden_grad = dot_t(branch, self.weight(l, CO))
        hat = self.xh[5].astype(F32)
        inner = hat * self.gain(l, G_MIX)
        gate = sigmoid(inner)
        inner_grad = hidden_grad * (gate + inner * gate * (1.0 - gate))
        self.pad[1, 8 : n + 8, :] = self.leave(l, 5, G_MIX, inner_grad)
        first = self.gates[:, :512].astype(F32)
        gate = sigmoid(self.gates[:, 512:].astype(F32))
        self.pad[0, 8 : n + 8, :] = first * gate * self.live[...]
        mixed_grad = self.pad[1, 8 : n + 8, :]
        total = None
        for k in range(KERNEL):
            row = jnp.sum(mixed_grad * self.pad[0, k + 1 : k + 1 + n, :], axis=0, keepdims=True)
            if k > KERNEL // 2:
                row = row * self.whole
            self.smg[l, TAPS + k : TAPS + k + 1, :] = row
            term = self.tap(l, k) * self.pad[1, 15 - k : 15 - k + n, :]
            total = term if total is None else total + term
        total = total * self.live[...]
        first_grad = (total * gate).astype(LOW)
        second_grad = (total * first * gate * (1.0 - gate)).astype(LOW)
        self.emit(l, CI, dot(self.at[2], first_grad))
        self.emit(l, CI + 512, dot(self.at[2], second_grad))
        total = dot_t(first_grad, self.weight(l, CI))
        total = total + dot_t(second_grad, self.weight(l, CI + 512))
        self.grad[...] += self.leave(l, 2, G_CONV, total)

    def prepare(self, length, flag, span):
        n = self.stream.shape[0]
        key = lax.broadcasted_iota(jnp.int32, (n, n), 0)
        query = lax.broadcasted_iota(jnp.int32, (n, n), 1)
        width = span.astype(F32)
        key_block = jnp.floor((key.astype(F32) + 0.5) / width)
        query_block = jnp.floor((query.astype(F32) + 0.5) / width)
        shown = (key < length) & ((flag == 0) | (key_block <= query_block))
        self.bias[...] = jnp.where(shown, 0.0, -1e30)
        place = lax.broadcasted_iota(jnp.int32, (n, 1), 0)
        self.live[...] = (place < length).astype(F32)
        self.whole = jnp.where(flag == 0, 1.0, 0.0)
        self.pad[...] = jnp.zeros_like(self.pad)
        self.smg[...] = jnp.zeros_like(self.smg)

    def finish_forward(self, l):
        hat, rate = norm_hat(self.stream[...])
        self.xh[4] = hat.astype(LOW)
        self.rate[l, :, 4:5] = rate
        return (hat * self.gain(l, G_FINAL)).astype(LOW)


def act_shapes(n):
    return dict(
        xh=((6, n, 512), LOW),
        at=((4, 512, n), LOW),
        u=((2, n, 2048), LOW),
        qkv=((3, n, 512), LOW),
        kt=((512, n), LOW),
        pt=((HEADS, n, n), LOW),
        ot=((512, n), LOW),
        gates=((n, 1024), LOW),
        wt=((512, n), LOW),
    )


MODULE_ACTS = (
    (("u", 0), ("xh", 0), ("at", 0)),
    (("qkv", None), ("kt", None), ("pt", None), ("ot", None), ("xh", 1), ("at", 1)),
    (("gates", None), ("wt", None), ("xh", 2), ("xh", 5), ("at", 2)),
    (("u", 1), ("xh", 3), ("xh", 4), ("at", 3)),
)


def work_shapes(n):
    return dict(
        w=pltpu.VMEM((4, 2, 2, 32, COLS), LOW),
        stream=pltpu.VMEM((n, 512), F32),
        grad=pltpu.VMEM((n, 512), F32),
        rate=pltpu.VMEM((2, n, 128), F32),
        vt=pltpu.VMEM((512, n), LOW),
        qt=pltpu.VMEM((512, n), F32),
        ctx=pltpu.VMEM((n, 512), LOW),
        pad=pltpu.VMEM((2, n + 16, 512), F32),
        sm=pltpu.VMEM((2, 32, 512), F32),
        smg=pltpu.VMEM((2, 128, 512), F32),
        bias=pltpu.VMEM((n, n), F32),
        live=pltpu.VMEM((n, 1), F32),
        given=pltpu.VMEM((2, n, 512), LOW),
        result=pltpu.VMEM((2, n, 512), LOW),
        result_grad=pltpu.VMEM((2, n, 512), LOW),
    )
MESH = pl.DeviceIdType.MESH

FORWARD_PIECES = (
    [(SM, 128)]
    + [(base + j, STEP) for j in range(0, 2048, STEP) for base in (EU, ED)]
    + [(PJ, STEP), (PJ + 512, STEP), (PJ + 1024, STEP), (AO, STEP), (CI, STEP), (CI + 512, STEP), (CO, STEP)]
    + [(base + j, STEP) for j in range(0, 2048, STEP) for base in (LU, LD)]
)
WAYS = "FFAFGFAFGFAG" + "FAFGFAFGFAGF"


class Place:
    def __init__(self):
        p, d = lax.axis_index("pipe"), lax.axis_index("dp")
        self.p, self.z, self.y, self.c = p, d // 4, d // 2 % 2, d % 2
        z, y, c = self.z, self.y, self.c
        self.across = (1 - p, d)
        self.beside = (p, z * 4 + (1 - y) * 2 + c)
        self.twin = (p, z * 4 + y * 2 + 1 - c)
        self.column = [(p, (z + j) % 4 * 4 + y * 2 + c) for j in (1, 2, 3)]

    def greet(self):
        barrier = pltpu.get_barrier_semaphore()
        partners = [self.across, self.beside, self.twin] + self.column
        for partner in partners:
            pl.semaphore_signal(barrier, inc=1, device_id=partner, device_id_type=MESH)
        pl.semaphore_wait(barrier, len(partners))


def remote(source, target, send, arrive, device):
    return pltpu.make_async_remote_copy(
        src_ref=source, dst_ref=target, send_sem=send, recv_sem=arrive, device_id=device, device_id_type=MESH
    )


class Gather:
    def __init__(self, place, shard, w, sems):
        self.place, self.shard, self.w = place, shard, w
        self.zs, self.zr, self.ys, self.yr, self.xs, self.xr, self.ds, self.dr, self.own = sems

    def cols(self, k):
        return pl.ds(*FORWARD_PIECES[k])

    def block(self, l, k, z, y):
        return self.w.at[l, z, y, self.place.c, :, self.cols(k)]

    def mine(self, l, k):
        return self.block(l, k, self.place.z, self.place.y)

    def z_copy(self, l, k, j, source=None):
        target = self.mine(l, k)
        source = target if source is None else source
        return remote(source, target, self.zs.at[l, k, j], self.zr.at[l, k, j], self.place.column[j])

    def z_wait(self, l, k):
        for j in range(3):
            got = self.block(l, k, (self.place.z + 3 - j) % 4, self.place.y)
            remote(got, got, self.zs.at[l, k, j], self.zr.at[l, k, j], self.place.column[j]).wait_recv()

    def y_copy(self, l, k, y):
        part = self.w.at[l, :, y, self.place.c, :, self.cols(k)]
        return remote(part, part, self.ys.at[l, k], self.yr.at[l, k], self.place.beside)

    def x_one(self, l, k, source=None):
        target = self.mine(l, k)
        source = target if source is None else source
        return remote(source, target, self.xs.at[l, k], self.xr.at[l, k], self.place.across)

    def x_all(self, l, k):
        part = self.w.at[l, :, :, self.place.c, :, self.cols(k)]
        return remote(part, part, self.xs.at[l, k], self.xr.at[l, k], self.place.across)

    def d_copy(self, l, k, c):
        part = self.w.at[l, :, :, c, :, self.cols(k)]
        return remote(part, part, self.ds.at[l, k], self.dr.at[l, k], self.place.twin)

    def own_copy(self, k):
        target = self.w.at[self.place.p, self.place.z, self.place.y, self.place.c, :, self.cols(k)]
        return pltpu.make_async_copy(self.shard.at[:, self.cols(k)], target, self.own.at[k])

    def start_own(self):
        for k, way in enumerate(WAYS):
            if way != "G":
                self.own_copy(k).start()

    def owner(self, l):
        return pl.when(self.place.p == l)

    def other(self, l):
        return pl.when(self.place.p != l)

    def step0(self, l, k):
        way, piece = WAYS[k], self.shard.at[:, self.cols(k)]

        @self.owner(l)
        def _():
            if way in "FG":
                self.x_one(l, k, piece).start()
            if way in "FA":
                for j in range(3):
                    self.z_copy(l, k, j, piece).start()

    def step1(self, l, k):
        way = WAYS[k]
        if way in "FG":

            @self.other(l)
            def _():
                self.x_one(l, k).wait_recv()
                for j in range(3):
                    self.z_copy(l, k, j).start()

    def step2(self, l, k):
        way = WAYS[k]

        def send():
            self.z_wait(l, k)
            self.y_copy(l, k, self.place.y).start()

        if way in "FA":

            @self.owner(l)
            def _():
                self.own_copy(k).wait()
                send()

        if way in "FG":
            self.other(l)(send)

    def step3(self, l, k):
        way = WAYS[k]

        def send(on):
            self.y_copy(l, k, 1 - self.place.y).wait_recv()
            if on:
                self.x_all(l, k).start()
            self.d_copy(l, k, self.place.c).start()

        if way in "FA":
            self.owner(l)(functools.partial(send, way == "A"))
        if way in "FG":
            self.other(l)(functools.partial(send, way == "G"))

    def step4(self, l, k):
        way = WAYS[k]

        def send():
            self.x_all(l, k).wait_recv()
            self.d_copy(l, k, self.place.c).start()

        if way == "A":
            self.other(l)(send)
        if way == "G":
            self.owner(l)(send)

    def arrived(self, l, k):
        self.d_copy(l, k, 1 - self.place.c).wait_recv()

    def drain(self, l, k):
        way = WAYS[k]
        piece = self.shard.at[:, self.cols(k)]
        self.d_copy(l, k, self.place.c).wait_send()

        @self.owner(l)
        def _():
            if way in "FG":
                self.x_one(l, k, piece).wait_send()
            if way == "A":
                self.x_all(l, k).wait_send()
            if way in "FA":
                for j in range(3):
                    self.z_copy(l, k, j, piece).wait_send()
                self.y_copy(l, k, self.place.y).wait_send()

        @self.other(l)
        def _():
            if way == "G":
                self.x_all(l, k).wait_send()
            if way in "FG":
                for j in range(3):
                    self.z_copy(l, k, j).wait_send()
                self.y_copy(l, k, self.place.y).wait_send()


def gather_sems():
    dma, count = pltpu.SemaphoreType.DMA, len(FORWARD_PIECES)
    return [dma((2, count, 3))] * 2 + [dma((2, count))] * 6 + [dma((count,))]


BACKWARD_PIECES = (
    [(base + j, STEP) for j in range(0, 2048, STEP) for base in (LD, LU)]
    + [(CO, STEP), (CI, STEP), (CI + 512, STEP), (AO, STEP), (PJ, STEP), (PJ + 512, STEP), (PJ + 1024, STEP)]
    + [(base + j, STEP) for j in range(0, 2048, STEP) for base in (ED, EU)]
    + [(SM, 128)]
)
BACK_WAYS = "FAGFAGFFAGFFAGFAGFFAGFFF"
BACK_INDEX = {column: k for k, (column, _) in enumerate(BACKWARD_PIECES)}
WIDE = [k for k, way in enumerate(BACK_WAYS) if way in "AG"]
LATE = [k for k, way in enumerate(BACK_WAYS) if way in "FG"]
STAGES = 4


class Scatter:
    def __init__(self, place, out, refs, sems):
        self.place, self.out = place, out
        self.stage, self.part, self.wide, self.side, self.line, self.late = refs
        self.ds, self.dr, self.xs, self.xr, self.ys, self.yr, self.zs, self.zr = sems[:8]
        self.free_d, self.free_y, self.free_z = sems[8:]
        self.count = 0
        self.slot = {}

    def width(self, k):
        return BACKWARD_PIECES[k][1]

    def cols(self, k):
        return pl.ds(0, self.width(k))

    def roles(self, l, k, owner, other):
        if owner:
            pl.when(self.place.p == l)(owner)
        if other:
            pl.when(self.place.p != l)(other)

    def d_copy(self, l, k):
        source = self.stage.at[self.slot[l, k], :, :, 1 - self.place.c, :, self.cols(k)]
        target = self.part.at[k, :, :, :, self.cols(k)]
        return remote(source, target, self.ds.at[l, k], self.dr.at[l, k], self.place.twin)

    def x_wide(self, l, k):
        source = self.part.at[k, :, :, :, self.cols(k)]
        target = self.wide.at[WIDE.index(k), :, :, :, self.cols(k)]
        return remote(source, target, self.xs.at[l, k], self.xr.at[l, k], self.place.across)

    def x_late(self, l, k):
        source = self.part.at[k, self.place.z, self.place.y, :, self.cols(k)]
        target = self.late.at[LATE.index(k), :, self.cols(k)]
        return remote(source, target, self.xs.at[l, k], self.xr.at[l, k], self.place.across)

    def y_copy(self, l, k):
        source = self.part.at[k, :, 1 - self.place.y, :, self.cols(k)]
        target = self.side.at[k, :, :, self.cols(k)]
        return remote(source, target, self.ys.at[l, k], self.yr.at[l, k], self.place.beside)

    def z_copy(self, l, k, j):
        source = self.part.at[k, (self.place.z + j + 1) % 4, self.place.y, :, self.cols(k)]
        target = self.line.at[k, j, :, self.cols(k)]
        return remote(source, target, self.zs.at[l, k, j], self.zr.at[l, k, j], self.place.column[j])

    def offer(self, l, column, value):
        k = BACK_INDEX[column]
        width = self.width(k)
        slot = self.count % STAGES
        self.count += 1
        self.slot[l, k] = slot
        self.stage[slot, :, :, :, :, :width] = value.astype(LOW).reshape(4, 2, 2, 32, width)
        if l == 0:
            pl.semaphore_wait(self.free_d.at[k], 1)
        self.d_copy(l, k).start()

    def y_start(self, l, k):
        if l == 0 and BACK_WAYS[k] == "F":
            pl.semaphore_wait(self.free_y.at[k], 1)
        self.y_copy(l, k).start()

    def step1(self, l, k):
        way, cols = BACK_WAYS[k], self.cols(k)
        self.d_copy(l, k).wait()
        slot, c = self.slot[l, k], self.place.c

        def add(b, _):
            z, y = b // 2, b % 2
            total = self.part[k, z, y, :, cols].astype(F32)
            total = total + self.stage[slot, z, y, c, :, cols].astype(F32)
            self.part[k, z, y, :, cols] = total.astype(LOW)
            return _

        lax.fori_loop(0, 8, add, 0)

        def wide():
            self.x_wide(l, k).start()

        if way == "F":
            self.y_start(l, k)
        else:
            self.roles(l, k, wide if way == "G" else None, wide if way == "A" else None)

    def step2(self, l, k):
        way, cols = BACK_WAYS[k], self.cols(k)
        if way == "F":
            return
        w = WIDE.index(k)

        def run():
            self.x_wide(l, k).wait_recv()

            def add(b, _):
                z, y = b // 2, b % 2
                total = self.part[k, z, y, :, cols].astype(F32)
                total = total + self.wide[w, z, y, :, cols].astype(F32)
                self.part[k, z, y, :, cols] = total.astype(LOW)
                return _

            lax.fori_loop(0, 8, add, 0)
            self.y_start(l, k)

        self.roles(l, k, run if way == "A" else None, run if way == "G" else None)

    def step3(self, l, k):
        way, cols = BACK_WAYS[k], self.cols(k)

        def run():
            self.y_copy(l, k).wait_recv()
            y = self.place.y

            def add(z, _):
                total = self.part[k, z, y, :, cols].astype(F32)
                total = total + self.side[k, z, :, cols].astype(F32)
                self.part[k, z, y, :, cols] = total.astype(LOW)
                return _

            lax.fori_loop(0, 4, add, 0)
            for j in range(3):
                if l == 0 and way == "F":
                    pl.semaphore_wait(self.free_z.at[k, j], 1)
                self.z_copy(l, k, j).start()

        self.roles(l, k, run if way in "AF" else None, run if way in "GF" else None)

    def step4(self, l, k):
        way, cols = BACK_WAYS[k], self.cols(k)
        column = pl.ds(BACKWARD_PIECES[k][0], self.width(k))

        def total():
            for j in range(3):
                self.z_copy(l, k, j).wait_recv()
            result = self.part[k, self.place.z, self.place.y, :, cols].astype(F32)
            for j in range(3):
                result = result + self.line[k, j, :, cols].astype(F32)
            return result

        def owner():
            self.out[:, column] = total()

        def other():
            self.part[k, self.place.z, self.place.y, :, cols] = total().astype(LOW)
            self.x_late(l, k).start()

        self.roles(l, k, owner if way in "AF" else None, other if way in "GF" else None)

    def step5(self, l, k):
        way, cols = BACK_WAYS[k], self.cols(k)
        column = pl.ds(BACKWARD_PIECES[k][0], self.width(k))

        def owner():
            if way in "FG":
                self.x_late(l, k).wait_recv()
                got = self.late[LATE.index(k), :, cols].astype(F32)
                self.out[:, column] = self.out[:, column] + got if way == "F" else got
            if way == "G":
                self.x_wide(l, k).wait_send()
            else:
                sent()

        def sent():
            self.y_copy(l, k).wait_send()
            for j in range(3):
                self.z_copy(l, k, j).wait_send()

        def other():
            if way in "FG":
                sent()
                self.x_late(l, k).wait_send()
            else:
                self.x_wide(l, k).wait_send()

        self.roles(l, k, owner, other)
        if l == 1:
            pl.semaphore_signal(
                self.free_d.at[k], inc=1, device_id=self.place.twin, device_id_type=MESH
            )
            if way == "F":
                pl.semaphore_signal(
                    self.free_y.at[k], inc=1, device_id=self.place.beside, device_id_type=MESH
                )
                for j in range(3):
                    writer = self.place.column[2 - j]
                    pl.semaphore_signal(
                        self.free_z.at[k, j], inc=1, device_id=writer, device_id_type=MESH
                    )


def scatter_refs():
    count = len(BACKWARD_PIECES)
    return [
        pltpu.VMEM((STAGES, 4, 2, 2, 32, STEP), LOW),
        pltpu.VMEM((count, 4, 2, 32, STEP), LOW),
        pltpu.VMEM((len(WIDE), 4, 2, 32, STEP), LOW),
        pltpu.VMEM((count, 4, 32, STEP), LOW),
        pltpu.VMEM((count, 3, 32, STEP), LOW),
        pltpu.VMEM((len(LATE), 32, STEP), LOW),
    ]


def scatter_sems():
    dma, count = pltpu.SemaphoreType.DMA, len(BACKWARD_PIECES)
    regular = pltpu.SemaphoreType.REGULAR
    pairs = [dma((2, count))] * 6 + [dma((2, count, 3))] * 2
    return pairs + [regular((count,)), regular((count,)), regular((count, 3))]


GATHER_LAGS = (0, 2, 6, 12, 22)
ARRIVE_LAG, DRAIN_LAG = 24, 30
SCATTER_LAGS = (1, 5, 10, 13, 18)


def fused_kernel(groups, scalars, shard, frames, cotangent, cos, sin, y_out, dx_out, g_out, w, *rest):
    n_acts, act_names, work_names, n = groups
    kept, rest = dict(zip(act_names, rest[:n_acts])), rest[n_acts:]
    acts, rest = dict(zip(act_names, rest[:n_acts])), rest[n_acts:]
    work, rest = dict(zip(work_names, rest[: len(work_names)])), rest[len(work_names) :]
    back_refs, rest = rest[:6], rest[6:]
    gather_sem, rest = rest[:9], rest[9:]
    scatter_sem, rest = rest[:11], rest[11:]
    load_sem, keep_sem, given_sem, share_send, share_arrive = rest

    place = Place()
    p = place.p
    given = [
        pltpu.make_async_copy(source.at[p], work["given"].at[i], given_sem.at[i])
        for i, source in enumerate((frames, cotangent))
    ]
    for copy in given:
        copy.start()
    place.greet()

    gather = Gather(place, shard, w, gather_sem)
    count = len(FORWARD_PIECES)
    number = {column: k for k, (column, _) in enumerate(FORWARD_PIECES)}
    state = dict(slot=0, first_done=False, back=0)
    started, waiting = set(), []

    def load(l, k):
        cols = gather.cols(k)
        return pltpu.make_async_copy(
            w.at[l, :, :, :, :, cols], work["w"].at[:, :, :, :, cols], load_sem.at[l, k]
        )

    def run_slot():
        t = state["slot"]
        state["slot"] += 1
        steps = (gather.step0, gather.step1, gather.step2, gather.step3, gather.step4)
        for step, lag in zip(steps, GATHER_LAGS):
            if 0 <= t - lag < 2 * count:
                step((t - lag) // count, (t - lag) % count)
        i = t - ARRIVE_LAG
        if 0 <= i < 2 * count:
            l, k = i // count, i % count
            gather.arrived(l, k)
            if l == 0 or state["first_done"]:
                load(l, k).start()
            else:
                waiting.append((l, k))
        i = t - DRAIN_LAG
        if 0 <= i < 2 * count:
            gather.drain(i // count, i % count)

    last_slot = 2 * count + DRAIN_LAG

    def need(l, *columns):
        for column in columns:
            k = number[column]
            while state["slot"] <= l * count + k + ARRIVE_LAG:
                run_slot()
        for column in columns:
            load(l, number[column]).wait()

    def keep(module, back):
        copies = []
        for i, (name, index) in enumerate(MODULE_ACTS[module]):
            near, far = acts[name], kept[name]
            if index is not None:
                near, far = near.at[index], far.at[index]
            source, target = (far, near) if back else (near, far)
            copies.append(pltpu.make_async_copy(source, target, keep_sem.at[int(back), module, i]))
        return copies

    scatter = Scatter(place, g_out, back_refs, scatter_sem)
    order = [(l, k) for l in (1, 0) for k in range(count)]
    steps = (scatter.step1, scatter.step2, scatter.step3, scatter.step4, scatter.step5)
    done = [0] * len(steps)

    def back_slot(offered, lags):
        for i, step in enumerate(steps):
            while done[i] < min(len(order), offered - lags[i]):
                step(*order[done[i]])
                done[i] += 1

    def emit(l, column, value):
        scatter.offer(l, column, value)
        back_slot(scatter.count, SCATTER_LAGS)

    def poll():
        if state["back"] == 0 and state["slot"] < last_slot:
            run_slot()

    run = Layer({**acts, **work, "cos": cos, "sin": sin}, emit, need, poll)

    def share(i, l, results, out):
        own = pltpu.make_async_copy(results.at[l], out.at[p], share_send.at[i, l])
        away = remote(
            results.at[l], out.at[p], share_send.at[i, l], share_arrive.at[i], place.across
        )

        def go():
            pl.when(p == l)(own.start)
            pl.when(p != l)(away.start)

        def finish():
            pl.when(p == l)(own.wait)

            @pl.when(p != l)
            def _():
                away.wait_send()
                remote(
                    results.at[l], out.at[1 - p], share_send.at[i, l], share_arrive.at[i], place.across
                ).wait_recv()

        return go, finish

    shares = [[share(0, l, work["result"], y_out) for l in range(2)]]
    shares.append([share(1, l, work["result_grad"], dx_out) for l in range(2)])

    gather.start_own()
    for _ in range(8):
        run_slot()
    run.prepare(scalars[0, p], scalars[1, p], scalars[2, p])
    given[0].wait()
    run.stream[...] = run.given[0].astype(F32)
    modules = (
        lambda l: run.feed_forward(l, 0, G_EARLY, 0, EU, ED),
        run.attend_forward,
        run.convolve_forward,
        lambda l: run.feed_forward(l, 3, G_LATE, 3, LU, LD),
    )
    for l in range(2):
        run.small_forward(l)
        for m, module in enumerate(modules):
            if l == 1:
                for copy in keep(m, False):
                    copy.wait()
            module(l)
            if l == 0 and m < 3:
                for copy in keep(m, False):
                    copy.start()
        run.result[l] = run.finish_forward(l)
        shares[0][l][0]()
        if l == 0:
            for copy in keep(3, False):
                copy.start()
            run.stream[...] = run.result[0].astype(F32)
            state["first_done"] = True
            for item in waiting:
                load(*item).start()
    while state["slot"] < last_slot:
        run_slot()
    state["back"] = 1
    given[1].wait()
    back_modules = (
        lambda l: run.feed_backward(l, 0, G_EARLY, 0, EU, ED),
        run.attend_backward,
        run.convolve_backward,
        lambda l: run.feed_backward(l, 3, G_LATE, 3, LU, LD),
    )
    columns = ((EU, 4096), (PJ, 2048), (CI, 1536), (LU, 4096))

    def reload(m):
        cols = pl.ds(*columns[m])
        return pltpu.make_async_copy(
            w.at[0, :, :, :, :, cols], work["w"].at[:, :, :, :, cols], load_sem.at[0, m]
        )

    for l in (1, 0):
        if l == 0:
            for copy in keep(3, True):
                copy.wait()
        start = run.given[1].astype(F32) if l == 1 else run.result_grad[1].astype(F32)
        run.grad[...] = run.leave(l, 4, G_FINAL, start)
        for m in (3, 2, 1, 0):
            if l == 0:
                if m < 3:
                    for copy in keep(m, True):
                        copy.wait()
                reload(m).wait()
            back_modules[m](l)
            if l == 1:
                for copy in keep(m, True):
                    copy.start()
                reload(m).start()
        run.small_backward(l)
        run.result_grad[l] = run.grad[...].astype(LOW)
        shares[1][l][0]()
    for extra in range(max(SCATTER_LAGS) + 1):
        back_slot(2 * count + extra, SCATTER_LAGS)
    for pair in shares:
        for _, finish in pair:
            finish()


def tables(n):
    rates = np.exp(np.arange(32, dtype=np.float64) * (-2.0 * math.log(10000.0) / 64))
    phases = np.arange(n, dtype=np.float64)[:, None] * np.tile(rates, 4)[None, :]
    return np.cos(phases).astype(np.float32), np.sin(phases).astype(np.float32)


def fused(scalars, shard, frames, cotangent):
    n = frames.shape[1]
    acts, work = act_shapes(n), work_shapes(n)
    cosine, sine = tables(n)
    vmem = pl.BlockSpec(memory_space=pltpu.VMEM)
    hbm = pl.BlockSpec(memory_space=pl.ANY)
    dma, count = pltpu.SemaphoreType.DMA, len(FORWARD_PIECES)
    groups = (len(acts), tuple(acts), tuple(work), n)
    outs = pl.pallas_call(
        functools.partial(fused_kernel, groups),
        out_shape=[
            jax.ShapeDtypeStruct((2, n, 512), LOW),
            jax.ShapeDtypeStruct((2, n, 512), LOW),
            jax.ShapeDtypeStruct((32, COLS), F32),
            jax.ShapeDtypeStruct((2, 4, 2, 2, 32, COLS), LOW),
        ]
        + [jax.ShapeDtypeStruct(shape, kind) for shape, kind in acts.values()],
        in_specs=[pl.BlockSpec(memory_space=pltpu.SMEM), hbm, hbm, hbm, vmem, vmem],
        out_specs=[hbm, hbm, vmem, hbm] + [hbm] * len(acts),
        scratch_shapes=[pltpu.VMEM(shape, kind) for shape, kind in acts.values()]
        + list(work.values())
        + scatter_refs()
        + gather_sems()
        + scatter_sems()
        + [dma((2, count)), dma((2, 4, 6)), dma((2,)), dma((2, 2)), dma((2,))],
        compiler_params=pltpu.CompilerParams(
            collective_id=0, has_side_effects=True, vmem_limit_bytes=63 * 2**20
        ),
        cost_estimate=pl.CostEstimate(
            flops=30 * 10**9, bytes_accessed=100 * 2**20, transcendentals=10**7
        ),
    )(scalars, shard, frames, cotangent, jnp.asarray(cosine), jnp.asarray(sine))
    return outs[:3]


def plain_kernel(groups, scalars, w, frames, cotangent, cos, sin, y_out, dx_out, g_out, *rest):
    n_acts, act_names, work_names, n = groups
    kept, rest = dict(zip(act_names, rest[:n_acts])), rest[n_acts:]
    acts, rest = dict(zip(act_names, rest[:n_acts])), rest[n_acts:]
    work, rest = dict(zip(work_names, rest[: len(work_names)])), rest[len(work_names) :]
    stage, sem = rest

    def move(source, target):
        copy = pltpu.make_async_copy(source, target, sem)
        copy.start()
        copy.wait()

    def emit(l, column, value):
        width = value.shape[1]
        stage[:, :width] = value.astype(LOW)
        move(stage.at[:, pl.ds(0, width)], g_out.at[l, :, pl.ds(column, width)])

    run = Layer(
        {**acts, **work, "cos": cos, "sin": sin}, emit, lambda *_: None, lambda: None
    )
    move(frames, run.given.at[0])
    move(cotangent, run.given.at[1])
    run.prepare(scalars[0], scalars[1], scalars[2])
    run.stream[...] = run.given[0].astype(F32)
    for l in range(2):
        move(w.at[l], work["w"])
        run.small_forward(l)
        run.feed_forward(l, 0, G_EARLY, 0, EU, ED)
        run.attend_forward(l)
        run.convolve_forward(l)
        run.feed_forward(l, 3, G_LATE, 3, LU, LD)
        run.result[l] = run.finish_forward(l)
        run.stream[...] = run.result[l].astype(F32)
        if l == 0:
            for name in act_names:
                move(acts[name], kept[name])
    for l in (1, 0):
        if l == 0:
            move(w.at[0], work["w"])
            for name in act_names:
                move(kept[name], acts[name])
        start = run.given[1].astype(F32) if l == 1 else run.result_grad[1].astype(F32)
        run.grad[...] = run.leave(l, 4, G_FINAL, start)
        run.feed_backward(l, 3, G_LATE, 3, LU, LD)
        run.convolve_backward(l)
        run.attend_backward(l)
        run.feed_backward(l, 0, G_EARLY, 0, EU, ED)
        run.small_backward(l)
        run.result_grad[l] = run.grad[...].astype(LOW)
    move(run.result, y_out)
    move(run.result_grad, dx_out)


def plain(scalars, weights, frames, cotangent):
    n = frames.shape[0]
    acts, work = act_shapes(n), work_shapes(n)
    cosine, sine = tables(n)
    vmem = pl.BlockSpec(memory_space=pltpu.VMEM)
    hbm = pl.BlockSpec(memory_space=pl.ANY)
    outs = pl.pallas_call(
        functools.partial(plain_kernel, (len(acts), tuple(acts), tuple(work), n)),
        out_shape=[
            jax.ShapeDtypeStruct((2, n, 512), LOW),
            jax.ShapeDtypeStruct((2, n, 512), LOW),
            jax.ShapeDtypeStruct((2, 512, COLS), LOW),
        ]
        + [jax.ShapeDtypeStruct(shape, kind) for shape, kind in acts.values()],
        in_specs=[pl.BlockSpec(memory_space=pltpu.SMEM), hbm, hbm, hbm, vmem, vmem],
        out_specs=[hbm] * (3 + len(acts)),
        scratch_shapes=[pltpu.VMEM(shape, kind) for shape, kind in acts.values()]
        + list(work.values())
        + [pltpu.VMEM((512, STEP), LOW), pltpu.SemaphoreType.DMA],
        compiler_params=pltpu.CompilerParams(vmem_limit_bytes=60 * 2**20),
    )(scalars, weights, frames, cotangent, jnp.asarray(cosine), jnp.asarray(sine))
    return outs[:3]


def swap_halves(columns, back=False):
    rows = columns.shape[0]
    shape = (rows, 4, 2, 4, 32) if back else (rows, 4, 4, 2, 32)
    return columns.reshape(shape).swapaxes(2, 3).reshape(rows, 1024)


def pack(shards):
    eg, eu, ed, ag, pj, ao, cg, ci, cd, cn, co, lg, lu, ld, fg = (piece[0] for piece in shards)
    rows = eu.shape[0]
    small = jnp.concatenate(
        [gain[:, None] for gain in (eg, ag, cg, cn, lg, fg)]
        + [cd.T, jnp.zeros((rows, 128 - 6 - KERNEL), LOW)],
        axis=1,
    )
    proj = jnp.concatenate([swap_halves(pj[:, :1024]), pj[:, 1024:]], axis=1)
    return jnp.concatenate([eu, ed.T, proj, ao, ci, co, lu, ld.T, small], axis=1)


def unpack(block):
    proj = block[:, PJ : PJ + 1536]
    proj = jnp.concatenate([swap_halves(proj[:, :1024], True), proj[:, 1024:]], axis=1)
    gains = [block[:, SM + i] for i in range(6)]
    eg, ag, cg, cn, lg, fg = gains
    outs = (
        eg,
        block[:, EU:ED],
        block[:, ED:PJ].T,
        ag,
        proj,
        block[:, AO:CI],
        cg,
        block[:, CI:CO],
        block[:, SM + TAPS : SM + TAPS + KERNEL].T,
        cn,
        block[:, CO:LU],
        lg,
        block[:, LU:LD],
        block[:, LD:SM].T,
        fg,
    )
    return tuple(piece[None] for piece in outs)


def by_collectives(scalars, packed, frames, cotangent):
    section = lax.axis_index("pipe")

    def mine(block, axis=0):
        return lax.dynamic_index_in_dim(block, section, axis, keepdims=False)

    full = lax.all_gather(packed, ("pipe", "dp"), axis=0, tiled=True)
    full = full.reshape(2, 4, 2, 2, 32, COLS)
    ys, dxs, grads = plain(mine(scalars, 1), full, mine(frames), mine(cotangent))
    summed = lax.psum_scatter(
        grads.reshape(1024, COLS), ("pipe", "dp"), scatter_dimension=0, tiled=True
    ).astype(F32)

    def share(pair):
        own, other = mine(pair), jnp.where(section == 0, pair[1], pair[0])
        got = lax.ppermute(other, "pipe", [(0, 1), (1, 0)])
        return jnp.where(section == 0, jnp.stack([own, got]), jnp.stack([got, own]))

    return share(ys), share(dxs), summed


def body(frames, cotangent, lengths, stream_flags, span_sizes, *shards):
    scalars = jnp.stack([lengths[:, 0], stream_flags[:, 0], span_sizes[:, 0]])
    run = fused if lax.axis_size("dp") == 16 else by_collectives
    ys, dxs, summed = run(scalars, pack(shards), frames[:, 0], cotangent[:, 0])
    return (ys[None, :, None], dxs[None, :, None]) + unpack(summed)


def solution(mesh):
    gain, matrix, column = P("pipe", "dp"), P("pipe", "dp", None), P("pipe", None, "dp")
    weights = (gain, matrix, column, gain, matrix, matrix, gain, matrix, column, gain, matrix)
    weights = weights + (gain, matrix, column, gain)
    frames, stacked = P(None, "dp", None, None), P("pipe", None, "dp", None, None)
    return jax.shard_map(
        body,
        mesh=mesh,
        in_specs=(frames, frames) + (P(None, "dp"),) * 3 + weights,
        out_specs=(stacked, stacked) + weights,
        check_vma=False,
    )
```

```python
import functools
import math

import jax
import jax.numpy as jnp
import numpy as np
from jax import lax
from jax.experimental import pallas as pl
from jax.experimental.pallas import tpu as pltpu
from jax.sharding import PartitionSpec as P

HEADS = 8
KERNEL = 15
EPSILON = 1e-05
LOW = jnp.bfloat16
F32 = jnp.float32

EU, ED, PJ, AO, CI, CO, LU, LD, SM = 0, 2048, 4096, 5632, 6144, 7168, 7680, 9728, 11776
COLS = 11904
STEP = 512
OWNERS = [(z, y, c) for z in range(4) for y in range(2) for c in range(2)]
G_EARLY, G_ATTEND, G_CONV, G_MIX, G_LATE, G_FINAL, TAPS = 0, 1, 2, 3, 4, 5, 6


def dot(left, right):
    return lax.dot_general(left, right, (((1,), (0,)), ((), ())), preferred_element_type=F32)


def dot_t(left, right):
    return lax.dot_general(left, right, (((1,), (1,)), ((), ())), preferred_element_type=F32)


def sigmoid(values):
    return 0.5 * jnp.tanh(0.5 * values) + 0.5


def norm_hat(values):
    center = values - jnp.mean(values, axis=-1, keepdims=True)
    rate = lax.rsqrt(jnp.mean(center * center, axis=-1, keepdims=True) + EPSILON)
    return center * rate, rate


def norm_grad(grad_hat, hat, rate):
    first = jnp.mean(grad_hat, axis=-1, keepdims=True)
    second = jnp.mean(grad_hat * hat, axis=-1, keepdims=True)
    return rate * (grad_hat - first - hat * second)


class Layer:
    def __init__(self, refs, emit, need):
        self.__dict__.update(refs)
        self.emit, self.need = emit, need

    def gain(self, l, row):
        return self.sm[l, row : row + 1, :]

    def weight(self, l, column, size=STEP):
        return self.w[:, :, :, :, column : column + size].reshape(512, size)

    def enter(self, l, site, row):
        values = self.stream[...]
        hat, rate = norm_hat(values)
        self.xh[site] = hat.astype(LOW)
        self.rate[l, :, site : site + 1] = rate
        return (hat * self.gain(l, row)).astype(LOW)

    def leave(self, l, site, row, grad):
        hat = self.xh[site].astype(F32)
        rate = self.rate[l, :, site : site + 1]
        self.smg[l, row : row + 1, :] = jnp.sum(grad * hat, axis=0, keepdims=True)
        return norm_grad(grad * self.gain(l, row), hat, rate)

    def small_forward(self, l):
        self.need(l, SM)
        blocks = [self.w[z, y, c, :, SM : SM + 128].astype(F32)[:, :32] for z, y, c in OWNERS]
        self.sm[l] = jnp.concatenate(blocks, axis=1)

    def small_backward(self, l):
        blocks = [self.smg[l, :, 32 * o : 32 * o + 32] for o in range(len(OWNERS))]
        block = jnp.concatenate(blocks, axis=0)
        self.emit(l, SM, jnp.concatenate([block, jnp.zeros((512, 96), F32)], axis=1))

    def feed_forward(self, l, site, row, place, up, down):
        normed = self.enter(l, site, row)
        self.at[place] = normed.T
        side = 0 if site == 0 else 1
        total = None
        for j in range(0, 2048, STEP):
            self.need(l, up + j, down + j)
            inner = dot(normed, self.weight(l, up + j))
            self.u[side, :, j : j + STEP] = inner.astype(LOW)
            hidden = (inner * sigmoid(inner)).astype(LOW)
            term = dot_t(hidden, self.weight(l, down + j))
            total = term if total is None else total + term
            if j + STEP < 2048:
                yield
        self.stream[...] += 0.5 * total

    def feed_backward(self, l, site, row, place, up, down):
        branch = (0.5 * self.grad[...]).astype(LOW)
        turned = branch.T
        side = 0 if site == 0 else 1
        total = None
        for j in range(0, 2048, STEP):
            hidden_grad = dot(branch, self.weight(l, down + j))
            inner = self.u[side, :, j : j + STEP].astype(F32)
            gate = sigmoid(inner)
            hidden = inner * gate
            inner_grad = (hidden_grad * (gate + hidden * (1.0 - gate))).astype(LOW)
            self.emit(l, down + j, dot(turned, hidden.astype(LOW)))
            self.emit(l, up + j, dot(self.at[place], inner_grad))
            term = dot_t(inner_grad, self.weight(l, up + j))
            total = term if total is None else total + term
            if j + STEP < 2048:
                yield
        self.grad[...] += self.leave(l, site, row, total)

    def rotate(self, values, sign):
        cosine, sine = self.cos[...], self.sin[...]
        if sign < 0:
            sine = -sine
        parts = []
        for g in range(0, 512, 256):
            front, behind = values[:, g : g + 128], values[:, g + 128 : g + 256]
            parts += [front * cosine - behind * sine, front * sine + behind * cosine]
        return parts

    def pair_mask(self, j):
        lane = lax.broadcasted_iota(jnp.int32, (1, 256), 1)
        return (lane % 128) // 32 == j

    def head_mask(self, j):
        lane = lax.broadcasted_iota(jnp.int32, (1, 256), 1)
        return lane // 64 == j

    def attend_forward(self, l):
        normed = self.enter(l, 1, G_ATTEND)
        self.at[1] = normed.T
        self.need(l, PJ, PJ + 512, PJ + 1024)
        for which, scale in ((0, 0.125), (1, 1.0)):
            parts = self.rotate(dot(normed, self.weight(l, PJ + 512 * which)), 1)
            for i, part in enumerate(parts):
                self.qkv[which, :, 128 * i : 128 * i + 128] = part.astype(LOW) * LOW(scale)
        self.kt[...] = self.qkv[1].T
        value_rows = dot(normed, self.weight(l, PJ + 1024)).astype(LOW)
        self.qkv[2] = value_rows
        self.vt[...] = value_rows.T
        yield
        for h in range(HEADS):
            g, j = h // 4 * 256, h % 4
            keys = self.qkv[1, :, g : g + 256]
            keys = jnp.where(self.pair_mask(j), keys, jnp.zeros_like(keys))
            scores = dot_t(keys, self.qkv[0, :, g : g + 256]) + self.bias[...]
            powers = jnp.exp(scores - jnp.max(scores, axis=0, keepdims=True))
            powers = powers * (1.0 / jnp.sum(powers, axis=0, keepdims=True))
            powers = powers.astype(LOW)
            self.pt[h] = powers
            self.ot[64 * h : 64 * h + 64, :] = dot(
                self.vt[64 * h : 64 * h + 64, :], powers
            ).astype(LOW)
            yield
        self.need(l, AO)
        self.stream[...] += dot(self.ot[...].T, self.weight(l, AO))

    def attend_backward(self, l):
        branch = self.grad[...].astype(LOW)
        self.emit(l, AO, dot(self.ot[...], branch))
        self.ctx[...] = dot_t(branch, self.weight(l, AO)).astype(LOW)
        yield
        key_total, value_total = [], []
        for g in range(0, 512, 256):
            ctx = self.ctx[:, g : g + 256]
            queries = self.qkv[0, :, g : g + 256]
            values = self.qkv[2, :, g : g + 256]
            key_grad = value_grad = None
            for j in range(4):
                h = g // 64 + j
                head = self.head_mask(j)
                soft_grad = dot_t(jnp.where(head, values, jnp.zeros_like(values)), ctx)
                soft_low = self.pt[h]
                soft = soft_low.astype(F32)
                delta = jnp.sum(soft_grad * soft, axis=0, keepdims=True)
                score_grad = (soft * (soft_grad - delta)).astype(LOW)
                term = dot(soft_low, jnp.where(head, ctx, jnp.zeros_like(ctx)))
                value_grad = term if value_grad is None else value_grad + term
                term = dot(
                    score_grad, jnp.where(self.pair_mask(j), queries, jnp.zeros_like(queries))
                )
                key_grad = term if key_grad is None else key_grad + term
                front, behind = g + 32 * j, g + 128 + 32 * j
                rows = jnp.concatenate(
                    [self.kt[front : front + 32, :], self.kt[behind : behind + 32, :]], axis=0
                )
                turned = dot(rows, score_grad)
                self.qt[front : front + 32, :] = turned[:32]
                self.qt[behind : behind + 32, :] = turned[32:]
                yield
            key_total.append(key_grad)
            value_total.append(value_grad)
        query_grad = self.qt[...].T * 0.125
        query_grad = jnp.concatenate(self.rotate(query_grad, -1), axis=1).astype(LOW)
        key_grad = jnp.concatenate(key_total, axis=1)
        key_grad = jnp.concatenate(self.rotate(key_grad, -1), axis=1).astype(LOW)
        value_grad = jnp.concatenate(value_total, axis=1).astype(LOW)
        total = None
        for i, part in enumerate((query_grad, key_grad, value_grad)):
            self.emit(l, PJ + 512 * i, dot(self.at[1], part))
            term = dot_t(part, self.weight(l, PJ + 512 * i))
            total = term if total is None else total + term
        self.grad[...] += self.leave(l, 1, G_ATTEND, total)

    def tap(self, l, k):
        row = self.sm[l, TAPS + k : TAPS + k + 1, :]
        return row if k <= KERNEL // 2 else row * self.whole

    def convolve_forward(self, l):
        normed = self.enter(l, 2, G_CONV)
        self.at[2] = normed.T
        self.need(l, CI, CI + 512)
        first = dot(normed, self.weight(l, CI))
        second = dot(normed, self.weight(l, CI + 512))
        self.gates[:, :512] = first.astype(LOW)
        self.gates[:, 512:] = second.astype(LOW)
        n = first.shape[0]
        self.pad[0, 8 : n + 8, :] = first * sigmoid(second) * self.live[...]
        yield
        mixed = None
        for k in range(KERNEL):
            term = self.tap(l, k) * self.pad[0, k + 1 : k + 1 + n, :]
            mixed = term if mixed is None else mixed + term
        hat, rate = norm_hat(mixed)
        self.xh[5] = hat.astype(LOW)
        self.rate[l, :, 5:6] = rate
        inner = hat * self.gain(l, G_MIX)
        hidden = (inner * sigmoid(inner)).astype(LOW)
        self.wt[...] = hidden.T
        yield
        self.need(l, CO)
        self.stream[...] += dot(hidden, self.weight(l, CO))

    def convolve_backward(self, l):
        branch = self.grad[...].astype(LOW)
        n = branch.shape[0]
        self.emit(l, CO, dot(self.wt[...], branch))
        hidden_grad = dot_t(branch, self.weight(l, CO))
        yield
        hat = self.xh[5].astype(F32)
        inner = hat * self.gain(l, G_MIX)
        gate = sigmoid(inner)
        inner_grad = hidden_grad * (gate + inner * gate * (1.0 - gate))
        self.pad[1, 8 : n + 8, :] = self.leave(l, 5, G_MIX, inner_grad)
        first = self.gates[:, :512].astype(F32)
        gate = sigmoid(self.gates[:, 512:].astype(F32))
        self.pad[0, 8 : n + 8, :] = first * gate * self.live[...]
        yield
        mixed_grad = self.pad[1, 8 : n + 8, :]
        total = None
        for k in range(KERNEL):
            row = jnp.sum(mixed_grad * self.pad[0, k + 1 : k + 1 + n, :], axis=0, keepdims=True)
            if k > KERNEL // 2:
                row = row * self.whole
            self.smg[l, TAPS + k : TAPS + k + 1, :] = row
            term = self.tap(l, k) * self.pad[1, 15 - k : 15 - k + n, :]
            total = term if total is None else total + term
        total = total * self.live[...]
        first_grad = (total * gate).astype(LOW)
        second_grad = (total * first * gate * (1.0 - gate)).astype(LOW)
        yield
        self.emit(l, CI, dot(self.at[2], first_grad))
        self.emit(l, CI + 512, dot(self.at[2], second_grad))
        total = dot_t(first_grad, self.weight(l, CI))
        total = total + dot_t(second_grad, self.weight(l, CI + 512))
        self.grad[...] += self.leave(l, 2, G_CONV, total)

    def prepare(self, length, flag, span):
        n = self.stream.shape[0]
        key = lax.broadcasted_iota(jnp.int32, (n, n), 0)
        query = lax.broadcasted_iota(jnp.int32, (n, n), 1)
        width = span.astype(F32)
        key_block = jnp.floor((key.astype(F32) + 0.5) / width)
        query_block = jnp.floor((query.astype(F32) + 0.5) / width)
        shown = (key < length) & ((flag == 0) | (key_block <= query_block))
        self.bias[...] = jnp.where(shown, 0.0, -1e30)
        place = lax.broadcasted_iota(jnp.int32, (n, 1), 0)
        self.live[...] = (place < length).astype(F32)
        self.whole = jnp.where(flag == 0, 1.0, 0.0)
        self.pad[...] = jnp.zeros_like(self.pad)
        self.smg[...] = jnp.zeros_like(self.smg)

    def finish_forward(self, l):
        hat, rate = norm_hat(self.stream[...])
        self.xh[4] = hat.astype(LOW)
        self.rate[l, :, 4:5] = rate
        return (hat * self.gain(l, G_FINAL)).astype(LOW)


def act_shapes(n):
    return dict(
        xh=((6, n, 512), LOW),
        at=((4, 512, n), LOW),
        u=((2, n, 2048), LOW),
        qkv=((3, n, 512), LOW),
        kt=((512, n), LOW),
        pt=((HEADS, n, n), LOW),
        ot=((512, n), LOW),
        gates=((n, 1024), LOW),
        wt=((512, n), LOW),
    )


MODULE_ACTS = (
    (("u", 0), ("xh", 0), ("at", 0)),
    (("qkv", None), ("kt", None), ("pt", None), ("ot", None), ("xh", 1), ("at", 1)),
    (("gates", None), ("wt", None), ("xh", 2), ("xh", 5), ("at", 2)),
    (("u", 1), ("xh", 3), ("xh", 4), ("at", 3)),
)


def work_shapes(n):
    return dict(
        w=pltpu.VMEM((4, 2, 2, 32, COLS), LOW),
        stream=pltpu.VMEM((n, 512), F32),
        grad=pltpu.VMEM((n, 512), F32),
        rate=pltpu.VMEM((2, n, 128), F32),
        vt=pltpu.VMEM((512, n), LOW),
        qt=pltpu.VMEM((512, n), F32),
        ctx=pltpu.VMEM((n, 512), LOW),
        pad=pltpu.VMEM((2, n + 16, 512), F32),
        sm=pltpu.VMEM((2, 32, 512), F32),
        smg=pltpu.VMEM((2, 32, 512), F32),
        bias=pltpu.VMEM((n, n), F32),
        live=pltpu.VMEM((n, 1), F32),
        given=pltpu.VMEM((2, n, 512), LOW),
        result=pltpu.VMEM((2, n, 512), LOW),
        result_grad=pltpu.VMEM((2, n, 512), LOW),
    )
MESH = pl.DeviceIdType.MESH

FORWARD_PIECES = (
    [(SM, 128)]
    + [(base + j, STEP) for j in range(0, 2048, STEP) for base in (EU, ED)]
    + [(PJ, STEP), (PJ + 512, STEP), (PJ + 1024, STEP), (AO, STEP), (CI, STEP), (CI + 512, STEP), (CO, STEP)]
    + [(base + j, STEP) for j in range(0, 2048, STEP) for base in (LU, LD)]
)


class Place:
    def __init__(self):
        p, d = lax.axis_index("pipe"), lax.axis_index("dp")
        self.p, self.z, self.y, self.c = p, d // 4, d // 2 % 2, d % 2
        z, y, c = self.z, self.y, self.c
        self.across = (1 - p, d)
        self.beside = (p, z * 4 + (1 - y) * 2 + c)
        self.twin = (p, z * 4 + y * 2 + 1 - c)
        self.column = [(p, (z + j) % 4 * 4 + y * 2 + c) for j in (1, 2, 3)]

    def greet(self):
        for partner in [self.across, self.beside, self.twin] + self.column:
            pl.semaphore_signal(
                pltpu.get_barrier_semaphore(), inc=1, device_id=partner, device_id_type=MESH
            )

    def meet(self):
        pl.semaphore_wait(pltpu.get_barrier_semaphore(), 6)


def remote(source, target, send, arrive, device):
    return pltpu.make_async_remote_copy(
        src_ref=source, dst_ref=target, send_sem=send, recv_sem=arrive, device_id=device, device_id_type=MESH
    )


class Gather:
    def __init__(self, place, ways, shard, w, sems):
        self.place, self.ways, self.shard, self.w = place, ways, shard, w
        self.zs, self.zr, self.ys, self.yr, self.xs, self.xr, self.ds, self.dr, self.own = sems

    def cols(self, k):
        return pl.ds(*FORWARD_PIECES[k])

    def block(self, l, k, z, y):
        return self.w.at[l, z, y, self.place.c, :, self.cols(k)]

    def mine(self, l, k):
        return self.block(l, k, self.place.z, self.place.y)

    def z_copy(self, l, k, j, source=None):
        target = self.mine(l, k)
        source = target if source is None else source
        return remote(source, target, self.zs.at[l, k, j], self.zr.at[l, k, j], self.place.column[j])

    def z_wait(self, l, k):
        for j in range(3):
            got = self.block(l, k, (self.place.z + 3 - j) % 4, self.place.y)
            remote(got, got, self.zs.at[l, k, j], self.zr.at[l, k, j], self.place.column[j]).wait_recv()

    def y_copy(self, l, k, y):
        part = self.w.at[l, :, y, self.place.c, :, self.cols(k)]
        return remote(part, part, self.ys.at[l, k], self.yr.at[l, k], self.place.beside)

    def x_one(self, l, k, source=None):
        target = self.mine(l, k)
        source = target if source is None else source
        return remote(source, target, self.xs.at[l, k], self.xr.at[l, k], self.place.across)

    def x_all(self, l, k):
        part = self.w.at[l, :, :, self.place.c, :, self.cols(k)]
        return remote(part, part, self.xs.at[l, k], self.xr.at[l, k], self.place.across)

    def d_copy(self, l, k, c):
        part = self.w.at[l, :, :, c, :, self.cols(k)]
        return remote(part, part, self.ds.at[l, k], self.dr.at[l, k], self.place.twin)

    def own_copy(self):
        place = self.place
        return pltpu.make_async_copy(
            self.shard, self.w.at[place.p, place.z, place.y, place.c], self.own.at[0]
        )

    def step(self, i, l, k, owner):
        way, piece = self.ways[l][k], self.shard.at[:, self.cols(k)]

        def start():
            if way in "FG":
                self.x_one(l, k, piece).start()
            if way in "FA":
                for j in range(3):
                    self.z_copy(l, k, j, piece).start()

        def spread():
            self.x_one(l, k).wait_recv()
            for j in range(3):
                self.z_copy(l, k, j).start()

        def beside():
            self.z_wait(l, k)
            self.y_copy(l, k, self.place.y).start()

        def across():
            self.y_copy(l, k, 1 - self.place.y).wait_recv()
            if way == ("A" if owner else "G"):
                self.x_all(l, k).start()
            self.d_copy(l, k, self.place.c).start()

        def twin():
            self.x_all(l, k).wait_recv()
            self.d_copy(l, k, self.place.c).start()

        plane = self.place.p == l if owner else self.place.p != l
        pl.when(plane)((start, spread, beside, across, twin)[i])

    def arrived(self, l, k):
        self.d_copy(l, k, 1 - self.place.c).wait_recv()

    def drain(self, l, k):
        way = self.ways[l][k]
        piece = self.shard.at[:, self.cols(k)]
        self.d_copy(l, k, self.place.c).wait_send()

        @pl.when(self.place.p == l)
        def _():
            if way in "FG":
                self.x_one(l, k, piece).wait_send()
            if way == "A":
                self.x_all(l, k).wait_send()
            if way in "FA":
                for j in range(3):
                    self.z_copy(l, k, j, piece).wait_send()
                self.y_copy(l, k, self.place.y).wait_send()

        @pl.when(self.place.p != l)
        def _():
            if way == "G":
                self.x_all(l, k).wait_send()
            if way in "FG":
                for j in range(3):
                    self.z_copy(l, k, j).wait_send()
                self.y_copy(l, k, self.place.y).wait_send()


def gather_sems():
    dma, count = pltpu.SemaphoreType.DMA, len(FORWARD_PIECES)
    return [dma((2, count, 3))] * 2 + [dma((2, count))] * 6 + [dma((1,))]


BACKWARD_PIECES = (
    [(base + j, STEP) for j in range(0, 2048, STEP) for base in (LD, LU)]
    + [(CO, STEP), (CI, STEP), (CI + 512, STEP), (AO, STEP), (PJ, STEP), (PJ + 512, STEP), (PJ + 1024, STEP)]
    + [(base + j, STEP) for j in range(0, 2048, STEP) for base in (ED, EU)]
    + [(SM, 128)]
)
BACK_INDEX = {column: k for k, (column, _) in enumerate(BACKWARD_PIECES)}
STAGES = 4


class Scatter:
    def __init__(self, place, ways, out, refs, sems):
        self.place, self.ways, self.out = place, ways, out
        self.wide_slot, self.late_slot = scatter_slots(ways)
        self.stage, self.part, self.wide, self.side, self.line, self.late = refs
        self.ds, self.dr, self.xs, self.xr, self.ys, self.yr, self.zs, self.zr = sems[:8]
        self.free_d, self.free_y, self.free_z = sems[8:]
        self.count = 0
        self.slot = {}

    def width(self, k):
        return BACKWARD_PIECES[k][1]

    def cols(self, k):
        return pl.ds(0, self.width(k))

    def d_copy(self, l, k):
        source = self.stage.at[self.slot[l, k], :, :, 1 - self.place.c, :, self.cols(k)]
        target = self.part.at[k, :, :, :, self.cols(k)]
        return remote(source, target, self.ds.at[l, k], self.dr.at[l, k], self.place.twin)

    def x_wide(self, l, k):
        source = self.part.at[k, :, :, :, self.cols(k)]
        target = self.wide.at[self.wide_slot[l, k], :, :, :, self.cols(k)]
        return remote(source, target, self.xs.at[l, k], self.xr.at[l, k], self.place.across)

    def x_late(self, l, k):
        source = self.part.at[k, self.place.z, self.place.y, :, self.cols(k)]
        target = self.late.at[self.late_slot[l, k], :, self.cols(k)]
        return remote(source, target, self.xs.at[l, k], self.xr.at[l, k], self.place.across)

    def y_copy(self, l, k):
        source = self.part.at[k, :, 1 - self.place.y, :, self.cols(k)]
        target = self.side.at[k, :, :, self.cols(k)]
        return remote(source, target, self.ys.at[l, k], self.yr.at[l, k], self.place.beside)

    def z_copy(self, l, k, j):
        source = self.part.at[k, (self.place.z + j + 1) % 4, self.place.y, :, self.cols(k)]
        target = self.line.at[k, j, :, self.cols(k)]
        return remote(source, target, self.zs.at[l, k, j], self.zr.at[l, k, j], self.place.column[j])

    def offer(self, l, column, value):
        k = BACK_INDEX[column]
        width = self.width(k)
        slot = self.count % STAGES
        self.count += 1
        self.slot[l, k] = slot
        self.stage[slot, :, :, :, :, :width] = value.astype(LOW).reshape(4, 2, 2, 32, width)
        if l == 0:
            pl.semaphore_wait(self.free_d.at[k], 1)
        self.d_copy(l, k).start()

    def shared(self, k, run):
        planes = [way_planes(self.ways[l][k], l) for l in (1, 0)]
        both = planes[0] & planes[1]
        if len(both) == 2:
            run()
        elif both:
            pl.when(self.place.p == both.pop())(run)

    def y_start(self, l, k):
        if l == 0:
            self.shared(k, lambda: pl.semaphore_wait(self.free_y.at[k], 1))
        self.y_copy(l, k).start()

    def step(self, i, l, k, owner):
        way, cols = self.ways[l][k], self.cols(k)
        column = pl.ds(BACKWARD_PIECES[k][0], self.width(k))
        place = self.place

        def pair():
            self.d_copy(l, k).wait()
            slot, c = self.slot[l, k], place.c
            stage = self.stage

            def one(b, carry):
                z, y = b // 2, b % 2
                total = self.part[k, z, y, :, cols].astype(F32)
                total = total + stage[slot, z, y, c, :, cols].astype(F32)
                self.part[k, z, y, :, cols] = total.astype(LOW)
                return carry

            lax.fori_loop(0, 8, one, 0)
            if way == "F":
                self.y_start(l, k)
            else:
                plane = place.p == l if way == "G" else place.p != l
                pl.when(plane)(self.x_wide(l, k).start)

        def wide():
            self.x_wide(l, k).wait_recv()
            slot = self.wide_slot[l, k]

            def one(b, carry):
                z, y = b // 2, b % 2
                total = self.part[k, z, y, :, cols].astype(F32)
                total = total + self.wide[slot, z, y, :, cols].astype(F32)
                self.part[k, z, y, :, cols] = total.astype(LOW)
                return carry

            lax.fori_loop(0, 8, one, 0)
            self.y_start(l, k)

        def side():
            self.y_copy(l, k).wait_recv()
            y = place.y

            def one(z, carry):
                total = self.part[k, z, y, :, cols].astype(F32)
                total = total + self.side[k, z, :, cols].astype(F32)
                self.part[k, z, y, :, cols] = total.astype(LOW)
                return carry

            lax.fori_loop(0, 4, one, 0)
            for j in range(3):
                if l == 0:
                    self.shared(k, lambda: pl.semaphore_wait(self.free_z.at[k, j], 1))
                self.z_copy(l, k, j).start()

        def line():
            for j in range(3):
                self.z_copy(l, k, j).wait_recv()
            result = self.part[k, place.z, place.y, :, cols].astype(F32)
            for j in range(3):
                result = result + self.line[k, j, :, cols].astype(F32)
            if owner:
                self.out[:, column] = result
            else:
                self.part[k, place.z, place.y, :, cols] = result.astype(LOW)
                self.x_late(l, k).start()

        def late():
            self.x_late(l, k).wait_recv()
            got = self.late[self.late_slot[l, k], :, cols].astype(F32)
            self.out[:, column] = self.out[:, column] + got if way == "F" else got

        run = (pair, wide, side, line, late)[i - 1]
        if owner is None:
            run()
        else:
            pl.when(place.p == l if owner else place.p != l)(run)

    def release(self, l, k):
        way, place = self.ways[l][k], self.place

        def sent():
            self.y_copy(l, k).wait_send()
            for j in range(3):
                self.z_copy(l, k, j).wait_send()

        @pl.when(place.p == l)
        def _():
            if way == "G":
                self.x_wide(l, k).wait_send()
            else:
                sent()

        @pl.when(place.p != l)
        def _():
            if way == "A":
                self.x_wide(l, k).wait_send()
            else:
                sent()
                self.x_late(l, k).wait_send()

        if l == 0:
            return
        pl.semaphore_signal(self.free_d.at[k], inc=1, device_id=place.twin, device_id_type=MESH)

        def free():
            pl.semaphore_signal(
                self.free_y.at[k], inc=1, device_id=place.beside, device_id_type=MESH
            )
            for j in range(3):
                pl.semaphore_signal(
                    self.free_z.at[k, j], inc=1, device_id=place.column[2 - j], device_id_type=MESH
                )

        self.shared(k, free)


def way_planes(way, l):
    return {"F": {0, 1}, "A": {l}, "G": {1 - l}}[way]


def scatter_slots(ways):
    wide, late, used = {}, {}, [0, 0]
    for l in (1, 0):
        for k, way in enumerate(ways[l]):
            if way in "AG":
                plane = l if way == "A" else 1 - l
                wide[l, k] = used[plane]
                used[plane] += 1
            if way in "FG":
                late[l, k] = sum(1 for item in late if item[0] == l)
    return wide, late


def scatter_refs(ways):
    count = len(BACKWARD_PIECES)
    wide, late = scatter_slots(ways)
    return [
        pltpu.VMEM((STAGES, 4, 2, 2, 32, STEP), LOW),
        pltpu.VMEM((count, 4, 2, 32, STEP), LOW),
        pltpu.VMEM((max(wide.values()) + 1, 4, 2, 32, STEP), LOW),
        pltpu.VMEM((count, 4, 32, STEP), LOW),
        pltpu.VMEM((count, 3, 32, STEP), LOW),
        pltpu.VMEM((max(late.values()) + 1, 32, STEP), LOW),
    ]


def scatter_sems():
    dma, count = pltpu.SemaphoreType.DMA, len(BACKWARD_PIECES)
    regular = pltpu.SemaphoreType.REGULAR
    pairs = [dma((2, count))] * 6 + [dma((2, count, 3))] * 2
    return pairs + [regular((count,)), regular((count,)), regular((count, 3))]


GATHER_WAYS = ("AGAGGAGAFFFAAFGGAFAFAAGF", "AAGGFFGAAFGFFFGAAFAFFGFF")
SCATTER_WAYS = ("AFAFFAFGAAFFAGFFFGFFGGAG", "AFFAFGFGFFAAFFAFFGFGFGAG")
FORWARD_ORDER = (
    1, 4, 7, 10, 13, 149, 16, 19, 155, 22, 158, 25, 28, 289, 164, 31, 34, 293, 295, 37, 170, 40, 173, 299, 43,
    176, 302, 433, 304, 46, 437, 49, 308, 439, 310, 52, 185, 443, 188, 55, 313, 446, 191, 58, 448, 316, 61, 319,
    322, 314, 452, 64, 197, 454, 325, 317, 67, 320, 70, 203, 328, 578, 332, 73, 580, 335, 466, 337, 76, 329, 212,
    723, 584, 726, 469, 79, 586, 215, 340, 343, 82, 589, 729, 457, 732, 458, 85, 476, 460, 593, 0, 735, 346, 349,
    461, 88, 341, 479, 595, 463, 481, 224, 352, 464, 91, 738, 747, 599, 0, 741, 227, 94, 347, 750, 356, 487, 0,
    97, 230, 744, 472, 753, 358, 473, 100, 233, 361, 493, 236, 0, 103, 364, 611, 496, 106, 359, 762, 614, 0, 109,
    500, 368, 756, 484, 485, 112, 245, 619, 371, 759, 248, 115, 622, 505, 490, 373, 765, 491, 118, 251, 508, 376,
    774, 626, 0, 768, 121, 254, 0, 380, 0, 382, 374, 512, 0, 0, 124, 257, 0, 771, 0, 385, 780, 632, 377, 0, 515,
    0, 260, 127, 0, 502, 0, 0, 503, 130, 777, 388, 638, 0, 133, 392, 641, 0, 524, 136, 269, 643, 526, 783, 394,
    792, 389, 139, 529, 786, 397, 0, 789, 142, 275, 400, 395, 517, 278, 650, 404, 406, 518, 398, 536, 281, 520,
    653, 409, 521, 401, 0, 655, 795, 0, 284, 0, 658, 798, 287, 807, 801, 412, 415, 810, 804, 548, 532, 0, 550,
    418, 533, 413, 667, 553, 421, 0, 538, 671, 813, 425, 539, 0, 419, 541, 822, 674, 559, 427, 542, 422, 816, 544,
    430, 545, 679, 819, 828, 0, 428, 831, 825, 431, 569, 834, 556, 0, 557, 691, 0, 562, 695, 0, 837, 0, 563, 0, 0,
    565, 846, 698, 0, 0, 566, 0, 0, 840, 0, 843, 571, 852, 704, 572, 0, 574, 0, 855, 575, 849, 0, 712, 861, 0,
    864, 858, 0, 0, 0, 0,
)
BACKWARD_ORDER = (
    0, 0, 219, 222, 0, 225, 228, 0, 231, 0, 234, 0, 0, 237, 0, 509, 508, 512, 240, 511, 0, 243, 361, 0, 0, 0, 518,
    246, 0, 0, 517, 0, 0, 377, 0, 249, 0, 524, 252, 370, 523, 255, 0, 383, 530, 258, 653, 529, 261, 0, 505, 533,
    656, 532, 264, 521, 267, 0, 662, 514, 542, 270, 527, 541, 273, 0, 545, 391, 668, 544, 276, 394, 665, 0, 652,
    796, 942, 551, 279, 674, 550, 649, 939, 282, 0, 655, 799, 945, 554, 677, 553, 671, 413, 285, 403, 288, 658,
    948, 0, 661, 805, 951, 560, 559, 535, 419, 147, 686, 150, 808, 954, 0, 667, 811, 957, 538, 566, 689, 565, 425,
    153, 156, 814, 960, 0, 673, 817, 963, 557, 695, 676, 820, 966, 547, 431, 159, 698, 0, 162, 563, 0, 0, 165,
    679, 969, 0, 437, 427, 704, 436, 685, 829, 975, 168, 569, 701, 682, 972, 0, 688, 832, 978, 443, 171, 289, 710,
    442, 0, 0, 0, 446, 174, 575, 0, 0, 445, 707, 0, 694, 838, 984, 0, 0, 177, 691, 981, 0, 295, 697, 841, 987,
    452, 180, 451, 713, 183, 0, 571, 311, 703, 847, 993, 186, 304, 581, 719, 844, 990, 189, 0, 433, 709, 853, 999,
    464, 192, 587, 463, 850, 996, 195, 0, 439, 467, 313, 590, 466, 198, 455, 316, 856, 1002, 201, 715, 1005, 0,
    329, 596, 448, 476, 204, 475, 862, 1008, 0, 580, 724, 870, 479, 207, 325, 478, 482, 210, 481, 599, 586, 730,
    876, 457, 341, 213, 608, 589, 733, 879, 460, 488, 216, 473, 611, 487, 491, 490, 595, 739, 885, 350, 469, 353,
    620, 485, 623, 617, 359, 626, 607, 751, 897, 610, 754, 900, 494, 355, 632, 497, 635, 629, 619, 763, 909, 503,
    622, 766, 912, 638, 625, 769, 915, 641, 499, 631, 775, 921, 647, 634, 778, 924, 577, 867, 583, 873, 592, 882,
    601, 891, 604, 894, 613, 903, 643, 933, 742, 888, 760, 906, 772, 918, 781, 927, 784, 930, 790, 936,
)


FORWARD_CHUNKS, BACKWARD_CHUNKS, SHARES = 23, 23, 8
MATRICES = ((EU, 2048), (ED, 2048), (PJ, 1536), (AO, 512), (CI, 1024), (CO, 512), (LU, 2048), (LD, 2048))


def swap_halves(columns, back=False):
    parts = []
    for g in range(0, 1024, 256):
        for i in range(8):
            a, b = divmod(i, 2 if back else 4)
            start = g + (b * 128 + a * 32 if back else b * 64 + a * 32)
            parts.append(columns[:, start : start + 32])
    return jnp.concatenate(parts, axis=1)


def fused_kernel(groups, length, flag, span, frames, cotangent, *rest):
    n_acts, act_names, work_names, n = groups
    matrices, small, rest = rest[:8], rest[8:15], rest[15:]
    cos, sin, y_out, dx_out, g_out, w, *rest = rest
    kept, rest = dict(zip(act_names, rest[:n_acts])), rest[n_acts:]
    acts, rest = dict(zip(act_names, rest[:n_acts])), rest[n_acts:]
    work, rest = dict(zip(work_names, rest[: len(work_names)])), rest[len(work_names) :]
    back_refs, rest = rest[:6], rest[6:]
    gather_sem, rest = rest[:9], rest[9:]
    scatter_sem, rest = rest[:11], rest[11:]
    load_sem, keep_sem, given_sem, share_send, share_arrive, shard_sem, shard, proj, rows = rest

    place = Place()
    place.greet()
    p = place.p
    given = [
        pltpu.make_async_copy(source.at[p], work["given"].at[i], given_sem.at[i])
        for i, source in enumerate((frames, cotangent))
    ]
    for copy in given:
        copy.start()
    pieces = []
    for i, (column, width) in enumerate(MATRICES):
        target = proj if column == PJ else shard.at[:, pl.ds(column, width)]
        pieces.append(pltpu.make_async_copy(matrices[i], target, shard_sem.at[i]))
        pieces[-1].start()
    rows[...] = jnp.zeros_like(rows)
    for i, gain in enumerate(small[:6]):
        rows[i : i + 1, :32] = gain[...].astype(F32)
    rows[TAPS : TAPS + KERNEL, :32] = small[6][...].astype(F32)
    shard[:, SM:] = rows[...].astype(LOW)
    for copy in pieces:
        copy.wait()
    shard[:, PJ : PJ + 1024] = swap_halves(proj[:, :1024].astype(F32)).astype(LOW)
    shard[:, PJ + 1024 : AO] = proj[:, 1024:]
    gather = Gather(place, GATHER_WAYS, shard, w, gather_sem)
    gather.own_copy().start()
    place.meet()
    gather.own_copy().wait()

    count = len(FORWARD_PIECES)
    number = {column: k for k, (column, _) in enumerate(FORWARD_PIECES)}
    waiting = []

    def load(l, k):
        cols = gather.cols(k)
        return pltpu.make_async_copy(
            w.at[l, :, :, :, :, cols], work["w"].at[:, :, :, :, cols], load_sem.at[l, k]
        )

    def need(l, *columns):
        for column in columns:
            load(l, number[column]).wait()

    def keep(module, back):
        copies = []
        for i, (name, index) in enumerate(MODULE_ACTS[module]):
            near, far = acts[name], kept[name]
            if index is not None:
                near, far = near.at[index], far.at[index]
            source, target = (far, near) if back else (near, far)
            copies.append(pltpu.make_async_copy(source, target, keep_sem.at[int(back), module, i]))
        return copies

    scatter = Scatter(place, SCATTER_WAYS, g_out, back_refs, scatter_sem)
    run = Layer({**acts, **work, "cos": cos, "sin": sin}, scatter.offer, need)

    def share(i, l, q):
        results, out = ((run.result, y_out), (run.result_grad, dx_out))[i]
        rows = pl.ds(q * (n // SHARES), n // SHARES)
        source, send, arrive = results.at[l, rows], share_send.at[i, l, q], share_arrive.at[i, q]
        own = pltpu.make_async_copy(source, out.at[p, rows], send)
        away = remote(source, out.at[p, rows], send, arrive, place.across)
        expected = remote(source, out.at[1 - p, rows], send, arrive, place.across)
        return own, away, expected

    def share_start(i, l, q):
        own, away, _ = share(i, l, q)
        pl.when(p == l)(own.start)
        pl.when(p != l)(away.start)

    def share_finish(i, l, q):
        own, away, expected = share(i, l, q)
        pl.when(p == l)(own.wait)

        @pl.when(p != l)
        def _():
            away.wait_send()
            expected.wait_recv()

    def forward():
        modules = (
            lambda l: run.feed_forward(l, 0, G_EARLY, 0, EU, ED),
            run.attend_forward,
            run.convolve_forward,
            lambda l: run.feed_forward(l, 3, G_LATE, 3, LU, LD),
        )
        for l in range(2):
            run.small_forward(l)
            yield
            for m, module in enumerate(modules):
                if l == 1:
                    for copy in keep(m, False):
                        copy.wait()
                yield from module(l)
                if l == 0:
                    for copy in keep(m, False):
                        if m < 3:
                            copy.start()
                yield
            run.result[l] = run.finish_forward(l)
            if l == 0:
                for copy in keep(3, False):
                    copy.start()
                run.stream[...] = run.result[0].astype(F32)
                for item in waiting:
                    load(*item).start()
                waiting.clear()
                run.first_done = True
            yield

    def reload(m):
        columns = ((EU, 4096), (PJ, 2048), (CI, 1536), (LU, 4096))
        cols = pl.ds(*columns[m])
        return pltpu.make_async_copy(
            w.at[0, :, :, :, :, cols], work["w"].at[:, :, :, :, cols], load_sem.at[0, m]
        )

    def backward():
        modules = (
            lambda l: run.feed_backward(l, 0, G_EARLY, 0, EU, ED),
            run.attend_backward,
            run.convolve_backward,
            lambda l: run.feed_backward(l, 3, G_LATE, 3, LU, LD),
        )
        for l in (1, 0):
            if l == 0:
                for copy in keep(3, True):
                    copy.wait()
            start = run.given[1].astype(F32) if l == 1 else run.result_grad[1].astype(F32)
            run.grad[...] = run.leave(l, 4, G_FINAL, start)
            for m in (3, 2, 1, 0):
                if l == 0:
                    if m < 3:
                        for copy in keep(m, True):
                            copy.wait()
                    reload(m).wait()
                yield from modules[m](l)
                if l == 1:
                    for copy in keep(m, True):
                        copy.start()
                    reload(m).start()
                yield
            run.small_backward(l)
            run.result_grad[l] = run.grad[...].astype(LOW)
            yield

    def item(code):
        if code == 0:
            return None, None, None, None
        code, owner = divmod(code - 1, 3)
        code, k = divmod(code, count)
        return code // 2, code % 2, k, (True, False, None)[owner]

    run.first_done = False
    chunks, chunk, prepared = forward(), 0, False
    for code in FORWARD_ORDER:
        i, l, k, owner = item(code)
        if not prepared and (code == 0 or i > 0):
            run.prepare(length[p], flag[p], span[p])
            given[0].wait()
            run.stream[...] = run.given[0].astype(F32)
            prepared = True
        if code == 0:
            next(chunks)
            if 0 <= chunk - FORWARD_CHUNKS < SHARES:
                share_start(0, 0, chunk - FORWARD_CHUNKS)
            chunk += 1
            continue
        if i < 5:
            gather.step(i, l, k, owner)
            continue
        gather.arrived(l, k)
        if l == 0 or run.first_done:
            load(l, k).start()
        else:
            waiting.append((l, k))
    given[1].wait()
    chunks, chunk = backward(), 0
    left = [(l, k) for l in range(2) for k in range(count)]
    for code in BACKWARD_ORDER:
        if code == 0:
            next(chunks)
            if left:
                gather.drain(*left.pop(0))
            if chunk < SHARES:
                share_start(0, 1, chunk)
            if 0 <= chunk - BACKWARD_CHUNKS < SHARES:
                share_start(1, 1, chunk - BACKWARD_CHUNKS)
            chunk += 1
            if chunk == 2 * BACKWARD_CHUNKS:
                for q in range(SHARES):
                    share_start(1, 0, q)
            continue
        i, l, k, owner = item(code)
        if i < 6:
            scatter.step(i, l, k, owner)
        else:
            scatter.release(l, k)
    for rest in left:
        gather.drain(*rest)
    for i in range(2):
        for l in range(2):
            for q in range(SHARES):
                share_finish(i, l, q)


def tables(n):
    rates = np.exp(np.arange(32, dtype=np.float64) * (-2.0 * math.log(10000.0) / 64))
    phases = np.arange(n, dtype=np.float64)[:, None] * np.tile(rates, 4)[None, :]
    return np.cos(phases).astype(np.float32), np.sin(phases).astype(np.float32)


def fused(lengths, flags, spans, frames, cotangent, shards):
    n = frames.shape[1]
    acts, work = act_shapes(n), work_shapes(n)
    cosine, sine = tables(n)
    eg, eu, ed, ag, pj, ao, cg, ci, cd, cn, co, lg, lu, ld, fg = shards
    matrices = [eu[0], ed[0].T, pj[0], ao[0], ci[0], co[0], lu[0], ld[0].T]
    small = [eg, ag, cg, cn, lg, fg, cd[0]]
    vmem = pl.BlockSpec(memory_space=pltpu.VMEM)
    hbm = pl.BlockSpec(memory_space=pl.ANY)
    smem = pl.BlockSpec(memory_space=pltpu.SMEM)
    dma, count = pltpu.SemaphoreType.DMA, len(FORWARD_PIECES)
    groups = (len(acts), tuple(acts), tuple(work), n)
    outs = pl.pallas_call(
        functools.partial(fused_kernel, groups),
        out_shape=[
            jax.ShapeDtypeStruct((2, n, 512), LOW),
            jax.ShapeDtypeStruct((2, n, 512), LOW),
            jax.ShapeDtypeStruct((32, COLS), F32),
            jax.ShapeDtypeStruct((2, 4, 2, 2, 32, COLS), LOW),
        ]
        + [jax.ShapeDtypeStruct(shape, kind) for shape, kind in acts.values()],
        in_specs=[smem] * 3 + [hbm] * 10 + [vmem] * 9,
        out_specs=[hbm, hbm, vmem, hbm] + [hbm] * len(acts),
        scratch_shapes=[pltpu.VMEM(shape, kind) for shape, kind in acts.values()]
        + list(work.values())
        + scatter_refs(SCATTER_WAYS)
        + gather_sems()
        + scatter_sems()
        + [dma((2, count)), dma((2, 4, 6)), dma((2,)), dma((2, 2, SHARES)), dma((2, SHARES)), dma((8,))]
        + [
            pltpu.VMEM((32, COLS), LOW),
            pltpu.VMEM((32, 1536), LOW),
            pltpu.VMEM((32, 128), F32),
        ],
        compiler_params=pltpu.CompilerParams(
            collective_id=0, has_side_effects=True, vmem_limit_bytes=63 * 2**20
        ),
        cost_estimate=pl.CostEstimate(
            flops=30 * 10**9, bytes_accessed=100 * 2**20, transcendentals=10**7
        ),
    )(lengths[:, 0], flags[:, 0], spans[:, 0], frames, cotangent, *matrices, *small, jnp.asarray(cosine), jnp.asarray(sine))
    return finish(*outs[:3])


def finish_kernel(y, dx, g, y_out, dx_out, *outs):
    y_out[...] = y[...]
    dx_out[...] = dx[...]
    matrices, small = outs[:8], outs[8:]
    for out, (column, width) in zip(matrices, MATRICES):
        if column == PJ:
            out[:, :1024] = swap_halves(g[:, PJ : PJ + 1024], True)
            out[:, 1024:] = g[:, PJ + 1024 : AO]
        else:
            out[...] = g[:, column : column + width]
    for i in range(6):
        small[i][...] = g[i : i + 1, SM : SM + 32]
    small[6][...] = g[TAPS : TAPS + KERNEL, SM : SM + 32]


def finish(y, dx, g):
    widths = [(32, width) for _, width in MATRICES] + [(1, 32)] * 6 + [(KERNEL, 32)]
    vmem = pl.BlockSpec(memory_space=pltpu.VMEM)
    y, dx, eu, ed, pj, ao, ci, co, lu, ld, eg, ag, cg, cn, lg, fg, cd = pl.pallas_call(
        finish_kernel,
        out_shape=[jax.ShapeDtypeStruct(y.shape, LOW)] * 2
        + [jax.ShapeDtypeStruct(shape, F32) for shape in widths],
        in_specs=[vmem] * 3,
        out_specs=[vmem] * 17,
        compiler_params=pltpu.CompilerParams(vmem_limit_bytes=32 * 2**20),
    )(y, dx, g)
    return (
        y[None, :, None],
        dx[None, :, None],
        eg,
        eu[None],
        ed.T[None],
        ag,
        pj[None],
        ao[None],
        cg,
        ci[None],
        cd[None],
        cn,
        co[None],
        lg,
        lu[None],
        ld.T[None],
        fg,
    )


def plain_kernel(groups, scalars, w, frames, cotangent, cos, sin, y_out, dx_out, g_out, *rest):
    n_acts, act_names, work_names, n = groups
    kept, rest = dict(zip(act_names, rest[:n_acts])), rest[n_acts:]
    acts, rest = dict(zip(act_names, rest[:n_acts])), rest[n_acts:]
    work, rest = dict(zip(work_names, rest[: len(work_names)])), rest[len(work_names) :]
    stage, sem = rest

    def move(source, target):
        copy = pltpu.make_async_copy(source, target, sem)
        copy.start()
        copy.wait()

    def emit(l, column, value):
        width = value.shape[1]
        stage[:, :width] = value.astype(LOW)
        move(stage.at[:, pl.ds(0, width)], g_out.at[l, :, pl.ds(column, width)])

    run = Layer({**acts, **work, "cos": cos, "sin": sin}, emit, lambda *_: None)

    def whole(*modules):
        for module in modules:
            for _ in module:
                pass

    move(frames, run.given.at[0])
    move(cotangent, run.given.at[1])
    run.prepare(scalars[0], scalars[1], scalars[2])
    run.stream[...] = run.given[0].astype(F32)
    for l in range(2):
        move(w.at[l], work["w"])
        run.small_forward(l)
        whole(
            run.feed_forward(l, 0, G_EARLY, 0, EU, ED),
            run.attend_forward(l),
            run.convolve_forward(l),
            run.feed_forward(l, 3, G_LATE, 3, LU, LD),
        )
        run.result[l] = run.finish_forward(l)
        run.stream[...] = run.result[l].astype(F32)
        if l == 0:
            for name in act_names:
                move(acts[name], kept[name])
    for l in (1, 0):
        if l == 0:
            move(w.at[0], work["w"])
            for name in act_names:
                move(kept[name], acts[name])
        start = run.given[1].astype(F32) if l == 1 else run.result_grad[1].astype(F32)
        run.grad[...] = run.leave(l, 4, G_FINAL, start)
        whole(
            run.feed_backward(l, 3, G_LATE, 3, LU, LD),
            run.convolve_backward(l),
            run.attend_backward(l),
            run.feed_backward(l, 0, G_EARLY, 0, EU, ED),
        )
        run.small_backward(l)
        run.result_grad[l] = run.grad[...].astype(LOW)
    move(run.result, y_out)
    move(run.result_grad, dx_out)


def plain(scalars, weights, frames, cotangent):
    n = frames.shape[0]
    acts, work = act_shapes(n), work_shapes(n)
    cosine, sine = tables(n)
    vmem = pl.BlockSpec(memory_space=pltpu.VMEM)
    hbm = pl.BlockSpec(memory_space=pl.ANY)
    outs = pl.pallas_call(
        functools.partial(plain_kernel, (len(acts), tuple(acts), tuple(work), n)),
        out_shape=[
            jax.ShapeDtypeStruct((2, n, 512), LOW),
            jax.ShapeDtypeStruct((2, n, 512), LOW),
            jax.ShapeDtypeStruct((2, 512, COLS), LOW),
        ]
        + [jax.ShapeDtypeStruct(shape, kind) for shape, kind in acts.values()],
        in_specs=[pl.BlockSpec(memory_space=pltpu.SMEM), hbm, hbm, hbm, vmem, vmem],
        out_specs=[hbm] * (3 + len(acts)),
        scratch_shapes=[pltpu.VMEM(shape, kind) for shape, kind in acts.values()]
        + list(work.values())
        + [pltpu.VMEM((512, STEP), LOW), pltpu.SemaphoreType.DMA],
        compiler_params=pltpu.CompilerParams(vmem_limit_bytes=60 * 2**20),
    )(scalars, weights, frames, cotangent, jnp.asarray(cosine), jnp.asarray(sine))
    return outs[:3]


def pack(shards):
    eg, eu, ed, ag, pj, ao, cg, ci, cd, cn, co, lg, lu, ld, fg = (piece[0] for piece in shards)
    rows = eu.shape[0]
    small = jnp.concatenate(
        [gain[:, None] for gain in (eg, ag, cg, cn, lg, fg)]
        + [cd.T, jnp.zeros((rows, 128 - 6 - KERNEL), LOW)],
        axis=1,
    )
    proj = jnp.concatenate([swap_halves(pj[:, :1024]), pj[:, 1024:]], axis=1)
    return jnp.concatenate([eu, ed.T, proj, ao, ci, co, lu, ld.T, small], axis=1)


def unpack(block):
    proj = block[:, PJ : PJ + 1536]
    proj = jnp.concatenate([swap_halves(proj[:, :1024], True), proj[:, 1024:]], axis=1)
    gains = [block[:, SM + i] for i in range(6)]
    eg, ag, cg, cn, lg, fg = gains
    outs = (
        eg,
        block[:, EU:ED],
        block[:, ED:PJ].T,
        ag,
        proj,
        block[:, AO:CI],
        cg,
        block[:, CI:CO],
        block[:, SM + TAPS : SM + TAPS + KERNEL].T,
        cn,
        block[:, CO:LU],
        lg,
        block[:, LU:LD],
        block[:, LD:SM].T,
        fg,
    )
    return tuple(piece[None] for piece in outs)


def turn_small(block):
    small = block[..., SM : SM + 32].reshape(2, len(OWNERS), 32, 32).swapaxes(2, 3)
    small = jnp.pad(small.reshape(2, 512, 32), ((0, 0), (0, 0), (0, 96)))
    return jnp.concatenate([block[..., :SM], small], axis=2)


def by_collectives(lengths, flags, spans, frames, cotangent, shards):
    section = lax.axis_index("pipe")

    def mine(block):
        return lax.dynamic_index_in_dim(block, section, 0, keepdims=False)

    full = lax.all_gather(pack(shards), ("pipe", "dp"), axis=0, tiled=True)
    full = turn_small(full.reshape(2, 512, COLS)).reshape(2, 4, 2, 2, 32, COLS)
    scalars = jnp.stack([mine(lengths)[0], mine(flags)[0], mine(spans)[0]])
    ys, dxs, grads = plain(scalars, full, mine(frames), mine(cotangent))
    summed = lax.psum_scatter(
        turn_small(grads).reshape(1024, COLS), ("pipe", "dp"), scatter_dimension=0, tiled=True
    ).astype(F32)

    def share(pair):
        own, other = mine(pair), jnp.where(section == 0, pair[1], pair[0])
        got = lax.ppermute(other, "pipe", [(0, 1), (1, 0)])
        pair = jnp.where(section == 0, jnp.stack([own, got]), jnp.stack([got, own]))
        return pair[None, :, None]

    return (share(ys), share(dxs)) + unpack(summed)


def body(frames, cotangent, lengths, stream_flags, span_sizes, *shards):
    run = fused if lax.axis_size("dp") == 16 else by_collectives
    return run(lengths, stream_flags, span_sizes, frames[:, 0], cotangent[:, 0], shards)


def solution(mesh):
    gain, matrix, column = P("pipe", "dp"), P("pipe", "dp", None), P("pipe", None, "dp")
    weights = (gain, matrix, column, gain, matrix, matrix, gain, matrix, column, gain, matrix)
    weights = weights + (gain, matrix, column, gain)
    frames, stacked = P(None, "dp", None, None), P("pipe", None, "dp", None, None)
    return jax.shard_map(
        body,
        mesh=mesh,
        in_specs=(frames, frames) + (P(None, "dp"),) * 3 + weights,
        out_specs=(stacked, stacked) + weights,
        check_vma=False,
    )
```

```python
import functools
import math

import jax
import jax.numpy as jnp
import numpy as np
from jax import lax
from jax.experimental import pallas as pl
from jax.experimental.pallas import tpu as pltpu
from jax.sharding import PartitionSpec as P

HEADS = 8
KERNEL = 15
EPSILON = 1e-05
LOW = jnp.bfloat16
F32 = jnp.float32

EU, ED, PJ, AO, CI, CO, LU, LD, SM = 0, 2048, 4096, 5632, 6144, 7168, 7680, 9728, 11776
COLS = 11904
STEP = 512
OWNERS = [(z, y, c) for z in range(4) for y in range(2) for c in range(2)]
G_EARLY, G_ATTEND, G_CONV, G_MIX, G_LATE, G_FINAL, TAPS = 0, 1, 2, 3, 4, 5, 6


def dot(left, right):
    return lax.dot_general(left, right, (((1,), (0,)), ((), ())), preferred_element_type=F32)


def dot_t(left, right):
    return lax.dot_general(left, right, (((1,), (1,)), ((), ())), preferred_element_type=F32)


def sigmoid(values):
    return 0.5 * jnp.tanh(0.5 * values) + 0.5


def norm_hat(values):
    center = values - jnp.mean(values, axis=-1, keepdims=True)
    rate = lax.rsqrt(jnp.mean(center * center, axis=-1, keepdims=True) + EPSILON)
    return center * rate, rate


def norm_grad(grad_hat, hat, rate):
    first = jnp.mean(grad_hat, axis=-1, keepdims=True)
    second = jnp.mean(grad_hat * hat, axis=-1, keepdims=True)
    return rate * (grad_hat - first - hat * second)


class Layer:
    def __init__(self, refs, emit, need):
        self.__dict__.update(refs)
        self.emit, self.need = emit, need

    def gain(self, l, row):
        return self.sm[l, row : row + 1, :]

    def weight(self, l, column, size=STEP):
        return self.w[:, :, :, :, column : column + size].reshape(512, size)

    def enter(self, l, site, row):
        values = self.stream[...]
        hat, rate = norm_hat(values)
        self.xh[site] = hat.astype(LOW)
        self.rate[l, :, site : site + 1] = rate
        return (hat * self.gain(l, row)).astype(LOW)

    def leave(self, l, site, row, grad):
        hat = self.xh[site].astype(F32)
        rate = self.rate[l, :, site : site + 1]
        self.smg[l, row : row + 1, :] = jnp.sum(grad * hat, axis=0, keepdims=True)
        return norm_grad(grad * self.gain(l, row), hat, rate)

    def small_forward(self, l):
        self.need(l, SM)
        blocks = [self.w[z, y, c, :, SM : SM + 128].astype(F32)[:, :32] for z, y, c in OWNERS]
        self.sm[l] = jnp.concatenate(blocks, axis=1)

    def small_backward(self, l):
        blocks = [self.smg[l, :, 32 * o : 32 * o + 32] for o in range(len(OWNERS))]
        block = jnp.concatenate(blocks, axis=0)
        self.emit(l, SM, jnp.concatenate([block, jnp.zeros((512, 96), F32)], axis=1))

    def feed_forward(self, l, site, row, place, up, down):
        normed = self.enter(l, site, row)
        self.at[place] = normed.T
        side = 0 if site == 0 else 1
        total = None
        for j in range(0, 2048, STEP):
            self.need(l, up + j, down + j)
            inner = dot(normed, self.weight(l, up + j))
            self.u[side, :, j : j + STEP] = inner.astype(LOW)
            hidden = (inner * sigmoid(inner)).astype(LOW)
            term = dot_t(hidden, self.weight(l, down + j))
            total = term if total is None else total + term
            if j + STEP < 2048:
                yield
        self.stream[...] += 0.5 * total

    def feed_backward(self, l, site, row, place, up, down):
        branch = (0.5 * self.grad[...]).astype(LOW)
        turned = branch.T
        side = 0 if site == 0 else 1
        total = None
        for j in range(0, 2048, STEP):
            hidden_grad = dot(branch, self.weight(l, down + j))
            inner = self.u[side, :, j : j + STEP].astype(F32)
            gate = sigmoid(inner)
            hidden = inner * gate
            inner_grad = (hidden_grad * (gate + hidden * (1.0 - gate))).astype(LOW)
            self.emit(l, down + j, dot(turned, hidden.astype(LOW)))
            self.emit(l, up + j, dot(self.at[place], inner_grad))
            term = dot_t(inner_grad, self.weight(l, up + j))
            total = term if total is None else total + term
            if j + STEP < 2048:
                yield
        self.grad[...] += self.leave(l, site, row, total)

    def rotate(self, values, sign):
        cosine, sine = self.cos[...], self.sin[...]
        if sign < 0:
            sine = -sine
        parts = []
        for g in range(0, 512, 256):
            front, behind = values[:, g : g + 128], values[:, g + 128 : g + 256]
            parts += [front * cosine - behind * sine, front * sine + behind * cosine]
        return parts

    def pair_mask(self, j):
        lane = lax.broadcasted_iota(jnp.int32, (1, 256), 1)
        return (lane % 128) // 32 == j

    def head_mask(self, j):
        lane = lax.broadcasted_iota(jnp.int32, (1, 256), 1)
        return lane // 64 == j

    def attend_forward(self, l):
        normed = self.enter(l, 1, G_ATTEND)
        self.at[1] = normed.T
        self.need(l, PJ, PJ + 512, PJ + 1024)
        for which, scale in ((0, 0.125), (1, 1.0)):
            parts = self.rotate(dot(normed, self.weight(l, PJ + 512 * which)), 1)
            for i, part in enumerate(parts):
                self.qkv[which, :, 128 * i : 128 * i + 128] = part.astype(LOW) * LOW(scale)
        self.kt[...] = self.qkv[1].T
        value_rows = dot(normed, self.weight(l, PJ + 1024)).astype(LOW)
        self.qkv[2] = value_rows
        self.vt[...] = value_rows.T
        yield
        for h in range(HEADS):
            g, j = h // 4 * 256, h % 4
            keys = self.qkv[1, :, g : g + 256]
            keys = jnp.where(self.pair_mask(j), keys, jnp.zeros_like(keys))
            scores = dot_t(keys, self.qkv[0, :, g : g + 256]) + self.bias[...]
            powers = jnp.exp(scores - jnp.max(scores, axis=0, keepdims=True))
            powers = powers * (1.0 / jnp.sum(powers, axis=0, keepdims=True))
            powers = powers.astype(LOW)
            self.pt[h] = powers
            self.ot[64 * h : 64 * h + 64, :] = dot(
                self.vt[64 * h : 64 * h + 64, :], powers
            ).astype(LOW)
            yield
        self.need(l, AO)
        self.stream[...] += dot(self.ot[...].T, self.weight(l, AO))

    def attend_backward(self, l):
        branch = self.grad[...].astype(LOW)
        self.emit(l, AO, dot(self.ot[...], branch))
        self.ctx[...] = dot_t(branch, self.weight(l, AO)).astype(LOW)
        yield
        key_total, value_total = [], []
        for g in range(0, 512, 256):
            ctx = self.ctx[:, g : g + 256]
            queries = self.qkv[0, :, g : g + 256]
            values = self.qkv[2, :, g : g + 256]
            key_grad = value_grad = None
            for j in range(4):
                h = g // 64 + j
                head = self.head_mask(j)
                soft_grad = dot_t(jnp.where(head, values, jnp.zeros_like(values)), ctx)
                soft_low = self.pt[h]
                soft = soft_low.astype(F32)
                delta = jnp.sum(soft_grad * soft, axis=0, keepdims=True)
                score_grad = (soft * (soft_grad - delta)).astype(LOW)
                term = dot(soft_low, jnp.where(head, ctx, jnp.zeros_like(ctx)))
                value_grad = term if value_grad is None else value_grad + term
                term = dot(
                    score_grad, jnp.where(self.pair_mask(j), queries, jnp.zeros_like(queries))
                )
                key_grad = term if key_grad is None else key_grad + term
                front, behind = g + 32 * j, g + 128 + 32 * j
                rows = jnp.concatenate(
                    [self.kt[front : front + 32, :], self.kt[behind : behind + 32, :]], axis=0
                )
                turned = dot(rows, score_grad)
                self.qt[front : front + 32, :] = turned[:32]
                self.qt[behind : behind + 32, :] = turned[32:]
                yield
            key_total.append(key_grad)
            value_total.append(value_grad)
        query_grad = self.qt[...].T * 0.125
        query_grad = jnp.concatenate(self.rotate(query_grad, -1), axis=1).astype(LOW)
        key_grad = jnp.concatenate(key_total, axis=1)
        key_grad = jnp.concatenate(self.rotate(key_grad, -1), axis=1).astype(LOW)
        value_grad = jnp.concatenate(value_total, axis=1).astype(LOW)
        total = None
        for i, part in enumerate((query_grad, key_grad, value_grad)):
            self.emit(l, PJ + 512 * i, dot(self.at[1], part))
            term = dot_t(part, self.weight(l, PJ + 512 * i))
            total = term if total is None else total + term
        self.grad[...] += self.leave(l, 1, G_ATTEND, total)

    def tap(self, l, k):
        row = self.sm[l, TAPS + k : TAPS + k + 1, :]
        return row if k <= KERNEL // 2 else row * self.whole

    def convolve_forward(self, l):
        normed = self.enter(l, 2, G_CONV)
        self.at[2] = normed.T
        self.need(l, CI, CI + 512)
        first = dot(normed, self.weight(l, CI))
        second = dot(normed, self.weight(l, CI + 512))
        self.gates[:, :512] = first.astype(LOW)
        self.gates[:, 512:] = second.astype(LOW)
        n = first.shape[0]
        self.pad[0, 8 : n + 8, :] = first * sigmoid(second) * self.live[...]
        yield
        mixed = None
        for k in range(KERNEL):
            term = self.tap(l, k) * self.pad[0, k + 1 : k + 1 + n, :]
            mixed = term if mixed is None else mixed + term
        hat, rate = norm_hat(mixed)
        self.xh[5] = hat.astype(LOW)
        self.rate[l, :, 5:6] = rate
        inner = hat * self.gain(l, G_MIX)
        hidden = (inner * sigmoid(inner)).astype(LOW)
        self.wt[...] = hidden.T
        yield
        self.need(l, CO)
        self.stream[...] += dot(hidden, self.weight(l, CO))

    def convolve_backward(self, l):
        branch = self.grad[...].astype(LOW)
        n = branch.shape[0]
        self.emit(l, CO, dot(self.wt[...], branch))
        hidden_grad = dot_t(branch, self.weight(l, CO))
        yield
        hat = self.xh[5].astype(F32)
        inner = hat * self.gain(l, G_MIX)
        gate = sigmoid(inner)
        inner_grad = hidden_grad * (gate + inner * gate * (1.0 - gate))
        self.pad[1, 8 : n + 8, :] = self.leave(l, 5, G_MIX, inner_grad)
        first = self.gates[:, :512].astype(F32)
        gate = sigmoid(self.gates[:, 512:].astype(F32))
        self.pad[0, 8 : n + 8, :] = first * gate * self.live[...]
        yield
        mixed_grad = self.pad[1, 8 : n + 8, :]
        total = None
        for k in range(KERNEL):
            row = jnp.sum(mixed_grad * self.pad[0, k + 1 : k + 1 + n, :], axis=0, keepdims=True)
            if k > KERNEL // 2:
                row = row * self.whole
            self.smg[l, TAPS + k : TAPS + k + 1, :] = row
            term = self.tap(l, k) * self.pad[1, 15 - k : 15 - k + n, :]
            total = term if total is None else total + term
        total = total * self.live[...]
        first_grad = (total * gate).astype(LOW)
        second_grad = (total * first * gate * (1.0 - gate)).astype(LOW)
        yield
        self.emit(l, CI, dot(self.at[2], first_grad))
        self.emit(l, CI + 512, dot(self.at[2], second_grad))
        total = dot_t(first_grad, self.weight(l, CI))
        total = total + dot_t(second_grad, self.weight(l, CI + 512))
        self.grad[...] += self.leave(l, 2, G_CONV, total)

    def prepare(self, length, flag, span):
        n = self.stream.shape[0]
        key = lax.broadcasted_iota(jnp.int32, (n, n), 0)
        query = lax.broadcasted_iota(jnp.int32, (n, n), 1)
        width = span.astype(F32)
        key_block = jnp.floor((key.astype(F32) + 0.5) / width)
        query_block = jnp.floor((query.astype(F32) + 0.5) / width)
        shown = (key < length) & ((flag == 0) | (key_block <= query_block))
        self.bias[...] = jnp.where(shown, 0.0, -1e30)
        place = lax.broadcasted_iota(jnp.int32, (n, 1), 0)
        self.live[...] = (place < length).astype(F32)
        self.whole = jnp.where(flag == 0, 1.0, 0.0)
        self.pad[...] = jnp.zeros_like(self.pad)
        self.smg[...] = jnp.zeros_like(self.smg)

    def finish_forward(self, l):
        hat, rate = norm_hat(self.stream[...])
        self.xh[4] = hat.astype(LOW)
        self.rate[l, :, 4:5] = rate
        return (hat * self.gain(l, G_FINAL)).astype(LOW)


def act_shapes(n):
    return dict(
        xh=((6, n, 512), LOW),
        at=((4, 512, n), LOW),
        u=((2, n, 2048), LOW),
        qkv=((3, n, 512), LOW),
        kt=((512, n), LOW),
        pt=((HEADS, n, n), LOW),
        ot=((512, n), LOW),
        gates=((n, 1024), LOW),
        wt=((512, n), LOW),
    )


MODULE_ACTS = (
    (("u", 0), ("xh", 0), ("at", 0)),
    (("qkv", None), ("kt", None), ("pt", None), ("ot", None), ("xh", 1), ("at", 1)),
    (("gates", None), ("wt", None), ("xh", 2), ("xh", 5), ("at", 2)),
    (("u", 1), ("xh", 3), ("xh", 4), ("at", 3)),
)


def work_shapes(n):
    return dict(
        w=pltpu.VMEM((4, 2, 2, 32, COLS), LOW),
        stream=pltpu.VMEM((n, 512), F32),
        grad=pltpu.VMEM((n, 512), F32),
        rate=pltpu.VMEM((2, n, 128), F32),
        vt=pltpu.VMEM((512, n), LOW),
        qt=pltpu.VMEM((512, n), F32),
        ctx=pltpu.VMEM((n, 512), LOW),
        pad=pltpu.VMEM((2, n + 16, 512), F32),
        sm=pltpu.VMEM((2, 32, 512), F32),
        smg=pltpu.VMEM((2, 32, 512), F32),
        bias=pltpu.VMEM((n, n), F32),
        live=pltpu.VMEM((n, 1), F32),
        given=pltpu.VMEM((2, n, 512), LOW),
        result=pltpu.VMEM((2, n, 512), LOW),
        result_grad=pltpu.VMEM((2, n, 512), LOW),
    )
MESH = pl.DeviceIdType.MESH

FORWARD_PIECES = (
    [(SM, 128)]
    + [(base + j, STEP) for j in range(0, 2048, STEP) for base in (EU, ED)]
    + [(PJ, STEP), (PJ + 512, STEP), (PJ + 1024, STEP), (AO, STEP), (CI, STEP), (CI + 512, STEP), (CO, STEP)]
    + [(base + j, STEP) for j in range(0, 2048, STEP) for base in (LU, LD)]
)


class Place:
    def __init__(self):
        p, d = lax.axis_index("pipe"), lax.axis_index("dp")
        self.p, self.z, self.y, self.c = p, d // 4, d // 2 % 2, d % 2
        z, y, c = self.z, self.y, self.c
        self.across = (1 - p, d)
        self.beside = (p, z * 4 + (1 - y) * 2 + c)
        self.twin = (p, z * 4 + y * 2 + 1 - c)
        self.column = [(p, (z + j) % 4 * 4 + y * 2 + c) for j in (1, 2, 3)]

    def greet(self):
        for partner in [self.across, self.beside, self.twin] + self.column:
            pl.semaphore_signal(
                pltpu.get_barrier_semaphore(), inc=1, device_id=partner, device_id_type=MESH
            )

    def meet(self):
        pl.semaphore_wait(pltpu.get_barrier_semaphore(), 6)


def remote(source, target, send, arrive, device):
    return pltpu.make_async_remote_copy(
        src_ref=source, dst_ref=target, send_sem=send, recv_sem=arrive, device_id=device, device_id_type=MESH
    )


class Gather:
    def __init__(self, place, ways, shard, w, sems):
        self.place, self.ways, self.shard, self.w = place, ways, shard, w
        self.zr, self.yr, self.xr, self.dr, self.sent, self.own = sems

    def cols(self, k):
        return pl.ds(*FORWARD_PIECES[k])

    def block(self, l, k, z, y):
        return self.w.at[l, z, y, self.place.c, :, self.cols(k)]

    def mine(self, l, k):
        return self.block(l, k, self.place.z, self.place.y)

    def z_copy(self, l, k, j, source=None):
        target = self.mine(l, k)
        source = target if source is None else source
        return remote(source, target, self.sent.at[l, 0], self.zr.at[l, k], self.place.column[j])

    def z_wait(self, l, k):
        three = self.w.at[l, pl.ds(0, 3), self.place.y, self.place.c, :, self.cols(k)]
        remote(three, three, self.sent.at[l, 0], self.zr.at[l, k], self.place.twin).wait_recv()

    def y_copy(self, l, k, y):
        part = self.w.at[l, :, y, self.place.c, :, self.cols(k)]
        return remote(part, part, self.sent.at[l, 1], self.yr.at[l, k], self.place.beside)

    def x_one(self, l, k, source=None):
        target = self.mine(l, k)
        source = target if source is None else source
        return remote(source, target, self.sent.at[l, 2], self.xr.at[l, k], self.place.across)

    def x_all(self, l, k):
        part = self.w.at[l, :, :, self.place.c, :, self.cols(k)]
        return remote(part, part, self.sent.at[l, 3], self.xr.at[l, k], self.place.across)

    def d_copy(self, l, k, c):
        part = self.w.at[l, :, :, c, :, self.cols(k)]
        return remote(part, part, self.sent.at[l, 4], self.dr.at[l, k], self.place.twin)

    def own_copy(self):
        place = self.place
        return pltpu.make_async_copy(
            self.shard, self.w.at[place.p, place.z, place.y, place.c], self.own.at[0]
        )

    def step(self, i, l, k, owner):
        way, piece = self.ways[l][k], self.shard.at[:, self.cols(k)]

        def start():
            if way in "FG":
                self.x_one(l, k, piece).start()
            if way in "FA":
                for j in range(3):
                    self.z_copy(l, k, j, piece).start()

        def spread():
            self.x_one(l, k).wait_recv()
            for j in range(3):
                self.z_copy(l, k, j).start()

        def beside():
            self.z_wait(l, k)
            self.y_copy(l, k, self.place.y).start()

        def across():
            self.y_copy(l, k, 1 - self.place.y).wait_recv()
            if way == ("A" if owner else "G"):
                self.x_all(l, k).start()
            self.d_copy(l, k, self.place.c).start()

        def twin():
            self.x_all(l, k).wait_recv()
            self.d_copy(l, k, self.place.c).start()

        plane = self.place.p == l if owner else self.place.p != l
        pl.when(plane)((start, spread, beside, across, twin)[i])

    def arrived(self, l, k):
        self.d_copy(l, k, 1 - self.place.c).wait_recv()

    def drain(self):
        def finish(l, kind, blocks, ways):
            width = sum(FORWARD_PIECES[k][1] for k, way in enumerate(self.ways[l]) if way in ways)
            if not width:
                return
            if blocks == 8:
                part = self.w.at[l, :, :, 0, :, pl.ds(0, width)]
            else:
                part = self.w.at[l, pl.ds(0, blocks), 0, 0, :, pl.ds(0, width)]
            sent, arrived = self.sent.at[l, kind], self.dr.at[l, 0]
            remote(part, part, sent, arrived, self.place.twin).wait_send()

        for l in range(2):
            finish(l, 4, 8, "FAG")

            @pl.when(self.place.p == l)
            def _():
                finish(l, 0, 3, "FA")
                finish(l, 1, 4, "FA")
                finish(l, 2, 1, "FG")
                finish(l, 3, 8, "A")

            @pl.when(self.place.p != l)
            def _():
                finish(l, 0, 3, "FG")
                finish(l, 1, 4, "FG")
                finish(l, 3, 8, "G")


def gather_sems():
    dma, count = pltpu.SemaphoreType.DMA, len(FORWARD_PIECES)
    return [dma((2, count))] * 4 + [dma((2, 5)), dma((1,))]


BACKWARD_PIECES = (
    [(base + j, STEP) for j in range(0, 2048, STEP) for base in (LD, LU)]
    + [(CO, STEP), (CI, STEP), (CI + 512, STEP), (AO, STEP), (PJ, STEP), (PJ + 512, STEP), (PJ + 1024, STEP)]
    + [(base + j, STEP) for j in range(0, 2048, STEP) for base in (ED, EU)]
    + [(SM, 128)]
)
BACK_INDEX = {column: k for k, (column, _) in enumerate(BACKWARD_PIECES)}
STAGES = 4


class Scatter:
    def __init__(self, place, ways, out, refs, sems):
        self.place, self.ways, self.out = place, ways, out
        self.wide_slot, self.late_slot = scatter_slots(ways)
        self.stage, self.part, self.wide, self.side, self.line, self.late = refs
        self.ds, self.dr, self.sent, self.xr, self.yr, self.zr, self.free = sems
        self.count = 0
        self.slot = {}

    def width(self, k):
        return BACKWARD_PIECES[k][1]

    def cols(self, k):
        return pl.ds(0, self.width(k))

    def d_copy(self, l, k):
        source = self.stage.at[self.slot[l, k], :, :, 1 - self.place.c, :, self.cols(k)]
        target = self.part.at[k, :, :, :, self.cols(k)]
        return remote(source, target, self.ds.at[self.slot[l, k]], self.dr.at[k], self.place.twin)

    def x_wide(self, l, k):
        source = self.part.at[k, :, :, :, self.cols(k)]
        target = self.wide.at[self.wide_slot[l, k], :, :, :, self.cols(k)]
        return remote(source, target, self.sent.at[k], self.xr.at[l, k], self.place.across)

    def x_late(self, l, k):
        source = self.part.at[k, self.place.z, self.place.y, :, self.cols(k)]
        target = self.late.at[self.late_slot[l, k], :, self.cols(k)]
        return remote(source, target, self.sent.at[k], self.xr.at[l, k], self.place.across)

    def y_copy(self, l, k):
        source = self.part.at[k, :, 1 - self.place.y, :, self.cols(k)]
        target = self.side.at[k, :, :, self.cols(k)]
        return remote(source, target, self.sent.at[k], self.yr.at[k], self.place.beside)

    def z_copy(self, l, k, j):
        source = self.part.at[k, (self.place.z + j + 1) % 4, self.place.y, :, self.cols(k)]
        target = self.line.at[k, j, :, self.cols(k)]
        return remote(source, target, self.sent.at[k], self.zr.at[k], self.place.column[j])

    def offer(self, l, column, value):
        k = BACK_INDEX[column]
        width = self.width(k)
        slot = self.count % STAGES
        self.count += 1
        self.slot[l, k] = slot
        self.stage[slot, :, :, :, :, :width] = value.astype(LOW).reshape(4, 2, 2, 32, width)
        if l == 0:
            self.shared(
                k,
                lambda: pl.semaphore_wait(self.free.at[k], 5),
                lambda: pl.semaphore_wait(self.free.at[k], 1),
            )
        self.d_copy(l, k).start()

    def shared(self, k, run, otherwise=lambda: None):
        both = way_planes(self.ways[1][k], 1) & way_planes(self.ways[0][k], 0)
        if len(both) == 2:
            run()
        elif both:
            plane = both.pop()
            pl.when(self.place.p == plane)(run)
            pl.when(self.place.p != plane)(otherwise)
        else:
            otherwise()

    def step(self, i, l, k, owner):
        way, cols = self.ways[l][k], self.cols(k)
        column = pl.ds(BACKWARD_PIECES[k][0], self.width(k))
        place = self.place

        def pair():
            self.d_copy(l, k).wait()
            slot, c = self.slot[l, k], place.c
            stage = self.stage

            total = self.part[k, :, :, :, cols].astype(F32)
            total = total + stage[slot, :, :, c, :, cols].astype(F32)
            self.part[k, :, :, :, cols] = total.astype(LOW)
            if way == "F":
                self.y_copy(l, k).start()
            else:
                plane = place.p == l if way == "G" else place.p != l
                pl.when(plane)(self.x_wide(l, k).start)

        def wide():
            self.x_wide(l, k).wait_recv()
            slot = self.wide_slot[l, k]

            total = self.part[k, :, :, :, cols].astype(F32)
            total = total + self.wide[slot, :, :, :, cols].astype(F32)
            self.part[k, :, :, :, cols] = total.astype(LOW)
            self.y_copy(l, k).start()

        def side():
            self.y_copy(l, k).wait_recv()
            y = place.y

            total = self.part[k, :, y, :, cols].astype(F32)
            total = total + self.side[k, :, :, cols].astype(F32)
            self.part[k, :, y, :, cols] = total.astype(LOW)
            for j in range(3):
                self.z_copy(l, k, j).start()

        def line():
            three = self.line.at[k, :, :, cols]
            remote(three, three, self.sent.at[k], self.zr.at[k], place.twin).wait_recv()
            result = self.part[k, place.z, place.y, :, cols].astype(F32)
            for j in range(3):
                result = result + self.line[k, j, :, cols].astype(F32)
            if owner:
                self.out[:, column] = result
            else:
                self.part[k, place.z, place.y, :, cols] = result.astype(LOW)
                self.x_late(l, k).start()

        def late():
            self.x_late(l, k).wait_recv()
            got = self.late[self.late_slot[l, k], :, cols].astype(F32)
            self.out[:, column] = self.out[:, column] + got if way == "F" else got

        run = (pair, wide, side, line, late)[i - 1]
        if owner is None:
            run()
        else:
            pl.when(place.p == l if owner else place.p != l)(run)

    def release(self, l, k):
        way, place = self.ways[l][k], self.place

        def sent(blocks):
            part = self.late.at[pl.ds(0, blocks), :, self.cols(k)]
            remote(part, part, self.sent.at[k], self.zr.at[k], place.twin).wait_send()

        pl.when(place.p == l)(lambda: sent(8 if way == "G" else 7))
        pl.when(place.p != l)(lambda: sent(8))
        if l == 0:
            return
        pl.semaphore_signal(self.free.at[k], inc=1, device_id=place.twin, device_id_type=MESH)

        def give():
            for device in [place.beside] + place.column:
                pl.semaphore_signal(self.free.at[k], inc=1, device_id=device, device_id_type=MESH)

        self.shared(k, give)


def way_planes(way, l):
    return {"F": {0, 1}, "A": {l}, "G": {1 - l}}[way]


def scatter_slots(ways):
    wide, late, used = {}, {}, [0, 0]
    for l in (1, 0):
        for k, way in enumerate(ways[l]):
            if way in "AG":
                plane = l if way == "A" else 1 - l
                wide[l, k] = used[plane]
                used[plane] += 1
            if way in "FG":
                late[l, k] = sum(1 for item in late if item[0] == l)
    return wide, late


def scatter_refs(ways):
    count = len(BACKWARD_PIECES)
    wide, late = scatter_slots(ways)
    return [
        pltpu.VMEM((STAGES, 4, 2, 2, 32, STEP), LOW),
        pltpu.VMEM((count, 4, 2, 32, STEP), LOW),
        pltpu.VMEM((max(wide.values()) + 1, 4, 2, 32, STEP), LOW),
        pltpu.VMEM((count, 4, 32, STEP), LOW),
        pltpu.VMEM((count, 3, 32, STEP), LOW),
        pltpu.VMEM((max(late.values()) + 1, 32, STEP), LOW),
    ]


def scatter_sems():
    dma, count = pltpu.SemaphoreType.DMA, len(BACKWARD_PIECES)
    each = [dma((count,))]
    return (
        [dma((STAGES,))]
        + each * 2
        + [dma((2, count))]
        + each * 2
        + [pltpu.SemaphoreType.REGULAR((count,))]
    )


GATHER_WAYS = ("AGAGGAGAFFFAAFGGAFAFAAGF", "AAGGFFGAAFGFFFGAAFAFFGFF")
SCATTER_WAYS = ("AFAFGFAGAFGAFGAFAGFAGFGA", "AFFAFFGFGAAFGFFAGAFGFAGF")
FORWARD_ORDER = (
    1, 4, 7, 10, 13, 149, 16, 19, 155, 22, 158, 25, 28, 289, 164, 31, 34, 293, 295, 37, 170, 40, 173, 299, 43,
    176, 302, 433, 304, 46, 437, 49, 308, 439, 310, 52, 185, 443, 188, 55, 313, 446, 191, 58, 448, 316, 61, 319,
    322, 314, 452, 64, 197, 454, 325, 317, 67, 320, 70, 203, 328, 578, 332, 73, 580, 335, 466, 337, 76, 329, 212,
    723, 584, 726, 469, 79, 586, 215, 340, 343, 82, 589, 729, 457, 732, 458, 85, 476, 460, 593, 0, 735, 346, 349,
    461, 88, 341, 479, 595, 463, 481, 224, 352, 464, 91, 738, 747, 599, 0, 741, 227, 94, 347, 750, 356, 487, 0,
    97, 230, 744, 472, 753, 358, 473, 100, 233, 361, 493, 236, 0, 103, 364, 611, 496, 106, 359, 762, 614, 0, 109,
    500, 368, 756, 484, 485, 112, 245, 619, 371, 759, 248, 115, 622, 505, 490, 373, 765, 491, 118, 251, 508, 376,
    774, 626, 0, 768, 121, 254, 0, 380, 0, 382, 374, 512, 0, 0, 124, 257, 0, 771, 0, 385, 780, 632, 377, 0, 515,
    0, 260, 127, 0, 502, 0, 0, 503, 130, 777, 388, 638, 0, 133, 392, 641, 0, 524, 136, 269, 643, 526, 783, 394,
    792, 389, 139, 529, 786, 397, 0, 789, 142, 275, 400, 395, 517, 278, 650, 404, 406, 518, 398, 536, 281, 520,
    653, 409, 521, 401, 0, 655, 795, 0, 284, 0, 658, 798, 287, 807, 801, 412, 415, 810, 804, 548, 532, 0, 550,
    418, 533, 413, 667, 553, 421, 0, 538, 671, 813, 425, 539, 0, 419, 541, 822, 674, 559, 427, 542, 422, 816, 544,
    430, 545, 679, 819, 828, 0, 428, 831, 825, 431, 569, 834, 556, 0, 557, 691, 0, 562, 695, 0, 837, 0, 563, 0, 0,
    565, 846, 698, 0, 0, 566, 0, 0, 840, 0, 843, 571, 852, 704, 572, 0, 574, 0, 855, 575, 849, 0, 712, 861, 0,
    864, 858, 0, 0, 0, 0,
)
BACKWARD_ORDER = (
    0, 0, 219, 222, 0, 225, 228, 0, 231, 0, 234, 0, 237, 0, 0, 508, 509, 361, 240, 511, 512, 0, 243, 0, 246, 0,
    517, 518, 0, 370, 0, 249, 0, 520, 0, 521, 380, 0, 0, 0, 252, 505, 255, 0, 526, 527, 386, 653, 258, 656, 261,
    0, 514, 264, 524, 388, 662, 267, 0, 538, 649, 939, 539, 391, 398, 665, 270, 530, 273, 0, 544, 545, 671, 276,
    547, 658, 948, 548, 0, 279, 532, 410, 282, 652, 796, 942, 0, 668, 542, 535, 406, 285, 683, 655, 799, 945, 288,
    0, 674, 559, 560, 412, 419, 147, 689, 661, 805, 951, 150, 664, 808, 954, 0, 554, 565, 676, 966, 566, 692, 153,
    679, 969, 550, 428, 811, 957, 156, 670, 814, 960, 0, 686, 424, 159, 563, 574, 556, 575, 817, 963, 0, 162, 704,
    0, 165, 0, 0, 436, 437, 289, 168, 698, 572, 694, 984, 710, 682, 826, 972, 0, 171, 442, 568, 443, 295, 302, 0,
    174, 0, 700, 990, 0, 0, 177, 0, 707, 448, 0, 449, 0, 719, 0, 829, 975, 688, 832, 978, 691, 835, 981, 0, 180,
    433, 311, 183, 841, 987, 0, 307, 581, 186, 716, 446, 712, 1002, 439, 189, 703, 847, 993, 0, 460, 461, 313,
    320, 587, 192, 850, 996, 195, 709, 853, 999, 0, 455, 577, 867, 593, 198, 469, 451, 470, 322, 329, 201, 859,
    1005, 0, 583, 873, 204, 590, 464, 457, 718, 862, 1008, 0, 207, 478, 479, 331, 605, 210, 341, 213, 599, 473,
    595, 885, 466, 337, 216, 487, 488, 614, 580, 601, 891, 350, 608, 475, 346, 485, 586, 496, 497, 356, 623, 610,
    900, 481, 617, 592, 494, 358, 632, 619, 909, 490, 500, 629, 604, 625, 915, 641, 502, 638, 613, 634, 924, 644,
    622, 646, 936, 631, 640, 724, 870, 730, 876, 736, 882, 748, 894, 757, 903, 766, 912, 775, 921, 784, 930, 733,
    879, 742, 888, 751, 897, 760, 906, 772, 918, 781, 927, 787, 933,
)


FORWARD_CHUNKS, BACKWARD_CHUNKS, SHARES = 23, 23, 8
MATRICES = ((EU, 2048), (ED, 2048), (PJ, 1536), (AO, 512), (CI, 1024), (CO, 512), (LU, 2048), (LD, 2048))


def swap_halves(columns, back=False):
    parts = []
    for g in range(0, 1024, 256):
        for i in range(8):
            a, b = divmod(i, 2 if back else 4)
            start = g + (b * 128 + a * 32 if back else b * 64 + a * 32)
            parts.append(columns[:, start : start + 32])
    return jnp.concatenate(parts, axis=1)


def fused_kernel(groups, length, flag, span, frames, cotangent, *rest):
    n_acts, act_names, work_names, n = groups
    matrices, small, rest = rest[:8], rest[8:15], rest[15:]
    cos, sin, y_out, dx_out, g_out, w, *rest = rest
    kept, rest = dict(zip(act_names, rest[:n_acts])), rest[n_acts:]
    acts, rest = dict(zip(act_names, rest[:n_acts])), rest[n_acts:]
    work, rest = dict(zip(work_names, rest[: len(work_names)])), rest[len(work_names) :]
    back_refs, rest = rest[:6], rest[6:]
    gather_sem, rest = rest[:6], rest[6:]
    scatter_sem, rest = rest[:7], rest[7:]
    load_sem, keep_sem, given_sem, share_send, share_arrive, shard_sem, shard, proj, rows = rest

    place = Place()
    place.greet()
    p = place.p
    given = [
        pltpu.make_async_copy(source.at[p], work["given"].at[i], given_sem.at[i])
        for i, source in enumerate((frames, cotangent))
    ]
    for copy in given:
        copy.start()
    pieces = []
    for i, (column, width) in enumerate(MATRICES):
        target = proj if column == PJ else shard.at[:, pl.ds(column, width)]
        pieces.append(pltpu.make_async_copy(matrices[i], target, shard_sem.at[i]))
        pieces[-1].start()
    rows[...] = jnp.zeros_like(rows)
    for i, gain in enumerate(small[:6]):
        rows[i : i + 1, :32] = gain[...].astype(F32)
    rows[TAPS : TAPS + KERNEL, :32] = small[6][...].astype(F32)
    shard[:, SM:] = rows[...].astype(LOW)
    for copy in pieces:
        copy.wait()
    shard[:, PJ : PJ + 1024] = swap_halves(proj[:, :1024].astype(F32)).astype(LOW)
    shard[:, PJ + 1024 : AO] = proj[:, 1024:]
    gather = Gather(place, GATHER_WAYS, shard, w, gather_sem)
    gather.own_copy().start()
    place.meet()
    gather.own_copy().wait()

    count = len(FORWARD_PIECES)
    number = {column: k for k, (column, _) in enumerate(FORWARD_PIECES)}
    waiting = []

    def load(l, k):
        cols = gather.cols(k)
        return pltpu.make_async_copy(
            w.at[l, :, :, :, :, cols], work["w"].at[:, :, :, :, cols], load_sem.at[k]
        )

    def need(l, *columns):
        for column in columns:
            load(l, number[column]).wait()

    def keep(module, back):
        copies = []
        for i, (name, index) in enumerate(MODULE_ACTS[module]):
            near, far = acts[name], kept[name]
            if index is not None:
                near, far = near.at[index], far.at[index]
            source, target = (far, near) if back else (near, far)
            copies.append(pltpu.make_async_copy(source, target, keep_sem.at[module, i]))
        return copies

    scatter = Scatter(place, SCATTER_WAYS, g_out, back_refs, scatter_sem)
    run = Layer({**acts, **work, "cos": cos, "sin": sin}, scatter.offer, need)

    def share(i, l, rows):
        results, out = ((run.result, y_out), (run.result_grad, dx_out))[i]
        source, send, arrive = results.at[l, rows], share_send.at[i, l], share_arrive.at[i]
        own = pltpu.make_async_copy(source, out.at[p, rows], send)
        away = remote(source, out.at[p, rows], send, arrive, place.across)
        expected = remote(source, out.at[1 - p, rows], send, arrive, place.across)
        return own, away, expected

    def share_start(i, l, q):
        own, away, _ = share(i, l, pl.ds(q * (n // SHARES), n // SHARES))
        pl.when(p == l)(own.start)
        pl.when(p != l)(away.start)

    def share_finish(i, l):
        own, away, expected = share(i, l, pl.ds(0, n))
        pl.when(p == l)(own.wait)

        @pl.when(p != l)
        def _():
            away.wait_send()
            expected.wait_recv()

    def forward():
        modules = (
            lambda l: run.feed_forward(l, 0, G_EARLY, 0, EU, ED),
            run.attend_forward,
            run.convolve_forward,
            lambda l: run.feed_forward(l, 3, G_LATE, 3, LU, LD),
        )
        for l in range(2):
            run.small_forward(l)
            yield
            for m, module in enumerate(modules):
                if l == 1:
                    for copy in keep(m, False):
                        copy.wait()
                yield from module(l)
                if l == 0:
                    for copy in keep(m, False):
                        if m < 3:
                            copy.start()
                yield
            run.result[l] = run.finish_forward(l)
            if l == 0:
                for copy in keep(3, False):
                    copy.start()
                run.stream[...] = run.result[0].astype(F32)
                for item in waiting:
                    load(*item).start()
                waiting.clear()
                run.first_done = True
            yield

    def reload(m):
        columns = ((EU, 4096), (PJ, 2048), (CI, 1536), (LU, 4096))
        cols = pl.ds(*columns[m])
        return pltpu.make_async_copy(
            w.at[0, :, :, :, :, cols], work["w"].at[:, :, :, :, cols], load_sem.at[m]
        )

    def backward():
        modules = (
            lambda l: run.feed_backward(l, 0, G_EARLY, 0, EU, ED),
            run.attend_backward,
            run.convolve_backward,
            lambda l: run.feed_backward(l, 3, G_LATE, 3, LU, LD),
        )
        for l in (1, 0):
            if l == 0:
                for copy in keep(3, True):
                    copy.wait()
            start = run.given[1].astype(F32) if l == 1 else run.result_grad[1].astype(F32)
            run.grad[...] = run.leave(l, 4, G_FINAL, start)
            for m in (3, 2, 1, 0):
                if l == 0:
                    if m < 3:
                        for copy in keep(m, True):
                            copy.wait()
                    reload(m).wait()
                yield from modules[m](l)
                if l == 1:
                    for copy in keep(m, True):
                        copy.start()
                    reload(m).start()
                yield
            run.small_backward(l)
            run.result_grad[l] = run.grad[...].astype(LOW)
            yield

    def item(code):
        if code == 0:
            return None, None, None, None
        code, owner = divmod(code - 1, 3)
        code, k = divmod(code, count)
        return code // 2, code % 2, k, (True, False, None)[owner]

    run.first_done = False
    chunks, chunk, prepared = forward(), 0, False
    for code in FORWARD_ORDER:
        i, l, k, owner = item(code)
        if not prepared and (code == 0 or i > 0):
            run.prepare(length[p], flag[p], span[p])
            given[0].wait()
            run.stream[...] = run.given[0].astype(F32)
            prepared = True
        if code == 0:
            next(chunks)
            if 0 <= chunk - FORWARD_CHUNKS < SHARES:
                share_start(0, 0, chunk - FORWARD_CHUNKS)
            chunk += 1
            continue
        if i < 5:
            gather.step(i, l, k, owner)
            continue
        gather.arrived(l, k)
        if l == 0 or run.first_done:
            load(l, k).start()
        else:
            waiting.append((l, k))
    given[1].wait()
    chunks, chunk = backward(), 0
    for code in BACKWARD_ORDER:
        if code == 0:
            next(chunks)
            if chunk < SHARES:
                share_start(0, 1, chunk)
            if 0 <= chunk - BACKWARD_CHUNKS < SHARES:
                share_start(1, 1, chunk - BACKWARD_CHUNKS)
            chunk += 1
            if chunk == 2 * BACKWARD_CHUNKS:
                for q in range(SHARES):
                    share_start(1, 0, q)
            continue
        i, l, k, owner = item(code)
        if i < 6:
            scatter.step(i, l, k, owner)
        else:
            scatter.release(l, k)
    gather.drain()
    for i in range(2):
        for l in range(2):
            share_finish(i, l)


def tables(n):
    rates = np.exp(np.arange(32, dtype=np.float64) * (-2.0 * math.log(10000.0) / 64))
    phases = np.arange(n, dtype=np.float64)[:, None] * np.tile(rates, 4)[None, :]
    return np.cos(phases).astype(np.float32), np.sin(phases).astype(np.float32)


def fused(lengths, flags, spans, frames, cotangent, shards):
    n = frames.shape[1]
    acts, work = act_shapes(n), work_shapes(n)
    cosine, sine = tables(n)
    eg, eu, ed, ag, pj, ao, cg, ci, cd, cn, co, lg, lu, ld, fg = shards
    matrices = [eu[0], ed[0].T, pj[0], ao[0], ci[0], co[0], lu[0], ld[0].T]
    small = [eg, ag, cg, cn, lg, fg, cd[0]]
    vmem = pl.BlockSpec(memory_space=pltpu.VMEM)
    hbm = pl.BlockSpec(memory_space=pl.ANY)
    smem = pl.BlockSpec(memory_space=pltpu.SMEM)
    dma, count = pltpu.SemaphoreType.DMA, len(FORWARD_PIECES)
    groups = (len(acts), tuple(acts), tuple(work), n)
    outs = pl.pallas_call(
        functools.partial(fused_kernel, groups),
        out_shape=[
            jax.ShapeDtypeStruct((2, n, 512), LOW),
            jax.ShapeDtypeStruct((2, n, 512), LOW),
            jax.ShapeDtypeStruct((32, COLS), F32),
            jax.ShapeDtypeStruct((2, 4, 2, 2, 32, COLS), LOW),
        ]
        + [jax.ShapeDtypeStruct(shape, kind) for shape, kind in acts.values()],
        in_specs=[smem] * 3 + [hbm] * 10 + [vmem] * 9,
        out_specs=[hbm, hbm, vmem, hbm] + [hbm] * len(acts),
        scratch_shapes=[pltpu.VMEM(shape, kind) for shape, kind in acts.values()]
        + list(work.values())
        + scatter_refs(SCATTER_WAYS)
        + gather_sems()
        + scatter_sems()
        + [dma((count,)), dma((4, 6)), dma((2,)), dma((2, 2)), dma((2,)), dma((8,))]
        + [
            pltpu.VMEM((32, COLS), LOW),
            pltpu.VMEM((32, 1536), LOW),
            pltpu.VMEM((32, 128), F32),
        ],
        compiler_params=pltpu.CompilerParams(
            collective_id=0, has_side_effects=True, vmem_limit_bytes=63 * 2**20
        ),
        cost_estimate=pl.CostEstimate(
            flops=30 * 10**9, bytes_accessed=100 * 2**20, transcendentals=10**7
        ),
    )(lengths[:, 0], flags[:, 0], spans[:, 0], frames, cotangent, *matrices, *small, jnp.asarray(cosine), jnp.asarray(sine))
    return finish(*outs[:3])


def finish_kernel(y, dx, g, y_out, dx_out, *outs):
    y_out[...] = y[...]
    dx_out[...] = dx[...]
    matrices, small = outs[:8], outs[8:]
    for out, (column, width) in zip(matrices, MATRICES):
        if column == PJ:
            out[:, :1024] = swap_halves(g[:, PJ : PJ + 1024], True)
            out[:, 1024:] = g[:, PJ + 1024 : AO]
        else:
            out[...] = g[:, column : column + width]
    for i in range(6):
        small[i][...] = g[i : i + 1, SM : SM + 32]
    small[6][...] = g[TAPS : TAPS + KERNEL, SM : SM + 32]


def finish(y, dx, g):
    widths = [(32, width) for _, width in MATRICES] + [(1, 32)] * 6 + [(KERNEL, 32)]
    vmem = pl.BlockSpec(memory_space=pltpu.VMEM)
    y, dx, eu, ed, pj, ao, ci, co, lu, ld, eg, ag, cg, cn, lg, fg, cd = pl.pallas_call(
        finish_kernel,
        out_shape=[jax.ShapeDtypeStruct(y.shape, LOW)] * 2
        + [jax.ShapeDtypeStruct(shape, F32) for shape in widths],
        in_specs=[vmem] * 3,
        out_specs=[vmem] * 17,
        compiler_params=pltpu.CompilerParams(vmem_limit_bytes=32 * 2**20),
    )(y, dx, g)
    return (
        y[None, :, None],
        dx[None, :, None],
        eg,
        eu[None],
        ed.T[None],
        ag,
        pj[None],
        ao[None],
        cg,
        ci[None],
        cd[None],
        cn,
        co[None],
        lg,
        lu[None],
        ld.T[None],
        fg,
    )


def plain_kernel(groups, scalars, w, frames, cotangent, cos, sin, y_out, dx_out, g_out, *rest):
    n_acts, act_names, work_names, n = groups
    kept, rest = dict(zip(act_names, rest[:n_acts])), rest[n_acts:]
    acts, rest = dict(zip(act_names, rest[:n_acts])), rest[n_acts:]
    work, rest = dict(zip(work_names, rest[: len(work_names)])), rest[len(work_names) :]
    stage, sem = rest

    def move(source, target):
        copy = pltpu.make_async_copy(source, target, sem)
        copy.start()
        copy.wait()

    def emit(l, column, value):
        width = value.shape[1]
        stage[:, :width] = value.astype(LOW)
        move(stage.at[:, pl.ds(0, width)], g_out.at[l, :, pl.ds(column, width)])

    run = Layer({**acts, **work, "cos": cos, "sin": sin}, emit, lambda *_: None)

    def whole(*modules):
        for module in modules:
            for _ in module:
                pass

    move(frames, run.given.at[0])
    move(cotangent, run.given.at[1])
    run.prepare(scalars[0], scalars[1], scalars[2])
    run.stream[...] = run.given[0].astype(F32)
    for l in range(2):
        move(w.at[l], work["w"])
        run.small_forward(l)
        whole(
            run.feed_forward(l, 0, G_EARLY, 0, EU, ED),
            run.attend_forward(l),
            run.convolve_forward(l),
            run.feed_forward(l, 3, G_LATE, 3, LU, LD),
        )
        run.result[l] = run.finish_forward(l)
        run.stream[...] = run.result[l].astype(F32)
        if l == 0:
            for name in act_names:
                move(acts[name], kept[name])
    for l in (1, 0):
        if l == 0:
            move(w.at[0], work["w"])
            for name in act_names:
                move(kept[name], acts[name])
        start = run.given[1].astype(F32) if l == 1 else run.result_grad[1].astype(F32)
        run.grad[...] = run.leave(l, 4, G_FINAL, start)
        whole(
            run.feed_backward(l, 3, G_LATE, 3, LU, LD),
            run.convolve_backward(l),
            run.attend_backward(l),
            run.feed_backward(l, 0, G_EARLY, 0, EU, ED),
        )
        run.small_backward(l)
        run.result_grad[l] = run.grad[...].astype(LOW)
    move(run.result, y_out)
    move(run.result_grad, dx_out)


def plain(scalars, weights, frames, cotangent):
    n = frames.shape[0]
    acts, work = act_shapes(n), work_shapes(n)
    cosine, sine = tables(n)
    vmem = pl.BlockSpec(memory_space=pltpu.VMEM)
    hbm = pl.BlockSpec(memory_space=pl.ANY)
    outs = pl.pallas_call(
        functools.partial(plain_kernel, (len(acts), tuple(acts), tuple(work), n)),
        out_shape=[
            jax.ShapeDtypeStruct((2, n, 512), LOW),
            jax.ShapeDtypeStruct((2, n, 512), LOW),
            jax.ShapeDtypeStruct((2, 512, COLS), LOW),
        ]
        + [jax.ShapeDtypeStruct(shape, kind) for shape, kind in acts.values()],
        in_specs=[pl.BlockSpec(memory_space=pltpu.SMEM), hbm, hbm, hbm, vmem, vmem],
        out_specs=[hbm] * (3 + len(acts)),
        scratch_shapes=[pltpu.VMEM(shape, kind) for shape, kind in acts.values()]
        + list(work.values())
        + [pltpu.VMEM((512, STEP), LOW), pltpu.SemaphoreType.DMA],
        compiler_params=pltpu.CompilerParams(vmem_limit_bytes=60 * 2**20),
    )(scalars, weights, frames, cotangent, jnp.asarray(cosine), jnp.asarray(sine))
    return outs[:3]


def pack(shards):
    eg, eu, ed, ag, pj, ao, cg, ci, cd, cn, co, lg, lu, ld, fg = (piece[0] for piece in shards)
    rows = eu.shape[0]
    small = jnp.concatenate(
        [gain[:, None] for gain in (eg, ag, cg, cn, lg, fg)]
        + [cd.T, jnp.zeros((rows, 128 - 6 - KERNEL), LOW)],
        axis=1,
    )
    proj = jnp.concatenate([swap_halves(pj[:, :1024]), pj[:, 1024:]], axis=1)
    return jnp.concatenate([eu, ed.T, proj, ao, ci, co, lu, ld.T, small], axis=1)


def unpack(block):
    proj = block[:, PJ : PJ + 1536]
    proj = jnp.concatenate([swap_halves(proj[:, :1024], True), proj[:, 1024:]], axis=1)
    gains = [block[:, SM + i] for i in range(6)]
    eg, ag, cg, cn, lg, fg = gains
    outs = (
        eg,
        block[:, EU:ED],
        block[:, ED:PJ].T,
        ag,
        proj,
        block[:, AO:CI],
        cg,
        block[:, CI:CO],
        block[:, SM + TAPS : SM + TAPS + KERNEL].T,
        cn,
        block[:, CO:LU],
        lg,
        block[:, LU:LD],
        block[:, LD:SM].T,
        fg,
    )
    return tuple(piece[None] for piece in outs)


def turn_small(block):
    small = block[..., SM : SM + 32].reshape(2, len(OWNERS), 32, 32).swapaxes(2, 3)
    small = jnp.pad(small.reshape(2, 512, 32), ((0, 0), (0, 0), (0, 96)))
    return jnp.concatenate([block[..., :SM], small], axis=2)


def by_collectives(lengths, flags, spans, frames, cotangent, shards):
    section = lax.axis_index("pipe")

    def mine(block):
        return lax.dynamic_index_in_dim(block, section, 0, keepdims=False)

    full = lax.all_gather(pack(shards), ("pipe", "dp"), axis=0, tiled=True)
    full = turn_small(full.reshape(2, 512, COLS)).reshape(2, 4, 2, 2, 32, COLS)
    scalars = jnp.stack([mine(lengths)[0], mine(flags)[0], mine(spans)[0]])
    ys, dxs, grads = plain(scalars, full, mine(frames), mine(cotangent))
    summed = lax.psum_scatter(
        turn_small(grads).reshape(1024, COLS), ("pipe", "dp"), scatter_dimension=0, tiled=True
    ).astype(F32)

    def share(pair):
        own, other = mine(pair), jnp.where(section == 0, pair[1], pair[0])
        got = lax.ppermute(other, "pipe", [(0, 1), (1, 0)])
        pair = jnp.where(section == 0, jnp.stack([own, got]), jnp.stack([got, own]))
        return pair[None, :, None]

    return (share(ys), share(dxs)) + unpack(summed)


def body(frames, cotangent, lengths, stream_flags, span_sizes, *shards):
    run = fused if lax.axis_size("dp") == 16 else by_collectives
    return run(lengths, stream_flags, span_sizes, frames[:, 0], cotangent[:, 0], shards)


def solution(mesh):
    gain, matrix, column = P("pipe", "dp"), P("pipe", "dp", None), P("pipe", None, "dp")
    weights = (gain, matrix, column, gain, matrix, matrix, gain, matrix, column, gain, matrix)
    weights = weights + (gain, matrix, column, gain)
    frames, stacked = P(None, "dp", None, None), P("pipe", None, "dp", None, None)
    return jax.shard_map(
        body,
        mesh=mesh,
        in_specs=(frames, frames) + (P(None, "dp"),) * 3 + weights,
        out_specs=(stacked, stacked) + weights,
        check_vma=False,
    )
```

```python
import functools
import math

import jax
import jax.numpy as jnp
import numpy as np
from jax import lax
from jax.experimental import pallas as pl
from jax.experimental.pallas import tpu as pltpu
from jax.sharding import PartitionSpec as P

HEADS = 8
KERNEL = 15
EPSILON = 1e-05
LOW = jnp.bfloat16
F32 = jnp.float32

EU, ED, PJ, AO, CI, CO, LU, LD, SM = 0, 2048, 4096, 5632, 6144, 7168, 7680, 9728, 11776
COLS = 11904
STEP = 512
OWNERS = [(z, y, c) for z in range(4) for y in range(2) for c in range(2)]
G_EARLY, G_ATTEND, G_CONV, G_MIX, G_LATE, G_FINAL, TAPS = 0, 1, 2, 3, 4, 5, 6


def dot(left, right):
    return lax.dot_general(left, right, (((1,), (0,)), ((), ())), preferred_element_type=F32)


def dot_t(left, right):
    return lax.dot_general(left, right, (((1,), (1,)), ((), ())), preferred_element_type=F32)


def sigmoid(values):
    return 0.5 * jnp.tanh(0.5 * values) + 0.5


def norm_hat(values):
    center = values - jnp.mean(values, axis=-1, keepdims=True)
    rate = lax.rsqrt(jnp.mean(center * center, axis=-1, keepdims=True) + EPSILON)
    return center * rate, rate


def norm_grad(grad_hat, hat, rate):
    first = jnp.mean(grad_hat, axis=-1, keepdims=True)
    second = jnp.mean(grad_hat * hat, axis=-1, keepdims=True)
    return rate * (grad_hat - first - hat * second)


class Layer:
    def __init__(self, refs, emit, need):
        self.__dict__.update(refs)
        self.emit, self.need = emit, need

    def gain(self, l, row):
        return self.sm[l, row : row + 1, :]

    def weight(self, l, column, size=STEP):
        return self.w[:, :, :, :, column : column + size].reshape(512, size)

    def enter(self, l, site, row):
        values = self.stream[...]
        hat, rate = norm_hat(values)
        self.xh[site] = hat.astype(LOW)
        self.rate[l, :, site : site + 1] = rate
        return (hat * self.gain(l, row)).astype(LOW)

    def leave(self, l, site, row, grad):
        hat = self.xh[site].astype(F32)
        rate = self.rate[l, :, site : site + 1]
        self.smg[l, row : row + 1, :] = jnp.sum(grad * hat, axis=0, keepdims=True)
        return norm_grad(grad * self.gain(l, row), hat, rate)

    def small_forward(self, l):
        self.need(l, SM)
        blocks = [self.w[z, y, c, :, SM : SM + 128].astype(F32)[:, :32] for z, y, c in OWNERS]
        self.sm[l] = jnp.concatenate(blocks, axis=1)

    def small_backward(self, l):
        blocks = [self.smg[l, :, 32 * o : 32 * o + 32] for o in range(len(OWNERS))]
        block = jnp.concatenate(blocks, axis=0)
        self.emit(l, SM, jnp.concatenate([block, jnp.zeros((512, 96), F32)], axis=1))

    def feed_forward(self, l, site, row, place, up, down):
        normed = self.enter(l, site, row)
        self.at[place] = normed.T
        side = 0 if site == 0 else 1
        total = None
        for j in range(0, 2048, STEP):
            self.need(l, up + j, down + j)
            inner = dot(normed, self.weight(l, up + j))
            self.u[side, :, j : j + STEP] = inner.astype(LOW)
            hidden = (inner * sigmoid(inner)).astype(LOW)
            term = dot_t(hidden, self.weight(l, down + j))
            total = term if total is None else total + term
            if j + STEP < 2048:
                yield
        self.stream[...] += 0.5 * total

    def feed_backward(self, l, site, row, place, up, down):
        branch = (0.5 * self.grad[...]).astype(LOW)
        turned = branch.T
        side = 0 if site == 0 else 1
        total = None
        for j in range(0, 2048, STEP):
            hidden_grad = dot(branch, self.weight(l, down + j))
            inner = self.u[side, :, j : j + STEP].astype(F32)
            gate = sigmoid(inner)
            hidden = inner * gate
            inner_grad = (hidden_grad * (gate + hidden * (1.0 - gate))).astype(LOW)
            self.emit(l, down + j, dot(turned, hidden.astype(LOW)))
            self.emit(l, up + j, dot(self.at[place], inner_grad))
            term = dot_t(inner_grad, self.weight(l, up + j))
            total = term if total is None else total + term
            if j + STEP < 2048:
                yield
        self.grad[...] += self.leave(l, site, row, total)

    def rotate(self, values, sign):
        cosine, sine = self.cos[...], self.sin[...]
        if sign < 0:
            sine = -sine
        parts = []
        for g in range(0, 512, 256):
            front, behind = values[:, g : g + 128], values[:, g + 128 : g + 256]
            parts += [front * cosine - behind * sine, front * sine + behind * cosine]
        return parts

    def pair_mask(self, j):
        lane = lax.broadcasted_iota(jnp.int32, (1, 256), 1)
        return (lane % 128) // 32 == j

    def head_mask(self, j):
        lane = lax.broadcasted_iota(jnp.int32, (1, 256), 1)
        return lane // 64 == j

    def attend_forward(self, l):
        normed = self.enter(l, 1, G_ATTEND)
        self.at[1] = normed.T
        self.need(l, PJ, PJ + 512, PJ + 1024)
        for which, scale in ((0, 0.125), (1, 1.0)):
            parts = self.rotate(dot(normed, self.weight(l, PJ + 512 * which)), 1)
            for i, part in enumerate(parts):
                self.qkv[which, :, 128 * i : 128 * i + 128] = part.astype(LOW) * LOW(scale)
        self.kt[...] = self.qkv[1].T
        value_rows = dot(normed, self.weight(l, PJ + 1024)).astype(LOW)
        self.qkv[2] = value_rows
        self.vt[...] = value_rows.T
        yield
        for h in range(HEADS):
            g, j = h // 4 * 256, h % 4
            keys = self.qkv[1, :, g : g + 256]
            keys = jnp.where(self.pair_mask(j), keys, jnp.zeros_like(keys))
            scores = dot_t(keys, self.qkv[0, :, g : g + 256]) + self.bias[...]
            powers = jnp.exp(scores - jnp.max(scores, axis=0, keepdims=True))
            powers = powers * (1.0 / jnp.sum(powers, axis=0, keepdims=True))
            powers = powers.astype(LOW)
            self.pt[h] = powers
            self.ot[64 * h : 64 * h + 64, :] = dot(
                self.vt[64 * h : 64 * h + 64, :], powers
            ).astype(LOW)
            yield
        self.need(l, AO)
        self.stream[...] += dot(self.ot[...].T, self.weight(l, AO))

    def attend_backward(self, l):
        branch = self.grad[...].astype(LOW)
        self.emit(l, AO, dot(self.ot[...], branch))
        self.ctx[...] = dot_t(branch, self.weight(l, AO)).astype(LOW)
        yield
        key_total, value_total = [], []
        for g in range(0, 512, 256):
            ctx = self.ctx[:, g : g + 256]
            queries = self.qkv[0, :, g : g + 256]
            values = self.qkv[2, :, g : g + 256]
            key_grad = value_grad = None
            for j in range(4):
                h = g // 64 + j
                head = self.head_mask(j)
                soft_grad = dot_t(jnp.where(head, values, jnp.zeros_like(values)), ctx)
                soft_low = self.pt[h]
                soft = soft_low.astype(F32)
                delta = jnp.sum(soft_grad * soft, axis=0, keepdims=True)
                score_grad = (soft * (soft_grad - delta)).astype(LOW)
                term = dot(soft_low, jnp.where(head, ctx, jnp.zeros_like(ctx)))
                value_grad = term if value_grad is None else value_grad + term
                term = dot(
                    score_grad, jnp.where(self.pair_mask(j), queries, jnp.zeros_like(queries))
                )
                key_grad = term if key_grad is None else key_grad + term
                front, behind = g + 32 * j, g + 128 + 32 * j
                rows = jnp.concatenate(
                    [self.kt[front : front + 32, :], self.kt[behind : behind + 32, :]], axis=0
                )
                turned = dot(rows, score_grad)
                self.qt[front : front + 32, :] = turned[:32]
                self.qt[behind : behind + 32, :] = turned[32:]
                yield
            key_total.append(key_grad)
            value_total.append(value_grad)
        query_grad = self.qt[...].T * 0.125
        query_grad = jnp.concatenate(self.rotate(query_grad, -1), axis=1).astype(LOW)
        key_grad = jnp.concatenate(key_total, axis=1)
        key_grad = jnp.concatenate(self.rotate(key_grad, -1), axis=1).astype(LOW)
        value_grad = jnp.concatenate(value_total, axis=1).astype(LOW)
        total = None
        for i, part in enumerate((query_grad, key_grad, value_grad)):
            self.emit(l, PJ + 512 * i, dot(self.at[1], part))
            term = dot_t(part, self.weight(l, PJ + 512 * i))
            total = term if total is None else total + term
        self.grad[...] += self.leave(l, 1, G_ATTEND, total)

    def tap(self, l, k):
        row = self.sm[l, TAPS + k : TAPS + k + 1, :]
        return row if k <= KERNEL // 2 else row * self.whole

    def convolve_forward(self, l):
        normed = self.enter(l, 2, G_CONV)
        self.at[2] = normed.T
        self.need(l, CI, CI + 512)
        first = dot(normed, self.weight(l, CI))
        second = dot(normed, self.weight(l, CI + 512))
        self.gates[:, :512] = first.astype(LOW)
        self.gates[:, 512:] = second.astype(LOW)
        n = first.shape[0]
        self.pad[0, 8 : n + 8, :] = first * sigmoid(second) * self.live[...]
        yield
        mixed = None
        for k in range(KERNEL):
            term = self.tap(l, k) * self.pad[0, k + 1 : k + 1 + n, :]
            mixed = term if mixed is None else mixed + term
        hat, rate = norm_hat(mixed)
        self.xh[5] = hat.astype(LOW)
        self.rate[l, :, 5:6] = rate
        inner = hat * self.gain(l, G_MIX)
        hidden = (inner * sigmoid(inner)).astype(LOW)
        self.wt[...] = hidden.T
        yield
        self.need(l, CO)
        self.stream[...] += dot(hidden, self.weight(l, CO))

    def convolve_backward(self, l):
        branch = self.grad[...].astype(LOW)
        n = branch.shape[0]
        self.emit(l, CO, dot(self.wt[...], branch))
        hidden_grad = dot_t(branch, self.weight(l, CO))
        yield
        hat = self.xh[5].astype(F32)
        inner = hat * self.gain(l, G_MIX)
        gate = sigmoid(inner)
        inner_grad = hidden_grad * (gate + inner * gate * (1.0 - gate))
        self.pad[1, 8 : n + 8, :] = self.leave(l, 5, G_MIX, inner_grad)
        first = self.gates[:, :512].astype(F32)
        gate = sigmoid(self.gates[:, 512:].astype(F32))
        self.pad[0, 8 : n + 8, :] = first * gate * self.live[...]
        yield
        mixed_grad = self.pad[1, 8 : n + 8, :]
        total = None
        for k in range(KERNEL):
            row = jnp.sum(mixed_grad * self.pad[0, k + 1 : k + 1 + n, :], axis=0, keepdims=True)
            if k > KERNEL // 2:
                row = row * self.whole
            self.smg[l, TAPS + k : TAPS + k + 1, :] = row
            term = self.tap(l, k) * self.pad[1, 15 - k : 15 - k + n, :]
            total = term if total is None else total + term
        total = total * self.live[...]
        first_grad = (total * gate).astype(LOW)
        second_grad = (total * first * gate * (1.0 - gate)).astype(LOW)
        yield
        self.emit(l, CI, dot(self.at[2], first_grad))
        self.emit(l, CI + 512, dot(self.at[2], second_grad))
        total = dot_t(first_grad, self.weight(l, CI))
        total = total + dot_t(second_grad, self.weight(l, CI + 512))
        self.grad[...] += self.leave(l, 2, G_CONV, total)

    def prepare(self, length, flag, span):
        n = self.stream.shape[0]
        key = lax.broadcasted_iota(jnp.int32, (n, n), 0)
        query = lax.broadcasted_iota(jnp.int32, (n, n), 1)
        width = span.astype(F32)
        key_block = jnp.floor((key.astype(F32) + 0.5) / width)
        query_block = jnp.floor((query.astype(F32) + 0.5) / width)
        shown = (key < length) & ((flag == 0) | (key_block <= query_block))
        self.bias[...] = jnp.where(shown, 0.0, -1e30)
        place = lax.broadcasted_iota(jnp.int32, (n, 1), 0)
        self.live[...] = (place < length).astype(F32)
        self.whole = jnp.where(flag == 0, 1.0, 0.0)
        self.pad[...] = jnp.zeros_like(self.pad)
        self.smg[...] = jnp.zeros_like(self.smg)

    def finish_forward(self, l):
        hat, rate = norm_hat(self.stream[...])
        self.xh[4] = hat.astype(LOW)
        self.rate[l, :, 4:5] = rate
        return (hat * self.gain(l, G_FINAL)).astype(LOW)


def act_shapes(n):
    return dict(
        xh=((6, n, 512), LOW),
        at=((4, 512, n), LOW),
        u=((2, n, 2048), LOW),
        qkv=((3, n, 512), LOW),
        kt=((512, n), LOW),
        pt=((HEADS, n, n), LOW),
        ot=((512, n), LOW),
        gates=((n, 1024), LOW),
        wt=((512, n), LOW),
    )


MODULE_ACTS = (
    (("u", 0), ("xh", 0), ("at", 0)),
    (("qkv", None), ("kt", None), ("pt", None), ("ot", None), ("xh", 1), ("at", 1)),
    (("gates", None), ("wt", None), ("xh", 2), ("xh", 5), ("at", 2)),
    (("u", 1), ("xh", 3), ("xh", 4), ("at", 3)),
)


def work_shapes(n):
    return dict(
        w=pltpu.VMEM((4, 2, 2, 32, COLS), LOW),
        stream=pltpu.VMEM((n, 512), F32),
        grad=pltpu.VMEM((n, 512), F32),
        rate=pltpu.VMEM((2, n, 128), F32),
        vt=pltpu.VMEM((512, n), LOW),
        qt=pltpu.VMEM((512, n), F32),
        ctx=pltpu.VMEM((n, 512), LOW),
        pad=pltpu.VMEM((2, n + 16, 512), F32),
        sm=pltpu.VMEM((2, 32, 512), F32),
        smg=pltpu.VMEM((2, 32, 512), F32),
        bias=pltpu.VMEM((n, n), F32),
        live=pltpu.VMEM((n, 1), F32),
        given=pltpu.VMEM((2, n, 512), LOW),
        result=pltpu.VMEM((2, n, 512), LOW),
        result_grad=pltpu.VMEM((2, n, 512), LOW),
    )
MESH = pl.DeviceIdType.MESH

FORWARD_PIECES = (
    [(SM, 128)]
    + [(base + j, STEP) for j in range(0, 2048, STEP) for base in (EU, ED)]
    + [(PJ, STEP), (PJ + 512, STEP), (PJ + 1024, STEP), (AO, STEP), (CI, STEP), (CI + 512, STEP), (CO, STEP)]
    + [(base + j, STEP) for j in range(0, 2048, STEP) for base in (LU, LD)]
)


class Place:
    def __init__(self):
        p, d = lax.axis_index("pipe"), lax.axis_index("dp")
        self.p, self.z, self.y, self.c = p, d // 4, d // 2 % 2, d % 2
        z, y, c = self.z, self.y, self.c
        self.across = (1 - p, d)
        self.beside = (p, z * 4 + (1 - y) * 2 + c)
        self.twin = (p, z * 4 + y * 2 + 1 - c)
        self.column = [(p, (z + j) % 4 * 4 + y * 2 + c) for j in (1, 2, 3)]

    def greet(self):
        for partner in [self.across, self.beside, self.twin] + self.column:
            pl.semaphore_signal(
                pltpu.get_barrier_semaphore(), inc=1, device_id=partner, device_id_type=MESH
            )

    def meet(self):
        pl.semaphore_wait(pltpu.get_barrier_semaphore(), 6)


def remote(source, target, send, arrive, device):
    return pltpu.make_async_remote_copy(
        src_ref=source, dst_ref=target, send_sem=send, recv_sem=arrive, device_id=device, device_id_type=MESH
    )


class Gather:
    def __init__(self, place, ways, shard, w, sems):
        self.place, self.ways, self.shard, self.w = place, ways, shard, w
        self.zr, self.yr, self.xr, self.dr, self.sent, self.own = sems

    def cols(self, k):
        return pl.ds(*FORWARD_PIECES[k])

    def block(self, l, k, z, y):
        return self.w.at[l, z, y, self.place.c, :, self.cols(k)]

    def mine(self, l, k):
        return self.block(l, k, self.place.z, self.place.y)

    def z_copy(self, l, k, j, source=None):
        target = self.mine(l, k)
        source = target if source is None else source
        return remote(source, target, self.sent.at[l, 0], self.zr.at[l, k], self.place.column[j])

    def z_wait(self, l, k):
        three = self.w.at[l, pl.ds(0, 3), self.place.y, self.place.c, :, self.cols(k)]
        remote(three, three, self.sent.at[l, 0], self.zr.at[l, k], self.place.twin).wait_recv()

    def y_copy(self, l, k, y):
        part = self.w.at[l, :, y, self.place.c, :, self.cols(k)]
        return remote(part, part, self.sent.at[l, 1], self.yr.at[l, k], self.place.beside)

    def x_one(self, l, k, source=None):
        target = self.mine(l, k)
        source = target if source is None else source
        return remote(source, target, self.sent.at[l, 2], self.xr.at[l, k], self.place.across)

    def x_all(self, l, k):
        part = self.w.at[l, :, :, self.place.c, :, self.cols(k)]
        return remote(part, part, self.sent.at[l, 3], self.xr.at[l, k], self.place.across)

    def d_copy(self, l, k, c):
        part = self.w.at[l, :, :, c, :, self.cols(k)]
        return remote(part, part, self.sent.at[l, 4], self.dr.at[l, k], self.place.twin)

    def own_copy(self):
        place = self.place
        return pltpu.make_async_copy(
            self.shard, self.w.at[place.p, place.z, place.y, place.c], self.own.at[0]
        )

    def step(self, i, l, k, owner):
        way, piece = self.ways[l][k], self.shard.at[:, self.cols(k)]

        def start():
            if way in "FG":
                self.x_one(l, k, piece).start()
            if way in "FA":
                for j in range(3):
                    self.z_copy(l, k, j, piece).start()

        def spread():
            self.x_one(l, k).wait_recv()
            for j in range(3):
                self.z_copy(l, k, j).start()

        def beside():
            self.z_wait(l, k)
            self.y_copy(l, k, self.place.y).start()

        def across():
            self.y_copy(l, k, 1 - self.place.y).wait_recv()
            if way == ("A" if owner else "G"):
                self.x_all(l, k).start()
            self.d_copy(l, k, self.place.c).start()

        def twin():
            self.x_all(l, k).wait_recv()
            self.d_copy(l, k, self.place.c).start()

        plane = self.place.p == l if owner else self.place.p != l
        pl.when(plane)((start, spread, beside, across, twin)[i])

    def arrived(self, l, k):
        self.d_copy(l, k, 1 - self.place.c).wait_recv()

    def drain(self):
        def finish(l, kind, blocks, ways):
            width = sum(FORWARD_PIECES[k][1] for k, way in enumerate(self.ways[l]) if way in ways)
            if not width:
                return
            if blocks == 8:
                part = self.w.at[l, :, :, 0, :, pl.ds(0, width)]
            else:
                part = self.w.at[l, pl.ds(0, blocks), 0, 0, :, pl.ds(0, width)]
            sent, arrived = self.sent.at[l, kind], self.dr.at[l, 0]
            remote(part, part, sent, arrived, self.place.twin).wait_send()

        for l in range(2):
            finish(l, 4, 8, "FAG")

            @pl.when(self.place.p == l)
            def _():
                finish(l, 0, 3, "FA")
                finish(l, 1, 4, "FA")
                finish(l, 2, 1, "FG")
                finish(l, 3, 8, "A")

            @pl.when(self.place.p != l)
            def _():
                finish(l, 0, 3, "FG")
                finish(l, 1, 4, "FG")
                finish(l, 3, 8, "G")


def gather_sems():
    dma, count = pltpu.SemaphoreType.DMA, len(FORWARD_PIECES)
    return [dma((2, count))] * 4 + [dma((2, 5)), dma((1,))]


BACKWARD_PIECES = (
    [(base + j, STEP) for j in range(0, 2048, STEP) for base in (LD, LU)]
    + [(CO, STEP), (CI, STEP), (CI + 512, STEP), (AO, STEP), (PJ, STEP), (PJ + 512, STEP), (PJ + 1024, STEP)]
    + [(base + j, STEP) for j in range(0, 2048, STEP) for base in (ED, EU)]
    + [(SM, 128)]
)
BACK_INDEX = {column: k for k, (column, _) in enumerate(BACKWARD_PIECES)}
STAGES = 4


class Scatter:
    def __init__(self, place, ways, out, refs, sems):
        self.place, self.ways, self.out = place, ways, out
        self.wide_slot, self.late_slot = scatter_slots(ways)
        self.stage, self.part, self.wide, self.side, self.line, self.late = refs
        self.ds, self.dr, self.sent, self.xr, self.yr, self.zr, self.free = sems
        self.count = 0
        self.slot = {}

    def width(self, k):
        return BACKWARD_PIECES[k][1]

    def cols(self, k):
        return pl.ds(0, self.width(k))

    def d_copy(self, l, k):
        source = self.stage.at[self.slot[l, k], :, :, 1 - self.place.c, :, self.cols(k)]
        target = self.part.at[k, :, :, :, self.cols(k)]
        return remote(source, target, self.ds.at[self.slot[l, k]], self.dr.at[k], self.place.twin)

    def x_wide(self, l, k):
        source = self.part.at[k, :, :, :, self.cols(k)]
        target = self.wide.at[self.wide_slot[l, k], :, :, :, self.cols(k)]
        return remote(source, target, self.sent.at[k], self.xr.at[l, k], self.place.across)

    def x_late(self, l, k):
        source = self.part.at[k, self.place.z, self.place.y, :, self.cols(k)]
        target = self.late.at[self.late_slot[l, k], :, self.cols(k)]
        return remote(source, target, self.sent.at[k], self.xr.at[l, k], self.place.across)

    def y_copy(self, l, k):
        source = self.part.at[k, :, 1 - self.place.y, :, self.cols(k)]
        target = self.side.at[k, :, :, self.cols(k)]
        return remote(source, target, self.sent.at[k], self.yr.at[k], self.place.beside)

    def z_copy(self, l, k, j):
        source = self.part.at[k, (self.place.z + j + 1) % 4, self.place.y, :, self.cols(k)]
        target = self.line.at[k, j, :, self.cols(k)]
        return remote(source, target, self.sent.at[k], self.zr.at[k], self.place.column[j])

    def offer(self, l, column, value):
        k = BACK_INDEX[column]
        width = self.width(k)
        slot = self.count % STAGES
        self.count += 1
        self.slot[l, k] = slot
        self.stage[slot, :, :, :, :, :width] = value.astype(LOW).reshape(4, 2, 2, 32, width)
        if l == 0:
            self.shared(
                k,
                lambda: pl.semaphore_wait(self.free.at[k], 5),
                lambda: pl.semaphore_wait(self.free.at[k], 1),
            )
        self.d_copy(l, k).start()

    def shared(self, k, run, otherwise=lambda: None):
        both = way_planes(self.ways[1][k], 1) & way_planes(self.ways[0][k], 0)
        if len(both) == 2:
            run()
        elif both:
            plane = both.pop()
            pl.when(self.place.p == plane)(run)
            pl.when(self.place.p != plane)(otherwise)
        else:
            otherwise()

    def step(self, i, l, k, owner):
        way, cols = self.ways[l][k], self.cols(k)
        column = pl.ds(BACKWARD_PIECES[k][0], self.width(k))
        place = self.place

        def pair():
            self.d_copy(l, k).wait()
            slot, c = self.slot[l, k], place.c
            stage = self.stage

            total = self.part[k, :, :, :, cols].astype(F32)
            total = total + stage[slot, :, :, c, :, cols].astype(F32)
            self.part[k, :, :, :, cols] = total.astype(LOW)
            if way == "F":
                self.y_copy(l, k).start()
            else:
                plane = place.p == l if way == "G" else place.p != l
                pl.when(plane)(self.x_wide(l, k).start)

        def wide():
            self.x_wide(l, k).wait_recv()
            slot = self.wide_slot[l, k]

            total = self.part[k, :, :, :, cols].astype(F32)
            total = total + self.wide[slot, :, :, :, cols].astype(F32)
            self.part[k, :, :, :, cols] = total.astype(LOW)
            self.y_copy(l, k).start()

        def side():
            self.y_copy(l, k).wait_recv()
            y = place.y

            total = self.part[k, :, y, :, cols].astype(F32)
            total = total + self.side[k, :, :, cols].astype(F32)
            self.part[k, :, y, :, cols] = total.astype(LOW)
            for j in range(3):
                self.z_copy(l, k, j).start()

        def line():
            three = self.line.at[k, :, :, cols]
            remote(three, three, self.sent.at[k], self.zr.at[k], place.twin).wait_recv()
            result = self.part[k, place.z, place.y, :, cols].astype(F32)
            for j in range(3):
                result = result + self.line[k, j, :, cols].astype(F32)
            if owner:
                self.out[:, column] = result
            else:
                self.part[k, place.z, place.y, :, cols] = result.astype(LOW)
                self.x_late(l, k).start()

        def late():
            self.x_late(l, k).wait_recv()
            got = self.late[self.late_slot[l, k], :, cols].astype(F32)
            self.out[:, column] = self.out[:, column] + got if way == "F" else got

        run = (pair, wide, side, line, late)[i - 1]
        if owner is None:
            run()
        else:
            pl.when(place.p == l if owner else place.p != l)(run)

    def release(self, l, k):
        way, place = self.ways[l][k], self.place

        def sent(blocks):
            part = self.late.at[pl.ds(0, blocks), :, self.cols(k)]
            remote(part, part, self.sent.at[k], self.zr.at[k], place.twin).wait_send()

        pl.when(place.p == l)(lambda: sent(8 if way == "G" else 7))
        pl.when(place.p != l)(lambda: sent(8))
        if l == 0:
            return
        pl.semaphore_signal(self.free.at[k], inc=1, device_id=place.twin, device_id_type=MESH)

        def give():
            for device in [place.beside] + place.column:
                pl.semaphore_signal(self.free.at[k], inc=1, device_id=device, device_id_type=MESH)

        self.shared(k, give)


def way_planes(way, l):
    return {"F": {0, 1}, "A": {l}, "G": {1 - l}}[way]


def scatter_slots(ways):
    wide, late, used = {}, {}, [0, 0]
    for l in (1, 0):
        for k, way in enumerate(ways[l]):
            if way in "AG":
                plane = l if way == "A" else 1 - l
                wide[l, k] = used[plane]
                used[plane] += 1
            if way in "FG":
                late[l, k] = sum(1 for item in late if item[0] == l)
    return wide, late


def scatter_refs(ways):
    count = len(BACKWARD_PIECES)
    wide, late = scatter_slots(ways)
    return [
        pltpu.VMEM((STAGES, 4, 2, 2, 32, STEP), LOW),
        pltpu.VMEM((count, 4, 2, 32, STEP), LOW),
        pltpu.VMEM((max(wide.values()) + 1, 4, 2, 32, STEP), LOW),
        pltpu.VMEM((count, 4, 32, STEP), LOW),
        pltpu.VMEM((count, 3, 32, STEP), LOW),
        pltpu.VMEM((max(late.values()) + 1, 32, STEP), LOW),
    ]


def scatter_sems():
    dma, count = pltpu.SemaphoreType.DMA, len(BACKWARD_PIECES)
    each = [dma((count,))]
    return (
        [dma((STAGES,))]
        + each * 2
        + [dma((2, count))]
        + each * 2
        + [pltpu.SemaphoreType.REGULAR((count,))]
    )


GATHER_WAYS = ("AGAGGAGAFFFAAFGGAFAFAAGF", "AAGGFFGAAFGFFFGAAFAFFGFF")
SCATTER_WAYS = ("AFAFFAFGFAFAAGFFFGFFGGAG", "AFFAFGGFFFAAFGFAGFFGFGAF")
FORWARD_ORDER = (
    1, 4, 7, 10, 13, 149, 16, 19, 155, 22, 158, 25, 28, 289, 164, 31, 34, 293, 295, 37, 170, 40, 173, 299, 43,
    176, 302, 433, 304, 46, 437, 49, 308, 439, 310, 52, 185, 443, 188, 55, 313, 446, 191, 58, 448, 316, 61, 319,
    322, 314, 452, 64, 197, 454, 325, 317, 67, 320, 70, 203, 328, 578, 332, 73, 580, 335, 466, 337, 76, 329, 212,
    723, 584, 726, 469, 79, 586, 215, 340, 343, 82, 589, 729, 457, 732, 458, 85, 476, 460, 593, 0, 735, 346, 349,
    461, 88, 341, 479, 595, 463, 481, 224, 352, 464, 91, 738, 747, 599, 0, 741, 227, 94, 347, 750, 356, 487, 0,
    97, 230, 744, 472, 753, 358, 473, 100, 233, 361, 493, 236, 0, 103, 364, 611, 496, 106, 359, 762, 614, 0, 109,
    500, 368, 756, 484, 485, 112, 245, 619, 371, 759, 248, 115, 622, 505, 490, 373, 765, 491, 118, 251, 508, 376,
    774, 626, 0, 768, 121, 254, 0, 380, 0, 382, 374, 512, 0, 0, 124, 257, 0, 771, 0, 385, 780, 632, 377, 0, 515,
    0, 260, 127, 0, 502, 0, 0, 503, 130, 777, 388, 638, 0, 133, 392, 641, 0, 524, 136, 269, 643, 526, 783, 394,
    792, 389, 139, 529, 786, 397, 0, 789, 142, 275, 400, 395, 517, 278, 650, 404, 406, 518, 398, 536, 281, 520,
    653, 409, 521, 401, 0, 655, 795, 0, 284, 0, 658, 798, 287, 807, 801, 412, 415, 810, 804, 548, 532, 0, 550,
    418, 533, 413, 667, 553, 421, 0, 538, 671, 813, 425, 539, 0, 419, 541, 822, 674, 559, 427, 542, 422, 816, 544,
    430, 545, 679, 819, 828, 0, 428, 831, 825, 431, 569, 834, 556, 0, 557, 691, 0, 562, 695, 0, 837, 0, 563, 0, 0,
    565, 846, 698, 0, 0, 566, 0, 0, 840, 0, 843, 571, 852, 704, 572, 0, 574, 0, 855, 575, 849, 0, 712, 861, 0,
    864, 858, 0, 0, 0, 0,
)
BACKWARD_ORDER = (
    0, 0, 219, 222, 0, 225, 228, 0, 231, 0, 234, 0, 237, 0, 0, 509, 508, 512, 240, 0, 511, 243, 361, 518, 0, 0,
    517, 246, 0, 0, 0, 0, 0, 0, 249, 0, 377, 527, 380, 370, 252, 255, 0, 526, 653, 530, 656, 258, 529, 261, 0,
    533, 505, 532, 662, 521, 264, 267, 524, 514, 0, 270, 273, 401, 391, 542, 276, 671, 0, 548, 541, 394, 547, 674,
    665, 0, 652, 796, 942, 279, 655, 799, 945, 649, 939, 282, 0, 668, 677, 410, 661, 805, 951, 557, 285, 288, 658,
    948, 0, 560, 556, 545, 406, 559, 419, 535, 147, 150, 808, 954, 0, 566, 538, 686, 565, 692, 670, 814, 960, 554,
    156, 425, 673, 817, 963, 153, 811, 957, 0, 689, 676, 820, 966, 159, 563, 550, 0, 701, 575, 704, 162, 0, 437,
    0, 574, 436, 698, 165, 679, 969, 0, 168, 710, 427, 682, 972, 0, 443, 569, 171, 685, 829, 975, 289, 442, 707,
    691, 835, 981, 446, 0, 0, 174, 445, 0, 0, 0, 0, 0, 0, 832, 978, 177, 0, 719, 180, 295, 452, 713, 451, 694,
    984, 183, 841, 987, 0, 311, 700, 844, 990, 581, 458, 703, 847, 993, 571, 186, 457, 304, 433, 189, 0, 587, 709,
    853, 999, 192, 464, 590, 850, 996, 195, 0, 463, 316, 455, 439, 596, 198, 718, 862, 1008, 329, 201, 322, 325,
    476, 448, 602, 204, 475, 580, 724, 870, 479, 856, 1002, 715, 1005, 0, 207, 478, 0, 482, 210, 599, 481, 586,
    730, 876, 460, 589, 733, 879, 488, 341, 216, 213, 473, 608, 487, 491, 466, 469, 490, 595, 739, 885, 350, 620,
    353, 601, 745, 891, 623, 485, 626, 617, 359, 632, 494, 607, 751, 897, 635, 355, 497, 629, 619, 763, 909, 503,
    622, 766, 912, 638, 625, 769, 915, 641, 499, 631, 775, 921, 647, 634, 778, 924, 577, 867, 583, 873, 592, 882,
    604, 894, 610, 900, 613, 903, 643, 933, 742, 888, 760, 906, 772, 918, 781, 927, 784, 930, 790, 936,
)


FORWARD_CHUNKS, BACKWARD_CHUNKS, SHARES = 23, 23, 8
MATRICES = ((EU, 2048), (ED, 2048), (PJ, 1536), (AO, 512), (CI, 1024), (CO, 512), (LU, 2048), (LD, 2048))


def swap_halves(columns, back=False):
    parts = []
    for g in range(0, 1024, 256):
        for i in range(8):
            a, b = divmod(i, 2 if back else 4)
            start = g + (b * 128 + a * 32 if back else b * 64 + a * 32)
            parts.append(columns[:, start : start + 32])
    return jnp.concatenate(parts, axis=1)


def fused_kernel(groups, length, flag, span, frames, cotangent, *rest):
    n_acts, act_names, work_names, n = groups
    matrices, small, rest = rest[:8], rest[8:15], rest[15:]
    cos, sin, y_out, dx_out, g_out, w, *rest = rest
    kept, rest = dict(zip(act_names, rest[:n_acts])), rest[n_acts:]
    acts, rest = dict(zip(act_names, rest[:n_acts])), rest[n_acts:]
    work, rest = dict(zip(work_names, rest[: len(work_names)])), rest[len(work_names) :]
    back_refs, rest = rest[:6], rest[6:]
    gather_sem, rest = rest[:6], rest[6:]
    scatter_sem, rest = rest[:7], rest[7:]
    load_sem, keep_sem, given_sem, share_send, share_arrive, shard_sem, shard, proj, rows = rest

    place = Place()
    place.greet()
    p = place.p
    given = [
        pltpu.make_async_copy(source.at[p], work["given"].at[i], given_sem.at[i])
        for i, source in enumerate((frames, cotangent))
    ]
    for copy in given:
        copy.start()
    pieces = []
    for i, (column, width) in enumerate(MATRICES):
        target = proj if column == PJ else shard.at[:, pl.ds(column, width)]
        pieces.append(pltpu.make_async_copy(matrices[i], target, shard_sem.at[i]))
        pieces[-1].start()
    rows[...] = jnp.zeros_like(rows)
    for i, gain in enumerate(small[:6]):
        rows[i : i + 1, :32] = gain[...].astype(F32)
    rows[TAPS : TAPS + KERNEL, :32] = small[6][...].astype(F32)
    shard[:, SM:] = rows[...].astype(LOW)
    for copy in pieces:
        copy.wait()
    shard[:, PJ : PJ + 1024] = swap_halves(proj[:, :1024].astype(F32)).astype(LOW)
    shard[:, PJ + 1024 : AO] = proj[:, 1024:]
    gather = Gather(place, GATHER_WAYS, shard, w, gather_sem)
    gather.own_copy().start()
    place.meet()
    gather.own_copy().wait()

    count = len(FORWARD_PIECES)
    number = {column: k for k, (column, _) in enumerate(FORWARD_PIECES)}
    waiting = []

    def load(l, k):
        cols = gather.cols(k)
        return pltpu.make_async_copy(
            w.at[l, :, :, :, :, cols], work["w"].at[:, :, :, :, cols], load_sem.at[k]
        )

    def need(l, *columns):
        for column in columns:
            load(l, number[column]).wait()

    def keep(module, back):
        copies = []
        for i, (name, index) in enumerate(MODULE_ACTS[module]):
            near, far = acts[name], kept[name]
            if index is not None:
                near, far = near.at[index], far.at[index]
            source, target = (far, near) if back else (near, far)
            copies.append(pltpu.make_async_copy(source, target, keep_sem.at[module, i]))
        return copies

    scatter = Scatter(place, SCATTER_WAYS, g_out, back_refs, scatter_sem)
    run = Layer({**acts, **work, "cos": cos, "sin": sin}, scatter.offer, need)

    def share(i, l, rows):
        results, out = ((run.result, y_out), (run.result_grad, dx_out))[i]
        source, send, arrive = results.at[l, rows], share_send.at[i, l], share_arrive.at[i]
        own = pltpu.make_async_copy(source, out.at[p, rows], send)
        away = remote(source, out.at[p, rows], send, arrive, place.across)
        expected = remote(source, out.at[1 - p, rows], send, arrive, place.across)
        return own, away, expected

    def share_start(i, l, q):
        own, away, _ = share(i, l, pl.ds(q * (n // SHARES), n // SHARES))
        pl.when(p == l)(own.start)
        pl.when(p != l)(away.start)

    def share_finish(i, l):
        own, away, expected = share(i, l, pl.ds(0, n))
        pl.when(p == l)(own.wait)

        @pl.when(p != l)
        def _():
            away.wait_send()
            expected.wait_recv()

    def forward():
        modules = (
            lambda l: run.feed_forward(l, 0, G_EARLY, 0, EU, ED),
            run.attend_forward,
            run.convolve_forward,
            lambda l: run.feed_forward(l, 3, G_LATE, 3, LU, LD),
        )
        for l in range(2):
            run.small_forward(l)
            yield
            for m, module in enumerate(modules):
                if l == 1:
                    for copy in keep(m, False):
                        copy.wait()
                yield from module(l)
                if l == 0:
                    for copy in keep(m, False):
                        if m < 3:
                            copy.start()
                yield
            run.result[l] = run.finish_forward(l)
            if l == 0:
                for copy in keep(3, False):
                    copy.start()
                run.stream[...] = run.result[0].astype(F32)
                for item in waiting:
                    load(*item).start()
                waiting.clear()
                run.first_done = True
            yield

    def reload(m):
        columns = ((EU, 4096), (PJ, 2048), (CI, 1536), (LU, 4096))
        cols = pl.ds(*columns[m])
        return pltpu.make_async_copy(
            w.at[0, :, :, :, :, cols], work["w"].at[:, :, :, :, cols], load_sem.at[m]
        )

    def backward():
        modules = (
            lambda l: run.feed_backward(l, 0, G_EARLY, 0, EU, ED),
            run.attend_backward,
            run.convolve_backward,
            lambda l: run.feed_backward(l, 3, G_LATE, 3, LU, LD),
        )
        for l in (1, 0):
            if l == 0:
                for copy in keep(3, True):
                    copy.wait()
            start = run.given[1].astype(F32) if l == 1 else run.result_grad[1].astype(F32)
            run.grad[...] = run.leave(l, 4, G_FINAL, start)
            for m in (3, 2, 1, 0):
                if l == 0:
                    if m < 3:
                        for copy in keep(m, True):
                            copy.wait()
                    reload(m).wait()
                yield from modules[m](l)
                if l == 1:
                    for copy in keep(m, True):
                        copy.start()
                    reload(m).start()
                yield
            run.small_backward(l)
            run.result_grad[l] = run.grad[...].astype(LOW)
            yield

    def item(code):
        if code == 0:
            return None, None, None, None
        code, owner = divmod(code - 1, 3)
        code, k = divmod(code, count)
        return code // 2, code % 2, k, (True, False, None)[owner]

    run.first_done = False
    chunks, chunk, prepared = forward(), 0, False
    for code in FORWARD_ORDER:
        i, l, k, owner = item(code)
        if not prepared and (code == 0 or i > 0):
            run.prepare(length[p], flag[p], span[p])
            given[0].wait()
            run.stream[...] = run.given[0].astype(F32)
            prepared = True
        if code == 0:
            next(chunks)
            if 0 <= chunk - FORWARD_CHUNKS < SHARES:
                share_start(0, 0, chunk - FORWARD_CHUNKS)
            chunk += 1
            continue
        if i < 5:
            gather.step(i, l, k, owner)
            continue
        gather.arrived(l, k)
        if l == 0 or run.first_done:
            load(l, k).start()
        else:
            waiting.append((l, k))
    given[1].wait()
    chunks, chunk = backward(), 0
    for code in BACKWARD_ORDER:
        if code == 0:
            next(chunks)
            if chunk < SHARES:
                share_start(0, 1, chunk)
            if 0 <= chunk - BACKWARD_CHUNKS < SHARES:
                share_start(1, 1, chunk - BACKWARD_CHUNKS)
            chunk += 1
            if chunk == 2 * BACKWARD_CHUNKS:
                for q in range(SHARES):
                    share_start(1, 0, q)
            continue
        i, l, k, owner = item(code)
        if i < 6:
            scatter.step(i, l, k, owner)
        else:
            scatter.release(l, k)
    gather.drain()
    for i in range(2):
        for l in range(2):
            share_finish(i, l)


def tables(n):
    rates = np.exp(np.arange(32, dtype=np.float64) * (-2.0 * math.log(10000.0) / 64))
    phases = np.arange(n, dtype=np.float64)[:, None] * np.tile(rates, 4)[None, :]
    return np.cos(phases).astype(np.float32), np.sin(phases).astype(np.float32)


def fused(lengths, flags, spans, frames, cotangent, shards):
    n = frames.shape[1]
    acts, work = act_shapes(n), work_shapes(n)
    cosine, sine = tables(n)
    eg, eu, ed, ag, pj, ao, cg, ci, cd, cn, co, lg, lu, ld, fg = shards
    matrices = [eu[0], ed[0].T, pj[0], ao[0], ci[0], co[0], lu[0], ld[0].T]
    small = [eg, ag, cg, cn, lg, fg, cd[0]]
    vmem = pl.BlockSpec(memory_space=pltpu.VMEM)
    hbm = pl.BlockSpec(memory_space=pl.ANY)
    smem = pl.BlockSpec(memory_space=pltpu.SMEM)
    dma, count = pltpu.SemaphoreType.DMA, len(FORWARD_PIECES)
    groups = (len(acts), tuple(acts), tuple(work), n)
    outs = pl.pallas_call(
        functools.partial(fused_kernel, groups),
        out_shape=[
            jax.ShapeDtypeStruct((2, n, 512), LOW),
            jax.ShapeDtypeStruct((2, n, 512), LOW),
            jax.ShapeDtypeStruct((32, COLS), F32),
            jax.ShapeDtypeStruct((2, 4, 2, 2, 32, COLS), LOW),
        ]
        + [jax.ShapeDtypeStruct(shape, kind) for shape, kind in acts.values()],
        in_specs=[smem] * 3 + [hbm] * 10 + [vmem] * 9,
        out_specs=[hbm, hbm, vmem, hbm] + [hbm] * len(acts),
        scratch_shapes=[pltpu.VMEM(shape, kind) for shape, kind in acts.values()]
        + list(work.values())
        + scatter_refs(SCATTER_WAYS)
        + gather_sems()
        + scatter_sems()
        + [dma((count,)), dma((4, 6)), dma((2,)), dma((2, 2)), dma((2,)), dma((8,))]
        + [
            pltpu.VMEM((32, COLS), LOW),
            pltpu.VMEM((32, 1536), LOW),
            pltpu.VMEM((32, 128), F32),
        ],
        compiler_params=pltpu.CompilerParams(
            collective_id=0, has_side_effects=True, vmem_limit_bytes=63 * 2**20
        ),
        cost_estimate=pl.CostEstimate(
            flops=30 * 10**9, bytes_accessed=100 * 2**20, transcendentals=10**7
        ),
    )(lengths[:, 0], flags[:, 0], spans[:, 0], frames, cotangent, *matrices, *small, jnp.asarray(cosine), jnp.asarray(sine))
    return finish(*outs[:3])


def finish_kernel(y, dx, g, y_out, dx_out, *rest):
    outs, (y_here, dx_here, g_here, heads, *small_here), sem = rest[:15], rest[15:-1], rest[-1]
    fetch = [
        pltpu.make_async_copy(source, here, sem.at[i])
        for i, (source, here) in enumerate(((g, g_here), (y, y_here), (dx, dx_here)))
    ]
    for copy in fetch:
        copy.start()
    fetch[0].wait()
    send = []

    def away(source, target):
        send.append(pltpu.make_async_copy(source, target, sem.at[3 + len(send)]))
        send[-1].start()

    for out, (column, width) in zip(outs, MATRICES):
        if column != PJ:
            away(g_here.at[:, pl.ds(column, width)], out)
    heads[:, :1024] = swap_halves(g_here[:, PJ : PJ + 1024], True)
    heads[:, 1024:] = g_here[:, PJ + 1024 : AO]
    away(heads, outs[2])
    for i in range(6):
        small_here[i][...] = g_here[i : i + 1, SM : SM + 32]
    small_here[6][...] = g_here[TAPS : TAPS + KERNEL, SM : SM + 32]
    for here, out in zip(small_here, outs[8:]):
        away(here, out)
    fetch[1].wait()
    away(y_here, y_out)
    fetch[2].wait()
    away(dx_here, dx_out)
    for copy in send:
        copy.wait()


def finish(y, dx, g):
    widths = [(32, width) for _, width in MATRICES] + [(1, 32)] * 6 + [(KERNEL, 32)]
    hbm = pl.BlockSpec(memory_space=pltpu.HBM)
    y, dx, eu, ed, pj, ao, ci, co, lu, ld, eg, ag, cg, cn, lg, fg, cd = pl.pallas_call(
        finish_kernel,
        out_shape=[jax.ShapeDtypeStruct(y.shape, LOW)] * 2
        + [jax.ShapeDtypeStruct(shape, F32) for shape in widths],
        in_specs=[hbm] * 3,
        out_specs=[hbm] * 17,
        scratch_shapes=[
            pltpu.VMEM(y.shape, LOW),
            pltpu.VMEM(y.shape, LOW),
            pltpu.VMEM(g.shape, F32),
            pltpu.VMEM((32, 1536), F32),
        ]
        + [pltpu.VMEM(shape, F32) for shape in widths[8:]]
        + [pltpu.SemaphoreType.DMA((20,))],
        compiler_params=pltpu.CompilerParams(vmem_limit_bytes=62 * 2**20),
    )(y, dx, g)
    return (
        y[None, :, None],
        dx[None, :, None],
        eg,
        eu[None],
        ed.T[None],
        ag,
        pj[None],
        ao[None],
        cg,
        ci[None],
        cd[None],
        cn,
        co[None],
        lg,
        lu[None],
        ld.T[None],
        fg,
    )


def plain_kernel(groups, scalars, w, frames, cotangent, cos, sin, y_out, dx_out, g_out, *rest):
    n_acts, act_names, work_names, n = groups
    kept, rest = dict(zip(act_names, rest[:n_acts])), rest[n_acts:]
    acts, rest = dict(zip(act_names, rest[:n_acts])), rest[n_acts:]
    work, rest = dict(zip(work_names, rest[: len(work_names)])), rest[len(work_names) :]
    stage, sem = rest

    def move(source, target):
        copy = pltpu.make_async_copy(source, target, sem)
        copy.start()
        copy.wait()

    def emit(l, column, value):
        width = value.shape[1]
        stage[:, :width] = value.astype(LOW)
        move(stage.at[:, pl.ds(0, width)], g_out.at[l, :, pl.ds(column, width)])

    run = Layer({**acts, **work, "cos": cos, "sin": sin}, emit, lambda *_: None)

    def whole(*modules):
        for module in modules:
            for _ in module:
                pass

    move(frames, run.given.at[0])
    move(cotangent, run.given.at[1])
    run.prepare(scalars[0], scalars[1], scalars[2])
    run.stream[...] = run.given[0].astype(F32)
    for l in range(2):
        move(w.at[l], work["w"])
        run.small_forward(l)
        whole(
            run.feed_forward(l, 0, G_EARLY, 0, EU, ED),
            run.attend_forward(l),
            run.convolve_forward(l),
            run.feed_forward(l, 3, G_LATE, 3, LU, LD),
        )
        run.result[l] = run.finish_forward(l)
        run.stream[...] = run.result[l].astype(F32)
        if l == 0:
            for name in act_names:
                move(acts[name], kept[name])
    for l in (1, 0):
        if l == 0:
            move(w.at[0], work["w"])
            for name in act_names:
                move(kept[name], acts[name])
        start = run.given[1].astype(F32) if l == 1 else run.result_grad[1].astype(F32)
        run.grad[...] = run.leave(l, 4, G_FINAL, start)
        whole(
            run.feed_backward(l, 3, G_LATE, 3, LU, LD),
            run.convolve_backward(l),
            run.attend_backward(l),
            run.feed_backward(l, 0, G_EARLY, 0, EU, ED),
        )
        run.small_backward(l)
        run.result_grad[l] = run.grad[...].astype(LOW)
    move(run.result, y_out)
    move(run.result_grad, dx_out)


def plain(scalars, weights, frames, cotangent):
    n = frames.shape[0]
    acts, work = act_shapes(n), work_shapes(n)
    cosine, sine = tables(n)
    vmem = pl.BlockSpec(memory_space=pltpu.VMEM)
    hbm = pl.BlockSpec(memory_space=pl.ANY)
    outs = pl.pallas_call(
        functools.partial(plain_kernel, (len(acts), tuple(acts), tuple(work), n)),
        out_shape=[
            jax.ShapeDtypeStruct((2, n, 512), LOW),
            jax.ShapeDtypeStruct((2, n, 512), LOW),
            jax.ShapeDtypeStruct((2, 512, COLS), LOW),
        ]
        + [jax.ShapeDtypeStruct(shape, kind) for shape, kind in acts.values()],
        in_specs=[pl.BlockSpec(memory_space=pltpu.SMEM), hbm, hbm, hbm, vmem, vmem],
        out_specs=[hbm] * (3 + len(acts)),
        scratch_shapes=[pltpu.VMEM(shape, kind) for shape, kind in acts.values()]
        + list(work.values())
        + [pltpu.VMEM((512, STEP), LOW), pltpu.SemaphoreType.DMA],
        compiler_params=pltpu.CompilerParams(vmem_limit_bytes=60 * 2**20),
    )(scalars, weights, frames, cotangent, jnp.asarray(cosine), jnp.asarray(sine))
    return outs[:3]


def pack(shards):
    eg, eu, ed, ag, pj, ao, cg, ci, cd, cn, co, lg, lu, ld, fg = (piece[0] for piece in shards)
    rows = eu.shape[0]
    small = jnp.concatenate(
        [gain[:, None] for gain in (eg, ag, cg, cn, lg, fg)]
        + [cd.T, jnp.zeros((rows, 128 - 6 - KERNEL), LOW)],
        axis=1,
    )
    proj = jnp.concatenate([swap_halves(pj[:, :1024]), pj[:, 1024:]], axis=1)
    return jnp.concatenate([eu, ed.T, proj, ao, ci, co, lu, ld.T, small], axis=1)


def unpack(block):
    proj = block[:, PJ : PJ + 1536]
    proj = jnp.concatenate([swap_halves(proj[:, :1024], True), proj[:, 1024:]], axis=1)
    gains = [block[:, SM + i] for i in range(6)]
    eg, ag, cg, cn, lg, fg = gains
    outs = (
        eg,
        block[:, EU:ED],
        block[:, ED:PJ].T,
        ag,
        proj,
        block[:, AO:CI],
        cg,
        block[:, CI:CO],
        block[:, SM + TAPS : SM + TAPS + KERNEL].T,
        cn,
        block[:, CO:LU],
        lg,
        block[:, LU:LD],
        block[:, LD:SM].T,
        fg,
    )
    return tuple(piece[None] for piece in outs)


def turn_small(block):
    small = block[..., SM : SM + 32].reshape(2, len(OWNERS), 32, 32).swapaxes(2, 3)
    small = jnp.pad(small.reshape(2, 512, 32), ((0, 0), (0, 0), (0, 96)))
    return jnp.concatenate([block[..., :SM], small], axis=2)


def by_collectives(lengths, flags, spans, frames, cotangent, shards):
    section = lax.axis_index("pipe")

    def mine(block):
        return lax.dynamic_index_in_dim(block, section, 0, keepdims=False)

    full = lax.all_gather(pack(shards), ("pipe", "dp"), axis=0, tiled=True)
    full = turn_small(full.reshape(2, 512, COLS)).reshape(2, 4, 2, 2, 32, COLS)
    scalars = jnp.stack([mine(lengths)[0], mine(flags)[0], mine(spans)[0]])
    ys, dxs, grads = plain(scalars, full, mine(frames), mine(cotangent))
    summed = lax.psum_scatter(
        turn_small(grads).reshape(1024, COLS), ("pipe", "dp"), scatter_dimension=0, tiled=True
    ).astype(F32)

    def share(pair):
        own, other = mine(pair), jnp.where(section == 0, pair[1], pair[0])
        got = lax.ppermute(other, "pipe", [(0, 1), (1, 0)])
        pair = jnp.where(section == 0, jnp.stack([own, got]), jnp.stack([got, own]))
        return pair[None, :, None]

    return (share(ys), share(dxs)) + unpack(summed)


def body(frames, cotangent, lengths, stream_flags, span_sizes, *shards):
    run = fused if lax.axis_size("dp") == 16 else by_collectives
    return run(lengths, stream_flags, span_sizes, frames[:, 0], cotangent[:, 0], shards)


def solution(mesh):
    gain, matrix, column = P("pipe", "dp"), P("pipe", "dp", None), P("pipe", None, "dp")
    weights = (gain, matrix, column, gain, matrix, matrix, gain, matrix, column, gain, matrix)
    weights = weights + (gain, matrix, column, gain)
    frames, stacked = P(None, "dp", None, None), P("pipe", None, "dp", None, None)
    return jax.shard_map(
        body,
        mesh=mesh,
        in_specs=(frames, frames) + (P(None, "dp"),) * 3 + weights,
        out_specs=(stacked, stacked) + weights,
        check_vma=False,
    )
```

```python
import functools
import math

import jax
import jax.numpy as jnp
import numpy as np
from jax import lax
from jax.experimental import pallas as pl
from jax.experimental.pallas import tpu as pltpu
from jax.sharding import PartitionSpec as P

HEADS = 8
KERNEL = 15
EPSILON = 1e-05
LOW = jnp.bfloat16
F32 = jnp.float32

EU, ED, PJ, AO, CI, CO, LU, LD, SM = 0, 2048, 4096, 5632, 6144, 7168, 7680, 9728, 11776
COLS = 11904
STEP = 512
OWNERS = [(z, y, c) for z in range(4) for y in range(2) for c in range(2)]
G_EARLY, G_ATTEND, G_CONV, G_MIX, G_LATE, G_FINAL, TAPS = 0, 1, 2, 3, 4, 5, 6


def dot(left, right):
    return lax.dot_general(left, right, (((1,), (0,)), ((), ())), preferred_element_type=F32)


def dot_t(left, right):
    return lax.dot_general(left, right, (((1,), (1,)), ((), ())), preferred_element_type=F32)


def sigmoid(values):
    return 0.5 * jnp.tanh(0.5 * values) + 0.5


def norm_hat(values):
    center = values - jnp.mean(values, axis=-1, keepdims=True)
    rate = lax.rsqrt(jnp.mean(center * center, axis=-1, keepdims=True) + EPSILON)
    return center * rate, rate


def norm_grad(grad_hat, hat, rate):
    first = jnp.mean(grad_hat, axis=-1, keepdims=True)
    second = jnp.mean(grad_hat * hat, axis=-1, keepdims=True)
    return rate * (grad_hat - first - hat * second)


class Layer:
    def __init__(self, refs, emit, need):
        self.__dict__.update(refs)
        self.emit, self.need = emit, need

    def gain(self, l, row):
        return self.sm[l, row : row + 1, :]

    def weight(self, l, column, size=STEP):
        return self.w[:, :, :, :, column : column + size].reshape(512, size)

    def enter(self, l, site, row):
        values = self.stream[...]
        hat, rate = norm_hat(values)
        self.xh[site] = hat.astype(LOW)
        self.rate[l, :, site : site + 1] = rate
        return (hat * self.gain(l, row)).astype(LOW)

    def leave(self, l, site, row, grad):
        hat = self.xh[site].astype(F32)
        rate = self.rate[l, :, site : site + 1]
        self.smg[l, row : row + 1, :] = jnp.sum(grad * hat, axis=0, keepdims=True)
        return norm_grad(grad * self.gain(l, row), hat, rate)

    def small_forward(self, l):
        self.need(l, SM)
        blocks = [self.w[z, y, c, :, SM : SM + 128].astype(F32)[:, :32] for z, y, c in OWNERS]
        self.sm[l] = jnp.concatenate(blocks, axis=1)

    def small_backward(self, l):
        blocks = [self.smg[l, :, 32 * o : 32 * o + 32] for o in range(len(OWNERS))]
        block = jnp.concatenate(blocks, axis=0)
        self.emit(l, SM, jnp.concatenate([block, jnp.zeros((512, 96), F32)], axis=1))

    def feed_forward(self, l, site, row, place, up, down):
        normed = self.enter(l, site, row)
        self.at[place] = normed.T
        side = 0 if site == 0 else 1
        total = None
        for j in range(0, 2048, STEP):
            self.need(l, up + j, down + j)
            inner = dot(normed, self.weight(l, up + j))
            self.u[side, :, j : j + STEP] = inner.astype(LOW)
            hidden = (inner * sigmoid(inner)).astype(LOW)
            term = dot_t(hidden, self.weight(l, down + j))
            total = term if total is None else total + term
            if j + STEP < 2048:
                yield
        self.stream[...] += 0.5 * total

    def feed_backward(self, l, site, row, place, up, down):
        branch = (0.5 * self.grad[...]).astype(LOW)
        turned = branch.T
        side = 0 if site == 0 else 1
        total = None
        for j in range(0, 2048, STEP):
            hidden_grad = dot(branch, self.weight(l, down + j))
            inner = self.u[side, :, j : j + STEP].astype(F32)
            gate = sigmoid(inner)
            hidden = inner * gate
            inner_grad = (hidden_grad * (gate + hidden * (1.0 - gate))).astype(LOW)
            self.emit(l, down + j, dot(turned, hidden.astype(LOW)))
            self.emit(l, up + j, dot(self.at[place], inner_grad))
            term = dot_t(inner_grad, self.weight(l, up + j))
            total = term if total is None else total + term
            if j + STEP < 2048:
                yield
        self.grad[...] += self.leave(l, site, row, total)

    def rotate(self, values, sign):
        cosine, sine = self.cos[...], self.sin[...]
        if sign < 0:
            sine = -sine
        parts = []
        for g in range(0, 512, 256):
            front, behind = values[:, g : g + 128], values[:, g + 128 : g + 256]
            parts += [front * cosine - behind * sine, front * sine + behind * cosine]
        return parts

    def pair_mask(self, j):
        lane = lax.broadcasted_iota(jnp.int32, (1, 256), 1)
        return (lane % 128) // 32 == j

    def head_mask(self, j):
        lane = lax.broadcasted_iota(jnp.int32, (1, 256), 1)
        return lane // 64 == j

    def attend_forward(self, l):
        normed = self.enter(l, 1, G_ATTEND)
        self.at[1] = normed.T
        self.need(l, PJ, PJ + 512, PJ + 1024)
        for which, scale in ((0, 0.125), (1, 1.0)):
            parts = self.rotate(dot(normed, self.weight(l, PJ + 512 * which)), 1)
            for i, part in enumerate(parts):
                self.qkv[which, :, 128 * i : 128 * i + 128] = part.astype(LOW) * LOW(scale)
        self.kt[...] = self.qkv[1].T
        value_rows = dot(normed, self.weight(l, PJ + 1024)).astype(LOW)
        self.qkv[2] = value_rows
        self.vt[...] = value_rows.T
        yield
        for h in range(HEADS):
            g, j = h // 4 * 256, h % 4
            keys = self.qkv[1, :, g : g + 256]
            keys = jnp.where(self.pair_mask(j), keys, jnp.zeros_like(keys))
            scores = dot_t(keys, self.qkv[0, :, g : g + 256]) + self.bias[...]
            powers = jnp.exp(scores - jnp.max(scores, axis=0, keepdims=True))
            powers = powers * (1.0 / jnp.sum(powers, axis=0, keepdims=True))
            powers = powers.astype(LOW)
            self.pt[h] = powers
            self.ot[64 * h : 64 * h + 64, :] = dot(
                self.vt[64 * h : 64 * h + 64, :], powers
            ).astype(LOW)
            yield
        self.need(l, AO)
        self.stream[...] += dot(self.ot[...].T, self.weight(l, AO))

    def attend_backward(self, l):
        branch = self.grad[...].astype(LOW)
        self.emit(l, AO, dot(self.ot[...], branch))
        self.ctx[...] = dot_t(branch, self.weight(l, AO)).astype(LOW)
        yield
        key_total, value_total = [], []
        for g in range(0, 512, 256):
            ctx = self.ctx[:, g : g + 256]
            queries = self.qkv[0, :, g : g + 256]
            values = self.qkv[2, :, g : g + 256]
            key_grad = value_grad = None
            for j in range(4):
                h = g // 64 + j
                head = self.head_mask(j)
                soft_grad = dot_t(jnp.where(head, values, jnp.zeros_like(values)), ctx)
                soft_low = self.pt[h]
                soft = soft_low.astype(F32)
                delta = jnp.sum(soft_grad * soft, axis=0, keepdims=True)
                score_grad = (soft * (soft_grad - delta)).astype(LOW)
                term = dot(soft_low, jnp.where(head, ctx, jnp.zeros_like(ctx)))
                value_grad = term if value_grad is None else value_grad + term
                term = dot(
                    score_grad, jnp.where(self.pair_mask(j), queries, jnp.zeros_like(queries))
                )
                key_grad = term if key_grad is None else key_grad + term
                front, behind = g + 32 * j, g + 128 + 32 * j
                rows = jnp.concatenate(
                    [self.kt[front : front + 32, :], self.kt[behind : behind + 32, :]], axis=0
                )
                turned = dot(rows, score_grad)
                self.qt[front : front + 32, :] = turned[:32]
                self.qt[behind : behind + 32, :] = turned[32:]
                yield
            key_total.append(key_grad)
            value_total.append(value_grad)
        query_grad = self.qt[...].T * 0.125
        query_grad = jnp.concatenate(self.rotate(query_grad, -1), axis=1).astype(LOW)
        key_grad = jnp.concatenate(key_total, axis=1)
        key_grad = jnp.concatenate(self.rotate(key_grad, -1), axis=1).astype(LOW)
        value_grad = jnp.concatenate(value_total, axis=1).astype(LOW)
        total = None
        for i, part in enumerate((query_grad, key_grad, value_grad)):
            self.emit(l, PJ + 512 * i, dot(self.at[1], part))
            term = dot_t(part, self.weight(l, PJ + 512 * i))
            total = term if total is None else total + term
        self.grad[...] += self.leave(l, 1, G_ATTEND, total)

    def tap(self, l, k):
        row = self.sm[l, TAPS + k : TAPS + k + 1, :]
        return row if k <= KERNEL // 2 else row * self.whole

    def convolve_forward(self, l):
        normed = self.enter(l, 2, G_CONV)
        self.at[2] = normed.T
        self.need(l, CI, CI + 512)
        first = dot(normed, self.weight(l, CI))
        second = dot(normed, self.weight(l, CI + 512))
        self.gates[:, :512] = first.astype(LOW)
        self.gates[:, 512:] = second.astype(LOW)
        n = first.shape[0]
        self.pad[0, 8 : n + 8, :] = first * sigmoid(second) * self.live[...]
        yield
        mixed = None
        for k in range(KERNEL):
            term = self.tap(l, k) * self.pad[0, k + 1 : k + 1 + n, :]
            mixed = term if mixed is None else mixed + term
        hat, rate = norm_hat(mixed)
        self.xh[5] = hat.astype(LOW)
        self.rate[l, :, 5:6] = rate
        inner = hat * self.gain(l, G_MIX)
        hidden = (inner * sigmoid(inner)).astype(LOW)
        self.wt[...] = hidden.T
        yield
        self.need(l, CO)
        self.stream[...] += dot(hidden, self.weight(l, CO))

    def convolve_backward(self, l):
        branch = self.grad[...].astype(LOW)
        n = branch.shape[0]
        self.emit(l, CO, dot(self.wt[...], branch))
        hidden_grad = dot_t(branch, self.weight(l, CO))
        yield
        hat = self.xh[5].astype(F32)
        inner = hat * self.gain(l, G_MIX)
        gate = sigmoid(inner)
        inner_grad = hidden_grad * (gate + inner * gate * (1.0 - gate))
        self.pad[1, 8 : n + 8, :] = self.leave(l, 5, G_MIX, inner_grad)
        first = self.gates[:, :512].astype(F32)
        gate = sigmoid(self.gates[:, 512:].astype(F32))
        self.pad[0, 8 : n + 8, :] = first * gate * self.live[...]
        yield
        mixed_grad = self.pad[1, 8 : n + 8, :]
        total = None
        for k in range(KERNEL):
            row = jnp.sum(mixed_grad * self.pad[0, k + 1 : k + 1 + n, :], axis=0, keepdims=True)
            if k > KERNEL // 2:
                row = row * self.whole
            self.smg[l, TAPS + k : TAPS + k + 1, :] = row
            term = self.tap(l, k) * self.pad[1, 15 - k : 15 - k + n, :]
            total = term if total is None else total + term
        total = total * self.live[...]
        first_grad = (total * gate).astype(LOW)
        second_grad = (total * first * gate * (1.0 - gate)).astype(LOW)
        yield
        self.emit(l, CI, dot(self.at[2], first_grad))
        self.emit(l, CI + 512, dot(self.at[2], second_grad))
        total = dot_t(first_grad, self.weight(l, CI))
        total = total + dot_t(second_grad, self.weight(l, CI + 512))
        self.grad[...] += self.leave(l, 2, G_CONV, total)

    def prepare(self, length, flag, span):
        n = self.stream.shape[0]
        key = lax.broadcasted_iota(jnp.int32, (n, n), 0)
        query = lax.broadcasted_iota(jnp.int32, (n, n), 1)
        width = span.astype(F32)
        key_block = jnp.floor((key.astype(F32) + 0.5) / width)
        query_block = jnp.floor((query.astype(F32) + 0.5) / width)
        shown = (key < length) & ((flag == 0) | (key_block <= query_block))
        self.bias[...] = jnp.where(shown, 0.0, -1e30)
        place = lax.broadcasted_iota(jnp.int32, (n, 1), 0)
        self.live[...] = (place < length).astype(F32)
        self.whole = jnp.where(flag == 0, 1.0, 0.0)
        self.pad[...] = jnp.zeros_like(self.pad)
        self.smg[...] = jnp.zeros_like(self.smg)

    def finish_forward(self, l):
        hat, rate = norm_hat(self.stream[...])
        self.xh[4] = hat.astype(LOW)
        self.rate[l, :, 4:5] = rate
        return (hat * self.gain(l, G_FINAL)).astype(LOW)


def act_shapes(n):
    return dict(
        xh=((6, n, 512), LOW),
        at=((4, 512, n), LOW),
        u=((2, n, 2048), LOW),
        qkv=((3, n, 512), LOW),
        kt=((512, n), LOW),
        pt=((HEADS, n, n), LOW),
        ot=((512, n), LOW),
        gates=((n, 1024), LOW),
        wt=((512, n), LOW),
    )


MODULE_ACTS = (
    (("u", 0), ("xh", 0), ("at", 0)),
    (("qkv", None), ("kt", None), ("pt", None), ("ot", None), ("xh", 1), ("at", 1)),
    (("gates", None), ("wt", None), ("xh", 2), ("xh", 5), ("at", 2)),
    (("u", 1), ("xh", 3), ("xh", 4), ("at", 3)),
)


def work_shapes(n):
    return dict(
        w=pltpu.VMEM((4, 2, 2, 32, COLS), LOW),
        stream=pltpu.VMEM((n, 512), F32),
        grad=pltpu.VMEM((n, 512), F32),
        rate=pltpu.VMEM((2, n, 128), F32),
        vt=pltpu.VMEM((512, n), LOW),
        qt=pltpu.VMEM((512, n), F32),
        ctx=pltpu.VMEM((n, 512), LOW),
        pad=pltpu.VMEM((2, n + 16, 512), F32),
        sm=pltpu.VMEM((2, 32, 512), F32),
        smg=pltpu.VMEM((2, 32, 512), F32),
        bias=pltpu.VMEM((n, n), F32),
        live=pltpu.VMEM((n, 1), F32),
        given=pltpu.VMEM((2, n, 512), LOW),
        result=pltpu.VMEM((2, n, 512), LOW),
        result_grad=pltpu.VMEM((2, n, 512), LOW),
    )
MESH = pl.DeviceIdType.MESH

FORWARD_PIECES = (
    [(SM, 128)]
    + [(base + j, STEP) for j in range(0, 2048, STEP) for base in (EU, ED)]
    + [(PJ, STEP), (PJ + 512, STEP), (PJ + 1024, STEP), (AO, STEP), (CI, STEP), (CI + 512, STEP), (CO, STEP)]
    + [(base + j, STEP) for j in range(0, 2048, STEP) for base in (LU, LD)]
)


class Place:
    def __init__(self):
        p, d = lax.axis_index("pipe"), lax.axis_index("dp")
        self.p, self.z, self.y, self.c = p, d // 4, d // 2 % 2, d % 2
        z, y, c = self.z, self.y, self.c
        self.across = (1 - p, d)
        self.beside = (p, z * 4 + (1 - y) * 2 + c)
        self.twin = (p, z * 4 + y * 2 + 1 - c)
        self.column = [(p, (z + j) % 4 * 4 + y * 2 + c) for j in (1, 2, 3)]

    def greet(self):
        for partner in [self.across, self.beside, self.twin] + self.column:
            pl.semaphore_signal(
                pltpu.get_barrier_semaphore(), inc=1, device_id=partner, device_id_type=MESH
            )

    def meet(self):
        pl.semaphore_wait(pltpu.get_barrier_semaphore(), 6)


def remote(source, target, send, arrive, device):
    return pltpu.make_async_remote_copy(
        src_ref=source, dst_ref=target, send_sem=send, recv_sem=arrive, device_id=device, device_id_type=MESH
    )


class Gather:
    def __init__(self, place, ways, shard, w, sems):
        self.place, self.ways, self.shard, self.w = place, ways, shard, w
        self.zr, self.yr, self.xr, self.dr, self.sent, self.own = sems

    def cols(self, k):
        return pl.ds(*FORWARD_PIECES[k])

    def block(self, l, k, z, y):
        return self.w.at[l, z, y, self.place.c, :, self.cols(k)]

    def mine(self, l, k):
        return self.block(l, k, self.place.z, self.place.y)

    def z_copy(self, l, k, j, source=None):
        target = self.mine(l, k)
        source = target if source is None else source
        return remote(source, target, self.sent.at[l, 0], self.zr.at[l, k], self.place.column[j])

    def z_wait(self, l, k):
        three = self.w.at[l, pl.ds(0, 3), self.place.y, self.place.c, :, self.cols(k)]
        remote(three, three, self.sent.at[l, 0], self.zr.at[l, k], self.place.twin).wait_recv()

    def y_copy(self, l, k, y):
        part = self.w.at[l, :, y, self.place.c, :, self.cols(k)]
        return remote(part, part, self.sent.at[l, 1], self.yr.at[l, k], self.place.beside)

    def x_one(self, l, k, source=None):
        target = self.mine(l, k)
        source = target if source is None else source
        return remote(source, target, self.sent.at[l, 2], self.xr.at[l, k], self.place.across)

    def x_all(self, l, k):
        part = self.w.at[l, :, :, self.place.c, :, self.cols(k)]
        return remote(part, part, self.sent.at[l, 3], self.xr.at[l, k], self.place.across)

    def d_copy(self, l, k, c):
        part = self.w.at[l, :, :, c, :, self.cols(k)]
        return remote(part, part, self.sent.at[l, 4], self.dr.at[l, k], self.place.twin)

    def own_copy(self):
        place = self.place
        return pltpu.make_async_copy(
            self.shard, self.w.at[place.p, place.z, place.y, place.c], self.own.at[0]
        )

    def step(self, i, l, k, owner):
        way, piece = self.ways[l][k], self.shard.at[:, self.cols(k)]

        def start():
            if way in "FG":
                self.x_one(l, k, piece).start()
            if way in "FA":
                for j in range(3):
                    self.z_copy(l, k, j, piece).start()

        def spread():
            self.x_one(l, k).wait_recv()
            for j in range(3):
                self.z_copy(l, k, j).start()

        def beside():
            self.z_wait(l, k)
            self.y_copy(l, k, self.place.y).start()

        def across():
            self.y_copy(l, k, 1 - self.place.y).wait_recv()
            if way == ("A" if owner else "G"):
                self.x_all(l, k).start()
            self.d_copy(l, k, self.place.c).start()

        def twin():
            self.x_all(l, k).wait_recv()
            self.d_copy(l, k, self.place.c).start()

        plane = self.place.p == l if owner else self.place.p != l
        pl.when(plane)((start, spread, beside, across, twin)[i])

    def arrived(self, l, k):
        self.d_copy(l, k, 1 - self.place.c).wait_recv()

    def drain(self):
        def finish(l, kind, blocks, ways):
            width = sum(FORWARD_PIECES[k][1] for k, way in enumerate(self.ways[l]) if way in ways)
            if not width:
                return
            if blocks == 8:
                part = self.w.at[l, :, :, 0, :, pl.ds(0, width)]
            else:
                part = self.w.at[l, pl.ds(0, blocks), 0, 0, :, pl.ds(0, width)]
            sent, arrived = self.sent.at[l, kind], self.dr.at[l, 0]
            remote(part, part, sent, arrived, self.place.twin).wait_send()

        for l in range(2):
            finish(l, 4, 8, "FAG")

            @pl.when(self.place.p == l)
            def _():
                finish(l, 0, 3, "FA")
                finish(l, 1, 4, "FA")
                finish(l, 2, 1, "FG")
                finish(l, 3, 8, "A")

            @pl.when(self.place.p != l)
            def _():
                finish(l, 0, 3, "FG")
                finish(l, 1, 4, "FG")
                finish(l, 3, 8, "G")


def gather_sems():
    dma, count = pltpu.SemaphoreType.DMA, len(FORWARD_PIECES)
    return [dma((2, count))] * 4 + [dma((2, 5)), dma((1,))]


BACKWARD_PIECES = (
    [(base + j, STEP) for j in range(0, 2048, STEP) for base in (LD, LU)]
    + [(CO, STEP), (CI, STEP), (CI + 512, STEP), (AO, STEP), (PJ, STEP), (PJ + 512, STEP), (PJ + 1024, STEP)]
    + [(base + j, STEP) for j in range(0, 2048, STEP) for base in (ED, EU)]
    + [(SM, 128)]
)
BACK_INDEX = {column: k for k, (column, _) in enumerate(BACKWARD_PIECES)}
STAGES = 4


class Scatter:
    def __init__(self, place, ways, out, refs, sems):
        self.place, self.ways, self.out = place, ways, out
        self.wide_slot, self.late_slot = scatter_slots(ways)
        self.stage, self.part, self.wide, self.side, self.line, self.late = refs
        self.ds, self.dr, self.sent, self.xr, self.yr, self.zr, self.free = sems
        self.count = 0
        self.slot = {}

    def width(self, k):
        return BACKWARD_PIECES[k][1]

    def cols(self, k):
        return pl.ds(0, self.width(k))

    def d_copy(self, l, k):
        source = self.stage.at[self.slot[l, k], :, :, 1 - self.place.c, :, self.cols(k)]
        target = self.part.at[k, :, :, :, self.cols(k)]
        return remote(source, target, self.ds.at[self.slot[l, k]], self.dr.at[k], self.place.twin)

    def x_wide(self, l, k):
        source = self.part.at[k, :, :, :, self.cols(k)]
        target = self.wide.at[self.wide_slot[l, k], :, :, :, self.cols(k)]
        return remote(source, target, self.sent.at[k], self.xr.at[l, k], self.place.across)

    def x_late(self, l, k):
        source = self.part.at[k, self.place.z, self.place.y, :, self.cols(k)]
        target = self.late.at[self.late_slot[l, k], :, self.cols(k)]
        return remote(source, target, self.sent.at[k], self.xr.at[l, k], self.place.across)

    def y_copy(self, l, k):
        source = self.part.at[k, :, 1 - self.place.y, :, self.cols(k)]
        target = self.side.at[k, :, :, self.cols(k)]
        return remote(source, target, self.sent.at[k], self.yr.at[k], self.place.beside)

    def z_copy(self, l, k, j):
        source = self.part.at[k, (self.place.z + j + 1) % 4, self.place.y, :, self.cols(k)]
        target = self.line.at[k, j, :, self.cols(k)]
        return remote(source, target, self.sent.at[k], self.zr.at[k], self.place.column[j])

    def offer(self, l, column, value):
        k = BACK_INDEX[column]
        width = self.width(k)
        slot = self.count % STAGES
        self.count += 1
        self.slot[l, k] = slot
        self.stage[slot, :, :, :, :, :width] = value.astype(LOW).reshape(4, 2, 2, 32, width)
        if l == 0:
            self.shared(
                k,
                lambda: pl.semaphore_wait(self.free.at[k], 5),
                lambda: pl.semaphore_wait(self.free.at[k], 1),
            )
        self.d_copy(l, k).start()

    def shared(self, k, run, otherwise=lambda: None):
        both = way_planes(self.ways[1][k], 1) & way_planes(self.ways[0][k], 0)
        if len(both) == 2:
            run()
        elif both:
            plane = both.pop()
            pl.when(self.place.p == plane)(run)
            pl.when(self.place.p != plane)(otherwise)
        else:
            otherwise()

    def step(self, i, l, k, owner):
        way, cols = self.ways[l][k], self.cols(k)
        column = pl.ds(BACKWARD_PIECES[k][0], self.width(k))
        place = self.place

        def pair():
            self.d_copy(l, k).wait()
            slot, c = self.slot[l, k], place.c
            stage = self.stage

            total = self.part[k, :, :, :, cols].astype(F32)
            total = total + stage[slot, :, :, c, :, cols].astype(F32)
            self.part[k, :, :, :, cols] = total.astype(LOW)
            if way == "F":
                self.y_copy(l, k).start()
            else:
                plane = place.p == l if way == "G" else place.p != l
                pl.when(plane)(self.x_wide(l, k).start)

        def wide():
            self.x_wide(l, k).wait_recv()
            slot = self.wide_slot[l, k]

            total = self.part[k, :, :, :, cols].astype(F32)
            total = total + self.wide[slot, :, :, :, cols].astype(F32)
            self.part[k, :, :, :, cols] = total.astype(LOW)
            self.y_copy(l, k).start()

        def side():
            self.y_copy(l, k).wait_recv()
            y = place.y

            total = self.part[k, :, y, :, cols].astype(F32)
            total = total + self.side[k, :, :, cols].astype(F32)
            self.part[k, :, y, :, cols] = total.astype(LOW)
            for j in range(3):
                self.z_copy(l, k, j).start()

        def line():
            three = self.line.at[k, :, :, cols]
            remote(three, three, self.sent.at[k], self.zr.at[k], place.twin).wait_recv()
            result = self.part[k, place.z, place.y, :, cols].astype(F32)
            for j in range(3):
                result = result + self.line[k, j, :, cols].astype(F32)
            if owner:
                self.out[:, column] = result
            else:
                self.part[k, place.z, place.y, :, cols] = result.astype(LOW)
                self.x_late(l, k).start()

        def late():
            self.x_late(l, k).wait_recv()
            got = self.late[self.late_slot[l, k], :, cols].astype(F32)
            self.out[:, column] = self.out[:, column] + got if way == "F" else got

        run = (pair, wide, side, line, late)[i - 1]
        if owner is None:
            run()
        else:
            pl.when(place.p == l if owner else place.p != l)(run)

    def release(self, l, k):
        way, place = self.ways[l][k], self.place

        def sent(blocks):
            part = self.late.at[pl.ds(0, blocks), :, self.cols(k)]
            remote(part, part, self.sent.at[k], self.zr.at[k], place.twin).wait_send()

        pl.when(place.p == l)(lambda: sent(8 if way == "G" else 7))
        pl.when(place.p != l)(lambda: sent(8))
        if l == 0:
            return
        pl.semaphore_signal(self.free.at[k], inc=1, device_id=place.twin, device_id_type=MESH)

        def give():
            for device in [place.beside] + place.column:
                pl.semaphore_signal(self.free.at[k], inc=1, device_id=device, device_id_type=MESH)

        self.shared(k, give)


def way_planes(way, l):
    return {"F": {0, 1}, "A": {l}, "G": {1 - l}}[way]


def scatter_slots(ways):
    wide, late, used = {}, {}, [0, 0]
    for l in (1, 0):
        for k, way in enumerate(ways[l]):
            if way in "AG":
                plane = l if way == "A" else 1 - l
                wide[l, k] = used[plane]
                used[plane] += 1
            if way in "FG":
                late[l, k] = sum(1 for item in late if item[0] == l)
    return wide, late


def scatter_refs(ways):
    count = len(BACKWARD_PIECES)
    wide, late = scatter_slots(ways)
    return [
        pltpu.VMEM((STAGES, 4, 2, 2, 32, STEP), LOW),
        pltpu.VMEM((count, 4, 2, 32, STEP), LOW),
        pltpu.VMEM((max(wide.values()) + 1, 4, 2, 32, STEP), LOW),
        pltpu.VMEM((count, 4, 32, STEP), LOW),
        pltpu.VMEM((count, 3, 32, STEP), LOW),
        pltpu.VMEM((max(late.values()) + 1, 32, STEP), LOW),
    ]


def scatter_sems():
    dma, count = pltpu.SemaphoreType.DMA, len(BACKWARD_PIECES)
    each = [dma((count,))]
    return (
        [dma((STAGES,))]
        + each * 2
        + [dma((2, count))]
        + each * 2
        + [pltpu.SemaphoreType.REGULAR((count,))]
    )


GATHER_WAYS = ("AGGAAGGAFAFAFGAFGAFFAGFA", "FGAGFGFAAFGFFFGAAAFGFFFF")
SCATTER_WAYS = ("FAAFFAFGAFFAGFAFGFFGFAGG", "AFGFFAFFGFAFFAFAGFFFGGAG")
FORWARD_ORDER = (
    1, 4, 149, 7, 10, 152, 49, 13, 16, 161, 19, 164, 28, 293, 25, 170, 289, 31, 296, 22, 43, 298, 433, 437, 40,
    185, 64, 37, 34, 578, 723, 308, 176, 209, 73, 301, 442, 76, 305, 440, 52, 58, 316, 194, 445, 313, 46, 452,
    182, 319, 329, 310, 61, 331, 314, 0, 67, 79, 320, 449, 103, 460, 94, 203, 88, 325, 580, 726, 322, 454, 583,
    82, 338, 729, 353, 221, 191, 346, 340, 326, 70, 130, 100, 473, 590, 735, 212, 595, 367, 55, 200, 469, 466,
    118, 587, 334, 347, 218, 349, 484, 245, 85, 463, 470, 759, 599, 109, 97, 464, 335, 355, 592, 738, 457, 497,
    382, 227, 365, 91, 493, 361, 230, 458, 747, 124, 121, 741, 611, 756, 358, 115, 388, 356, 343, 0, 511, 475,
    233, 106, 254, 629, 482, 362, 616, 762, 478, 112, 744, 605, 490, 750, 248, 389, 136, 344, 732, 0, 479, 373,
    753, 640, 491, 780, 502, 236, 406, 371, 620, 133, 0, 397, 487, 139, 509, 260, 526, 374, 638, 0, 488, 777, 127,
    379, 0, 377, 251, 515, 517, 0, 385, 398, 532, 0, 0, 0, 550, 0, 275, 0, 774, 392, 0, 625, 518, 0, 0, 533, 380,
    647, 409, 257, 771, 765, 783, 786, 499, 412, 768, 807, 394, 652, 281, 521, 0, 404, 500, 529, 142, 0, 278, 658,
    798, 505, 0, 400, 656, 523, 0, 395, 541, 0, 792, 506, 795, 419, 424, 524, 789, 671, 542, 664, 536, 401, 0, 0,
    553, 0, 272, 425, 284, 548, 556, 421, 801, 538, 695, 810, 804, 822, 813, 539, 0, 0, 422, 0, 679, 0, 828, 415,
    674, 819, 427, 816, 544, 825, 287, 563, 416, 430, 568, 428, 545, 0, 0, 834, 569, 0, 691, 698, 0, 0, 831, 0,
    431, 0, 0, 837, 0, 565, 0, 559, 840, 566, 571, 560, 0, 701, 0, 706, 572, 0, 574, 846, 843, 852, 575, 858, 861,
    855, 849, 0, 0, 864, 0, 0, 0, 0,
)
BACKWARD_ORDER = (
    0, 0, 222, 219, 0, 225, 228, 0, 231, 0, 0, 0, 234, 237, 0, 243, 514, 515, 240, 0, 0, 509, 508, 517, 518, 246,
    361, 368, 0, 0, 0, 0, 0, 0, 0, 249, 0, 523, 524, 659, 376, 386, 653, 252, 533, 526, 527, 532, 512, 255, 0,
    258, 261, 0, 264, 267, 0, 530, 520, 677, 505, 270, 273, 0, 662, 539, 538, 410, 279, 541, 542, 391, 656, 548,
    547, 400, 276, 0, 649, 939, 282, 652, 796, 942, 0, 671, 556, 557, 668, 559, 560, 674, 285, 799, 945, 288, 658,
    802, 948, 0, 147, 661, 805, 951, 150, 664, 954, 0, 422, 406, 554, 535, 683, 153, 667, 811, 957, 156, 670, 814,
    960, 0, 562, 563, 544, 692, 686, 159, 817, 963, 0, 0, 0, 434, 433, 566, 431, 162, 676, 820, 966, 165, 679,
    969, 0, 425, 550, 427, 704, 168, 682, 826, 972, 0, 0, 0, 0, 0, 442, 443, 575, 707, 698, 445, 446, 701, 292,
    295, 171, 710, 0, 0, 0, 569, 451, 452, 0, 685, 829, 975, 174, 688, 978, 177, 691, 835, 981, 0, 180, 694, 984,
    183, 841, 987, 0, 439, 713, 186, 571, 311, 460, 461, 719, 436, 700, 844, 990, 189, 703, 847, 993, 0, 192, 706,
    850, 996, 195, 853, 999, 0, 578, 464, 463, 473, 472, 207, 590, 455, 304, 201, 313, 326, 198, 856, 1002, 715,
    1005, 0, 204, 862, 1008, 0, 478, 479, 587, 213, 338, 448, 494, 493, 488, 487, 347, 596, 599, 470, 210, 617,
    322, 608, 482, 356, 632, 623, 485, 484, 605, 491, 500, 216, 359, 614, 457, 626, 638, 503, 331, 352, 466, 635,
    577, 721, 629, 583, 873, 589, 733, 879, 475, 580, 870, 867, 496, 586, 730, 876, 595, 739, 885, 644, 647, 616,
    760, 906, 607, 751, 897, 631, 775, 921, 622, 766, 912, 604, 748, 894, 619, 909, 601, 891, 592, 882, 637, 781,
    927, 628, 772, 918, 610, 900, 640, 930, 742, 888, 757, 903, 769, 915, 778, 924, 790, 936, 787, 933,
)


FORWARD_CHUNKS, BACKWARD_CHUNKS, SHARES = 23, 23, 8
MATRICES = ((EU, 2048), (ED, 2048), (PJ, 1536), (AO, 512), (CI, 1024), (CO, 512), (LU, 2048), (LD, 2048))


def swap_halves(columns, back=False):
    parts = []
    for g in range(0, 1024, 256):
        for i in range(8):
            a, b = divmod(i, 2 if back else 4)
            start = g + (b * 128 + a * 32 if back else b * 64 + a * 32)
            parts.append(columns[:, start : start + 32])
    return jnp.concatenate(parts, axis=1)


def fused_kernel(groups, length, flag, span, frames, cotangent, *rest):
    n_acts, act_names, work_names, n = groups
    matrices, small, rest = rest[:8], rest[8:15], rest[15:]
    cos, sin, y_out, dx_out, g_out, w, *rest = rest
    kept, rest = dict(zip(act_names, rest[:n_acts])), rest[n_acts:]
    acts, rest = dict(zip(act_names, rest[:n_acts])), rest[n_acts:]
    work, rest = dict(zip(work_names, rest[: len(work_names)])), rest[len(work_names) :]
    back_refs, rest = rest[:6], rest[6:]
    gather_sem, rest = rest[:6], rest[6:]
    scatter_sem, rest = rest[:7], rest[7:]
    load_sem, keep_sem, given_sem, share_send, share_arrive, shard_sem, shard, proj, rows = rest

    place = Place()
    place.greet()
    p = place.p
    given = [
        pltpu.make_async_copy(source.at[p], work["given"].at[i], given_sem.at[i])
        for i, source in enumerate((frames, cotangent))
    ]
    for copy in given:
        copy.start()
    pieces = []
    for i, (column, width) in enumerate(MATRICES):
        target = proj if column == PJ else shard.at[:, pl.ds(column, width)]
        pieces.append(pltpu.make_async_copy(matrices[i], target, shard_sem.at[i]))
        pieces[-1].start()
    rows[...] = jnp.zeros_like(rows)
    for i, gain in enumerate(small[:6]):
        rows[i : i + 1, :32] = gain[...].astype(F32)
    rows[TAPS : TAPS + KERNEL, :32] = small[6][...].astype(F32)
    shard[:, SM:] = rows[...].astype(LOW)
    for copy in pieces:
        copy.wait()
    shard[:, PJ : PJ + 1024] = swap_halves(proj[:, :1024].astype(F32)).astype(LOW)
    shard[:, PJ + 1024 : AO] = proj[:, 1024:]
    gather = Gather(place, GATHER_WAYS, shard, w, gather_sem)
    gather.own_copy().start()
    place.meet()
    gather.own_copy().wait()

    count = len(FORWARD_PIECES)
    number = {column: k for k, (column, _) in enumerate(FORWARD_PIECES)}
    waiting = []

    def load(l, k):
        cols = gather.cols(k)
        return pltpu.make_async_copy(
            w.at[l, :, :, :, :, cols], work["w"].at[:, :, :, :, cols], load_sem.at[k]
        )

    def need(l, *columns):
        for column in columns:
            load(l, number[column]).wait()

    def keep(module, back):
        copies = []
        for i, (name, index) in enumerate(MODULE_ACTS[module]):
            near, far = acts[name], kept[name]
            if index is not None:
                near, far = near.at[index], far.at[index]
            source, target = (far, near) if back else (near, far)
            copies.append(pltpu.make_async_copy(source, target, keep_sem.at[module, i]))
        return copies

    scatter = Scatter(place, SCATTER_WAYS, g_out, back_refs, scatter_sem)
    run = Layer({**acts, **work, "cos": cos, "sin": sin}, scatter.offer, need)

    def share(i, l, rows):
        results, out = ((run.result, y_out), (run.result_grad, dx_out))[i]
        source, send, arrive = results.at[l, rows], share_send.at[i, l], share_arrive.at[i]
        own = pltpu.make_async_copy(source, out.at[p, rows], send)
        away = remote(source, out.at[p, rows], send, arrive, place.across)
        expected = remote(source, out.at[1 - p, rows], send, arrive, place.across)
        return own, away, expected

    def share_start(i, l, q):
        own, away, _ = share(i, l, pl.ds(q * (n // SHARES), n // SHARES))
        pl.when(p == l)(own.start)
        pl.when(p != l)(away.start)

    def share_finish(i, l):
        own, away, expected = share(i, l, pl.ds(0, n))
        pl.when(p == l)(own.wait)

        @pl.when(p != l)
        def _():
            away.wait_send()
            expected.wait_recv()

    def forward():
        modules = (
            lambda l: run.feed_forward(l, 0, G_EARLY, 0, EU, ED),
            run.attend_forward,
            run.convolve_forward,
            lambda l: run.feed_forward(l, 3, G_LATE, 3, LU, LD),
        )
        for l in range(2):
            run.small_forward(l)
            yield
            for m, module in enumerate(modules):
                if l == 1:
                    for copy in keep(m, False):
                        copy.wait()
                yield from module(l)
                if l == 0:
                    for copy in keep(m, False):
                        if m < 3:
                            copy.start()
                yield
            run.result[l] = run.finish_forward(l)
            if l == 0:
                for copy in keep(3, False):
                    copy.start()
                run.stream[...] = run.result[0].astype(F32)
                for item in waiting:
                    load(*item).start()
                waiting.clear()
                run.first_done = True
            yield

    def reload(m):
        columns = ((EU, 4096), (PJ, 2048), (CI, 1536), (LU, 4096))
        cols = pl.ds(*columns[m])
        return pltpu.make_async_copy(
            w.at[0, :, :, :, :, cols], work["w"].at[:, :, :, :, cols], load_sem.at[m]
        )

    def backward():
        modules = (
            lambda l: run.feed_backward(l, 0, G_EARLY, 0, EU, ED),
            run.attend_backward,
            run.convolve_backward,
            lambda l: run.feed_backward(l, 3, G_LATE, 3, LU, LD),
        )
        for l in (1, 0):
            if l == 0:
                for copy in keep(3, True):
                    copy.wait()
            start = run.given[1].astype(F32) if l == 1 else run.result_grad[1].astype(F32)
            run.grad[...] = run.leave(l, 4, G_FINAL, start)
            for m in (3, 2, 1, 0):
                if l == 0:
                    if m < 3:
                        for copy in keep(m, True):
                            copy.wait()
                    reload(m).wait()
                yield from modules[m](l)
                if l == 1:
                    for copy in keep(m, True):
                        copy.start()
                    reload(m).start()
                yield
            run.small_backward(l)
            run.result_grad[l] = run.grad[...].astype(LOW)
            yield

    def item(code):
        if code == 0:
            return None, None, None, None
        code, owner = divmod(code - 1, 3)
        code, k = divmod(code, count)
        return code // 2, code % 2, k, (True, False, None)[owner]

    run.first_done = False
    chunks, chunk, prepared = forward(), 0, False
    for code in FORWARD_ORDER:
        i, l, k, owner = item(code)
        if not prepared and (code == 0 or i > 0):
            run.prepare(length[p], flag[p], span[p])
            given[0].wait()
            run.stream[...] = run.given[0].astype(F32)
            prepared = True
        if code == 0:
            next(chunks)
            if 0 <= chunk - FORWARD_CHUNKS < SHARES:
                share_start(0, 0, chunk - FORWARD_CHUNKS)
            chunk += 1
            continue
        if i < 5:
            gather.step(i, l, k, owner)
            continue
        gather.arrived(l, k)
        if l == 0 or run.first_done:
            load(l, k).start()
        else:
            waiting.append((l, k))
    given[1].wait()
    chunks, chunk = backward(), 0
    for code in BACKWARD_ORDER:
        if code == 0:
            next(chunks)
            if chunk < SHARES:
                share_start(0, 1, chunk)
            if 0 <= chunk - BACKWARD_CHUNKS < SHARES:
                share_start(1, 1, chunk - BACKWARD_CHUNKS)
            chunk += 1
            if chunk == 2 * BACKWARD_CHUNKS:
                for q in range(SHARES):
                    share_start(1, 0, q)
            continue
        i, l, k, owner = item(code)
        if i < 6:
            scatter.step(i, l, k, owner)
        else:
            scatter.release(l, k)
    gather.drain()
    for i in range(2):
        for l in range(2):
            share_finish(i, l)


def tables(n):
    rates = np.exp(np.arange(32, dtype=np.float64) * (-2.0 * math.log(10000.0) / 64))
    phases = np.arange(n, dtype=np.float64)[:, None] * np.tile(rates, 4)[None, :]
    return np.cos(phases).astype(np.float32), np.sin(phases).astype(np.float32)


def fused(lengths, flags, spans, frames, cotangent, shards):
    n = frames.shape[1]
    acts, work = act_shapes(n), work_shapes(n)
    cosine, sine = tables(n)
    eg, eu, ed, ag, pj, ao, cg, ci, cd, cn, co, lg, lu, ld, fg = shards
    matrices = [eu[0], ed[0].T, pj[0], ao[0], ci[0], co[0], lu[0], ld[0].T]
    small = [eg, ag, cg, cn, lg, fg, cd[0]]
    vmem = pl.BlockSpec(memory_space=pltpu.VMEM)
    hbm = pl.BlockSpec(memory_space=pl.ANY)
    smem = pl.BlockSpec(memory_space=pltpu.SMEM)
    dma, count = pltpu.SemaphoreType.DMA, len(FORWARD_PIECES)
    groups = (len(acts), tuple(acts), tuple(work), n)
    outs = pl.pallas_call(
        functools.partial(fused_kernel, groups),
        out_shape=[
            jax.ShapeDtypeStruct((2, n, 512), LOW),
            jax.ShapeDtypeStruct((2, n, 512), LOW),
            jax.ShapeDtypeStruct((32, COLS), F32),
            jax.ShapeDtypeStruct((2, 4, 2, 2, 32, COLS), LOW),
        ]
        + [jax.ShapeDtypeStruct(shape, kind) for shape, kind in acts.values()],
        in_specs=[smem] * 3 + [hbm] * 10 + [vmem] * 9,
        out_specs=[hbm, hbm, vmem, hbm] + [hbm] * len(acts),
        scratch_shapes=[pltpu.VMEM(shape, kind) for shape, kind in acts.values()]
        + list(work.values())
        + scatter_refs(SCATTER_WAYS)
        + gather_sems()
        + scatter_sems()
        + [dma((count,)), dma((4, 6)), dma((2,)), dma((2, 2)), dma((2,)), dma((8,))]
        + [
            pltpu.VMEM((32, COLS), LOW),
            pltpu.VMEM((32, 1536), LOW),
            pltpu.VMEM((32, 128), F32),
        ],
        compiler_params=pltpu.CompilerParams(
            collective_id=0, has_side_effects=True, vmem_limit_bytes=63 * 2**20
        ),
        cost_estimate=pl.CostEstimate(
            flops=30 * 10**9, bytes_accessed=100 * 2**20, transcendentals=10**7
        ),
    )(lengths[:, 0], flags[:, 0], spans[:, 0], frames, cotangent, *matrices, *small, jnp.asarray(cosine), jnp.asarray(sine))
    return finish(*outs[:3])


def finish_kernel(y, dx, g, y_out, dx_out, *rest):
    outs, (y_here, dx_here, g_here, heads, *small_here), sem = rest[:15], rest[15:-1], rest[-1]
    fetch = [
        pltpu.make_async_copy(source, here, sem.at[i])
        for i, (source, here) in enumerate(((g, g_here), (y, y_here), (dx, dx_here)))
    ]
    for copy in fetch:
        copy.start()
    fetch[0].wait()
    send = []

    def away(source, target):
        send.append(pltpu.make_async_copy(source, target, sem.at[3 + len(send)]))
        send[-1].start()

    for out, (column, width) in zip(outs, MATRICES):
        if column != PJ:
            away(g_here.at[:, pl.ds(column, width)], out)
    heads[:, :1024] = swap_halves(g_here[:, PJ : PJ + 1024], True)
    heads[:, 1024:] = g_here[:, PJ + 1024 : AO]
    away(heads, outs[2])
    for i in range(6):
        small_here[i][...] = g_here[i : i + 1, SM : SM + 32]
    small_here[6][...] = g_here[TAPS : TAPS + KERNEL, SM : SM + 32]
    for here, out in zip(small_here, outs[8:]):
        away(here, out)
    fetch[1].wait()
    away(y_here, y_out)
    fetch[2].wait()
    away(dx_here, dx_out)
    for copy in send:
        copy.wait()


def finish(y, dx, g):
    widths = [(32, width) for _, width in MATRICES] + [(1, 32)] * 6 + [(KERNEL, 32)]
    hbm = pl.BlockSpec(memory_space=pltpu.HBM)
    y, dx, eu, ed, pj, ao, ci, co, lu, ld, eg, ag, cg, cn, lg, fg, cd = pl.pallas_call(
        finish_kernel,
        out_shape=[jax.ShapeDtypeStruct(y.shape, LOW)] * 2
        + [jax.ShapeDtypeStruct(shape, F32) for shape in widths],
        in_specs=[hbm] * 3,
        out_specs=[hbm] * 17,
        scratch_shapes=[
            pltpu.VMEM(y.shape, LOW),
            pltpu.VMEM(y.shape, LOW),
            pltpu.VMEM(g.shape, F32),
            pltpu.VMEM((32, 1536), F32),
        ]
        + [pltpu.VMEM(shape, F32) for shape in widths[8:]]
        + [pltpu.SemaphoreType.DMA((20,))],
        compiler_params=pltpu.CompilerParams(vmem_limit_bytes=62 * 2**20),
    )(y, dx, g)
    return (
        y[None, :, None],
        dx[None, :, None],
        eg,
        eu[None],
        ed.T[None],
        ag,
        pj[None],
        ao[None],
        cg,
        ci[None],
        cd[None],
        cn,
        co[None],
        lg,
        lu[None],
        ld.T[None],
        fg,
    )


def plain_kernel(groups, scalars, w, frames, cotangent, cos, sin, y_out, dx_out, g_out, *rest):
    n_acts, act_names, work_names, n = groups
    kept, rest = dict(zip(act_names, rest[:n_acts])), rest[n_acts:]
    acts, rest = dict(zip(act_names, rest[:n_acts])), rest[n_acts:]
    work, rest = dict(zip(work_names, rest[: len(work_names)])), rest[len(work_names) :]
    stage, sem = rest

    def move(source, target):
        copy = pltpu.make_async_copy(source, target, sem)
        copy.start()
        copy.wait()

    def emit(l, column, value):
        width = value.shape[1]
        stage[:, :width] = value.astype(LOW)
        move(stage.at[:, pl.ds(0, width)], g_out.at[l, :, pl.ds(column, width)])

    run = Layer({**acts, **work, "cos": cos, "sin": sin}, emit, lambda *_: None)

    def whole(*modules):
        for module in modules:
            for _ in module:
                pass

    move(frames, run.given.at[0])
    move(cotangent, run.given.at[1])
    run.prepare(scalars[0], scalars[1], scalars[2])
    run.stream[...] = run.given[0].astype(F32)
    for l in range(2):
        move(w.at[l], work["w"])
        run.small_forward(l)
        whole(
            run.feed_forward(l, 0, G_EARLY, 0, EU, ED),
            run.attend_forward(l),
            run.convolve_forward(l),
            run.feed_forward(l, 3, G_LATE, 3, LU, LD),
        )
        run.result[l] = run.finish_forward(l)
        run.stream[...] = run.result[l].astype(F32)
        if l == 0:
            for name in act_names:
                move(acts[name], kept[name])
    for l in (1, 0):
        if l == 0:
            move(w.at[0], work["w"])
            for name in act_names:
                move(kept[name], acts[name])
        start = run.given[1].astype(F32) if l == 1 else run.result_grad[1].astype(F32)
        run.grad[...] = run.leave(l, 4, G_FINAL, start)
        whole(
            run.feed_backward(l, 3, G_LATE, 3, LU, LD),
            run.convolve_backward(l),
            run.attend_backward(l),
            run.feed_backward(l, 0, G_EARLY, 0, EU, ED),
        )
        run.small_backward(l)
        run.result_grad[l] = run.grad[...].astype(LOW)
    move(run.result, y_out)
    move(run.result_grad, dx_out)


def plain(scalars, weights, frames, cotangent):
    n = frames.shape[0]
    acts, work = act_shapes(n), work_shapes(n)
    cosine, sine = tables(n)
    vmem = pl.BlockSpec(memory_space=pltpu.VMEM)
    hbm = pl.BlockSpec(memory_space=pl.ANY)
    outs = pl.pallas_call(
        functools.partial(plain_kernel, (len(acts), tuple(acts), tuple(work), n)),
        out_shape=[
            jax.ShapeDtypeStruct((2, n, 512), LOW),
            jax.ShapeDtypeStruct((2, n, 512), LOW),
            jax.ShapeDtypeStruct((2, 512, COLS), LOW),
        ]
        + [jax.ShapeDtypeStruct(shape, kind) for shape, kind in acts.values()],
        in_specs=[pl.BlockSpec(memory_space=pltpu.SMEM), hbm, hbm, hbm, vmem, vmem],
        out_specs=[hbm] * (3 + len(acts)),
        scratch_shapes=[pltpu.VMEM(shape, kind) for shape, kind in acts.values()]
        + list(work.values())
        + [pltpu.VMEM((512, STEP), LOW), pltpu.SemaphoreType.DMA],
        compiler_params=pltpu.CompilerParams(vmem_limit_bytes=60 * 2**20),
    )(scalars, weights, frames, cotangent, jnp.asarray(cosine), jnp.asarray(sine))
    return outs[:3]


def pack(shards):
    eg, eu, ed, ag, pj, ao, cg, ci, cd, cn, co, lg, lu, ld, fg = (piece[0] for piece in shards)
    rows = eu.shape[0]
    small = jnp.concatenate(
        [gain[:, None] for gain in (eg, ag, cg, cn, lg, fg)]
        + [cd.T, jnp.zeros((rows, 128 - 6 - KERNEL), LOW)],
        axis=1,
    )
    proj = jnp.concatenate([swap_halves(pj[:, :1024]), pj[:, 1024:]], axis=1)
    return jnp.concatenate([eu, ed.T, proj, ao, ci, co, lu, ld.T, small], axis=1)


def unpack(block):
    proj = block[:, PJ : PJ + 1536]
    proj = jnp.concatenate([swap_halves(proj[:, :1024], True), proj[:, 1024:]], axis=1)
    gains = [block[:, SM + i] for i in range(6)]
    eg, ag, cg, cn, lg, fg = gains
    outs = (
        eg,
        block[:, EU:ED],
        block[:, ED:PJ].T,
        ag,
        proj,
        block[:, AO:CI],
        cg,
        block[:, CI:CO],
        block[:, SM + TAPS : SM + TAPS + KERNEL].T,
        cn,
        block[:, CO:LU],
        lg,
        block[:, LU:LD],
        block[:, LD:SM].T,
        fg,
    )
    return tuple(piece[None] for piece in outs)


def turn_small(block):
    small = block[..., SM : SM + 32].reshape(2, len(OWNERS), 32, 32).swapaxes(2, 3)
    small = jnp.pad(small.reshape(2, 512, 32), ((0, 0), (0, 0), (0, 96)))
    return jnp.concatenate([block[..., :SM], small], axis=2)


def by_collectives(lengths, flags, spans, frames, cotangent, shards):
    section = lax.axis_index("pipe")

    def mine(block):
        return lax.dynamic_index_in_dim(block, section, 0, keepdims=False)

    full = lax.all_gather(pack(shards), ("pipe", "dp"), axis=0, tiled=True)
    full = turn_small(full.reshape(2, 512, COLS)).reshape(2, 4, 2, 2, 32, COLS)
    scalars = jnp.stack([mine(lengths)[0], mine(flags)[0], mine(spans)[0]])
    ys, dxs, grads = plain(scalars, full, mine(frames), mine(cotangent))
    summed = lax.psum_scatter(
        turn_small(grads).reshape(1024, COLS), ("pipe", "dp"), scatter_dimension=0, tiled=True
    ).astype(F32)

    def share(pair):
        own, other = mine(pair), jnp.where(section == 0, pair[1], pair[0])
        got = lax.ppermute(other, "pipe", [(0, 1), (1, 0)])
        pair = jnp.where(section == 0, jnp.stack([own, got]), jnp.stack([got, own]))
        return pair[None, :, None]

    return (share(ys), share(dxs)) + unpack(summed)


def body(frames, cotangent, lengths, stream_flags, span_sizes, *shards):
    run = fused if lax.axis_size("dp") == 16 else by_collectives
    return run(lengths, stream_flags, span_sizes, frames[:, 0], cotangent[:, 0], shards)


def solution(mesh):
    gain, matrix, column = P("pipe", "dp"), P("pipe", "dp", None), P("pipe", None, "dp")
    weights = (gain, matrix, column, gain, matrix, matrix, gain, matrix, column, gain, matrix)
    weights = weights + (gain, matrix, column, gain)
    frames, stacked = P(None, "dp", None, None), P("pipe", None, "dp", None, None)
    return jax.shard_map(
        body,
        mesh=mesh,
        in_specs=(frames, frames) + (P(None, "dp"),) * 3 + weights,
        out_specs=(stacked, stacked) + weights,
        check_vma=False,
    )
```

```python
import functools
import math

import jax
import jax.numpy as jnp
import numpy as np
from jax import lax
from jax.experimental import pallas as pl
from jax.experimental.pallas import tpu as pltpu
from jax.sharding import PartitionSpec as P

HEADS = 8
KERNEL = 15
EPSILON = 1e-05
LOW = jnp.bfloat16
F32 = jnp.float32

EU, ED, PJ, AO, CI, CO, LU, LD, SM = 0, 2048, 4096, 5632, 6144, 7168, 7680, 9728, 11776
COLS = 11904
STEP = 512
OWNERS = [(z, y, c) for z in range(4) for y in range(2) for c in range(2)]
G_EARLY, G_ATTEND, G_CONV, G_MIX, G_LATE, G_FINAL, TAPS = 0, 1, 2, 3, 4, 5, 6


def dot(left, right):
    return lax.dot_general(left, right, (((1,), (0,)), ((), ())), preferred_element_type=F32)


def dot_t(left, right):
    return lax.dot_general(left, right, (((1,), (1,)), ((), ())), preferred_element_type=F32)


def sigmoid(values):
    return 0.5 * jnp.tanh(0.5 * values) + 0.5


def norm_hat(values):
    center = values - jnp.mean(values, axis=-1, keepdims=True)
    rate = lax.rsqrt(jnp.mean(center * center, axis=-1, keepdims=True) + EPSILON)
    return center * rate, rate


def norm_grad(grad_hat, hat, rate):
    first = jnp.mean(grad_hat, axis=-1, keepdims=True)
    second = jnp.mean(grad_hat * hat, axis=-1, keepdims=True)
    return rate * (grad_hat - first - hat * second)


class Layer:
    def __init__(self, refs, emit, need):
        self.__dict__.update(refs)
        self.emit, self.need = emit, need

    def gain(self, l, row):
        return self.sm[l, row : row + 1, :]

    def weight(self, l, column, size=STEP):
        return self.w[:, :, :, :, column : column + size].reshape(512, size)

    def enter(self, l, site, row):
        values = self.stream[...]
        hat, rate = norm_hat(values)
        self.xh[site] = hat.astype(LOW)
        self.rate[l, :, site : site + 1] = rate
        return (hat * self.gain(l, row)).astype(LOW)

    def leave(self, l, site, row, grad):
        hat = self.xh[site].astype(F32)
        rate = self.rate[l, :, site : site + 1]
        self.smg[l, row : row + 1, :] = jnp.sum(grad * hat, axis=0, keepdims=True)
        return norm_grad(grad * self.gain(l, row), hat, rate)

    def small_forward(self, l):
        self.need(l, SM)
        blocks = [self.w[z, y, c, :, SM : SM + 128].astype(F32)[:, :32] for z, y, c in OWNERS]
        self.sm[l] = jnp.concatenate(blocks, axis=1)

    def small_backward(self, l):
        blocks = [self.smg[l, :, 32 * o : 32 * o + 32] for o in range(len(OWNERS))]
        block = jnp.concatenate(blocks, axis=0)
        self.emit(l, SM, jnp.concatenate([block, jnp.zeros((512, 96), F32)], axis=1))

    def feed_forward(self, l, site, row, place, up, down):
        normed = self.enter(l, site, row)
        self.at[place] = normed.T
        side = 0 if site == 0 else 1
        total = None
        for j in range(0, 2048, STEP):
            self.need(l, up + j, down + j)
            inner = dot(normed, self.weight(l, up + j))
            self.u[side, :, j : j + STEP] = inner.astype(LOW)
            hidden = (inner * sigmoid(inner)).astype(LOW)
            term = dot_t(hidden, self.weight(l, down + j))
            total = term if total is None else total + term
            if j + STEP < 2048:
                yield
        self.stream[...] += 0.5 * total

    def feed_backward(self, l, site, row, place, up, down):
        branch = (0.5 * self.grad[...]).astype(LOW)
        turned = branch.T
        side = 0 if site == 0 else 1
        total = None
        for j in range(0, 2048, STEP):
            hidden_grad = dot(branch, self.weight(l, down + j))
            inner = self.u[side, :, j : j + STEP].astype(F32)
            gate = sigmoid(inner)
            hidden = inner * gate
            inner_grad = (hidden_grad * (gate + hidden * (1.0 - gate))).astype(LOW)
            self.emit(l, down + j, dot(turned, hidden.astype(LOW)))
            self.emit(l, up + j, dot(self.at[place], inner_grad))
            term = dot_t(inner_grad, self.weight(l, up + j))
            total = term if total is None else total + term
            if j + STEP < 2048:
                yield
        self.grad[...] += self.leave(l, site, row, total)

    def rotate(self, values, sign):
        cosine, sine = self.cos[...], self.sin[...]
        if sign < 0:
            sine = -sine
        parts = []
        for g in range(0, 512, 256):
            front, behind = values[:, g : g + 128], values[:, g + 128 : g + 256]
            parts += [front * cosine - behind * sine, front * sine + behind * cosine]
        return parts

    def pair_mask(self, j):
        lane = lax.broadcasted_iota(jnp.int32, (1, 256), 1)
        return (lane % 128) // 32 == j

    def head_mask(self, j):
        lane = lax.broadcasted_iota(jnp.int32, (1, 256), 1)
        return lane // 64 == j

    def attend_forward(self, l):
        normed = self.enter(l, 1, G_ATTEND)
        self.at[1] = normed.T
        self.need(l, PJ, PJ + 512, PJ + 1024)
        for which, scale in ((0, 0.125), (1, 1.0)):
            parts = self.rotate(dot(normed, self.weight(l, PJ + 512 * which)), 1)
            for i, part in enumerate(parts):
                self.qkv[which, :, 128 * i : 128 * i + 128] = part.astype(LOW) * LOW(scale)
        self.kt[...] = self.qkv[1].T
        value_rows = dot(normed, self.weight(l, PJ + 1024)).astype(LOW)
        self.qkv[2] = value_rows
        self.vt[...] = value_rows.T
        yield
        for h in range(HEADS):
            g, j = h // 4 * 256, h % 4
            keys = self.qkv[1, :, g : g + 256]
            keys = jnp.where(self.pair_mask(j), keys, jnp.zeros_like(keys))
            scores = dot_t(keys, self.qkv[0, :, g : g + 256]) + self.bias[...]
            powers = jnp.exp(scores - jnp.max(scores, axis=0, keepdims=True))
            powers = powers * (1.0 / jnp.sum(powers, axis=0, keepdims=True))
            powers = powers.astype(LOW)
            self.pt[h] = powers
            self.ot[64 * h : 64 * h + 64, :] = dot(
                self.vt[64 * h : 64 * h + 64, :], powers
            ).astype(LOW)
            yield
        self.need(l, AO)
        self.stream[...] += dot(self.ot[...].T, self.weight(l, AO))

    def attend_backward(self, l):
        branch = self.grad[...].astype(LOW)
        self.emit(l, AO, dot(self.ot[...], branch))
        self.ctx[...] = dot_t(branch, self.weight(l, AO)).astype(LOW)
        yield
        key_total, value_total = [], []
        for g in range(0, 512, 256):
            ctx = self.ctx[:, g : g + 256]
            queries = self.qkv[0, :, g : g + 256]
            values = self.qkv[2, :, g : g + 256]
            key_grad = value_grad = None
            for j in range(4):
                h = g // 64 + j
                head = self.head_mask(j)
                soft_grad = dot_t(jnp.where(head, values, jnp.zeros_like(values)), ctx)
                soft_low = self.pt[h]
                soft = soft_low.astype(F32)
                delta = jnp.sum(soft_grad * soft, axis=0, keepdims=True)
                score_grad = (soft * (soft_grad - delta)).astype(LOW)
                term = dot(soft_low, jnp.where(head, ctx, jnp.zeros_like(ctx)))
                value_grad = term if value_grad is None else value_grad + term
                term = dot(
                    score_grad, jnp.where(self.pair_mask(j), queries, jnp.zeros_like(queries))
                )
                key_grad = term if key_grad is None else key_grad + term
                front, behind = g + 32 * j, g + 128 + 32 * j
                rows = jnp.concatenate(
                    [self.kt[front : front + 32, :], self.kt[behind : behind + 32, :]], axis=0
                )
                turned = dot(rows, score_grad)
                self.qt[front : front + 32, :] = turned[:32]
                self.qt[behind : behind + 32, :] = turned[32:]
                yield
            key_total.append(key_grad)
            value_total.append(value_grad)
        query_grad = self.qt[...].T * 0.125
        query_grad = jnp.concatenate(self.rotate(query_grad, -1), axis=1).astype(LOW)
        key_grad = jnp.concatenate(key_total, axis=1)
        key_grad = jnp.concatenate(self.rotate(key_grad, -1), axis=1).astype(LOW)
        value_grad = jnp.concatenate(value_total, axis=1).astype(LOW)
        total = None
        for i, part in enumerate((query_grad, key_grad, value_grad)):
            self.emit(l, PJ + 512 * i, dot(self.at[1], part))
            term = dot_t(part, self.weight(l, PJ + 512 * i))
            total = term if total is None else total + term
        self.grad[...] += self.leave(l, 1, G_ATTEND, total)

    def tap(self, l, k):
        row = self.sm[l, TAPS + k : TAPS + k + 1, :]
        return row if k <= KERNEL // 2 else row * self.whole

    def convolve_forward(self, l):
        normed = self.enter(l, 2, G_CONV)
        self.at[2] = normed.T
        self.need(l, CI, CI + 512)
        first = dot(normed, self.weight(l, CI))
        second = dot(normed, self.weight(l, CI + 512))
        self.gates[:, :512] = first.astype(LOW)
        self.gates[:, 512:] = second.astype(LOW)
        n = first.shape[0]
        self.pad[0, 8 : n + 8, :] = first * sigmoid(second) * self.live[...]
        yield
        mixed = None
        for k in range(KERNEL):
            term = self.tap(l, k) * self.pad[0, k + 1 : k + 1 + n, :]
            mixed = term if mixed is None else mixed + term
        hat, rate = norm_hat(mixed)
        self.xh[5] = hat.astype(LOW)
        self.rate[l, :, 5:6] = rate
        inner = hat * self.gain(l, G_MIX)
        hidden = (inner * sigmoid(inner)).astype(LOW)
        self.wt[...] = hidden.T
        yield
        self.need(l, CO)
        self.stream[...] += dot(hidden, self.weight(l, CO))

    def convolve_backward(self, l):
        branch = self.grad[...].astype(LOW)
        n = branch.shape[0]
        self.emit(l, CO, dot(self.wt[...], branch))
        hidden_grad = dot_t(branch, self.weight(l, CO))
        yield
        hat = self.xh[5].astype(F32)
        inner = hat * self.gain(l, G_MIX)
        gate = sigmoid(inner)
        inner_grad = hidden_grad * (gate + inner * gate * (1.0 - gate))
        self.pad[1, 8 : n + 8, :] = self.leave(l, 5, G_MIX, inner_grad)
        first = self.gates[:, :512].astype(F32)
        gate = sigmoid(self.gates[:, 512:].astype(F32))
        self.pad[0, 8 : n + 8, :] = first * gate * self.live[...]
        yield
        mixed_grad = self.pad[1, 8 : n + 8, :]
        total = None
        for k in range(KERNEL):
            row = jnp.sum(mixed_grad * self.pad[0, k + 1 : k + 1 + n, :], axis=0, keepdims=True)
            if k > KERNEL // 2:
                row = row * self.whole
            self.smg[l, TAPS + k : TAPS + k + 1, :] = row
            term = self.tap(l, k) * self.pad[1, 15 - k : 15 - k + n, :]
            total = term if total is None else total + term
        total = total * self.live[...]
        first_grad = (total * gate).astype(LOW)
        second_grad = (total * first * gate * (1.0 - gate)).astype(LOW)
        yield
        self.emit(l, CI, dot(self.at[2], first_grad))
        self.emit(l, CI + 512, dot(self.at[2], second_grad))
        total = dot_t(first_grad, self.weight(l, CI))
        total = total + dot_t(second_grad, self.weight(l, CI + 512))
        self.grad[...] += self.leave(l, 2, G_CONV, total)

    def prepare(self, length, flag, span):
        n = self.stream.shape[0]
        key = lax.broadcasted_iota(jnp.int32, (n, n), 0)
        query = lax.broadcasted_iota(jnp.int32, (n, n), 1)
        width = span.astype(F32)
        key_block = jnp.floor((key.astype(F32) + 0.5) / width)
        query_block = jnp.floor((query.astype(F32) + 0.5) / width)
        shown = (key < length) & ((flag == 0) | (key_block <= query_block))
        self.bias[...] = jnp.where(shown, 0.0, -1e30)
        place = lax.broadcasted_iota(jnp.int32, (n, 1), 0)
        self.live[...] = (place < length).astype(F32)
        self.whole = jnp.where(flag == 0, 1.0, 0.0)
        self.pad[...] = jnp.zeros_like(self.pad)
        self.smg[...] = jnp.zeros_like(self.smg)

    def finish_forward(self, l):
        hat, rate = norm_hat(self.stream[...])
        self.xh[4] = hat.astype(LOW)
        self.rate[l, :, 4:5] = rate
        return (hat * self.gain(l, G_FINAL)).astype(LOW)


def act_shapes(n):
    return dict(
        xh=((6, n, 512), LOW),
        at=((4, 512, n), LOW),
        u=((2, n, 2048), LOW),
        qkv=((3, n, 512), LOW),
        kt=((512, n), LOW),
        pt=((HEADS, n, n), LOW),
        ot=((512, n), LOW),
        gates=((n, 1024), LOW),
        wt=((512, n), LOW),
    )


MODULE_ACTS = (
    (("u", 0), ("xh", 0), ("at", 0)),
    (("qkv", None), ("kt", None), ("pt", None), ("ot", None), ("xh", 1), ("at", 1)),
    (("gates", None), ("wt", None), ("xh", 2), ("xh", 5), ("at", 2)),
    (("u", 1), ("xh", 3), ("xh", 4), ("at", 3)),
)


def work_shapes(n):
    return dict(
        w=pltpu.VMEM((4, 2, 2, 32, COLS), LOW),
        stream=pltpu.VMEM((n, 512), F32),
        grad=pltpu.VMEM((n, 512), F32),
        rate=pltpu.VMEM((2, n, 128), F32),
        vt=pltpu.VMEM((512, n), LOW),
        qt=pltpu.VMEM((512, n), F32),
        ctx=pltpu.VMEM((n, 512), LOW),
        pad=pltpu.VMEM((2, n + 16, 512), F32),
        sm=pltpu.VMEM((2, 32, 512), F32),
        smg=pltpu.VMEM((2, 32, 512), F32),
        bias=pltpu.VMEM((n, n), F32),
        live=pltpu.VMEM((n, 1), F32),
        given=pltpu.VMEM((2, n, 512), LOW),
        result=pltpu.VMEM((2, n, 512), LOW),
        result_grad=pltpu.VMEM((2, n, 512), LOW),
    )
MESH = pl.DeviceIdType.MESH

FORWARD_PIECES = (
    [(SM, 128)]
    + [(base + j, STEP) for j in range(0, 2048, STEP) for base in (EU, ED)]
    + [(PJ, STEP), (PJ + 512, STEP), (PJ + 1024, STEP), (AO, STEP), (CI, STEP), (CI + 512, STEP), (CO, STEP)]
    + [(base + j, STEP) for j in range(0, 2048, STEP) for base in (LU, LD)]
)


class Place:
    def __init__(self):
        p, d = lax.axis_index("pipe"), lax.axis_index("dp")
        self.p, self.z, self.y, self.c = p, d // 4, d // 2 % 2, d % 2
        z, y, c = self.z, self.y, self.c
        self.across = (1 - p, d)
        self.beside = (p, z * 4 + (1 - y) * 2 + c)
        self.twin = (p, z * 4 + y * 2 + 1 - c)
        self.column = [(p, (z + j) % 4 * 4 + y * 2 + c) for j in (1, 2, 3)]

    def greet(self):
        for partner in [self.across, self.beside, self.twin] + self.column:
            pl.semaphore_signal(
                pltpu.get_barrier_semaphore(), inc=1, device_id=partner, device_id_type=MESH
            )

    def meet(self):
        pl.semaphore_wait(pltpu.get_barrier_semaphore(), 6)


def remote(source, target, send, arrive, device):
    return pltpu.make_async_remote_copy(
        src_ref=source, dst_ref=target, send_sem=send, recv_sem=arrive, device_id=device, device_id_type=MESH
    )


class Gather:
    def __init__(self, place, ways, shard, w, sems):
        self.place, self.ways, self.shard, self.w = place, ways, shard, w
        self.zr, self.yr, self.xr, self.dr, self.sent, self.own = sems

    def cols(self, k):
        return pl.ds(*FORWARD_PIECES[k])

    def block(self, l, k, z, y):
        return self.w.at[l, z, y, self.place.c, :, self.cols(k)]

    def mine(self, l, k):
        return self.block(l, k, self.place.z, self.place.y)

    def z_copy(self, l, k, j, source=None):
        target = self.mine(l, k)
        source = target if source is None else source
        return remote(source, target, self.sent.at[l, 0], self.zr.at[l, k], self.place.column[j])

    def z_wait(self, l, k):
        three = self.w.at[l, pl.ds(0, 3), self.place.y, self.place.c, :, self.cols(k)]
        remote(three, three, self.sent.at[l, 0], self.zr.at[l, k], self.place.twin).wait_recv()

    def y_copy(self, l, k, y):
        part = self.w.at[l, :, y, self.place.c, :, self.cols(k)]
        return remote(part, part, self.sent.at[l, 1], self.yr.at[l, k], self.place.beside)

    def x_one(self, l, k, source=None):
        target = self.mine(l, k)
        source = target if source is None else source
        return remote(source, target, self.sent.at[l, 2], self.xr.at[l, k], self.place.across)

    def x_all(self, l, k):
        part = self.w.at[l, :, :, self.place.c, :, self.cols(k)]
        return remote(part, part, self.sent.at[l, 3], self.xr.at[l, k], self.place.across)

    def d_copy(self, l, k, c):
        part = self.w.at[l, :, :, c, :, self.cols(k)]
        return remote(part, part, self.sent.at[l, 4], self.dr.at[l, k], self.place.twin)

    def own_start(self):
        place = self.place
        target = self.w.at[place.p, place.z, place.y, place.c]

        def start(l):
            for k in range(len(FORWARD_PIECES)):
                if self.ways[l][k] != "G":
                    cols = self.cols(k)
                    source = self.shard.at[:, cols]
                    pltpu.make_async_copy(source, target.at[:, cols], self.own.at[0]).start()

        for l in range(2):
            pl.when(place.p == l)(functools.partial(start, l))

    def own_wait(self):
        place = self.place
        target = self.w.at[place.p, place.z, place.y, place.c]

        def wait(l):
            pieces = [FORWARD_PIECES[k][1] for k, way in enumerate(self.ways[l]) if way != "G"]
            cols = pl.ds(0, sum(pieces))
            pltpu.make_async_copy(self.shard.at[:, cols], target.at[:, cols], self.own.at[0]).wait()

        for l in range(2):
            pl.when(place.p == l)(functools.partial(wait, l))

    def step(self, i, l, k, owner):
        way, piece = self.ways[l][k], self.shard.at[:, self.cols(k)]

        def start():
            if way in "FG":
                self.x_one(l, k, piece).start()
            if way in "FA":
                for j in range(3):
                    self.z_copy(l, k, j, piece).start()

        def spread():
            self.x_one(l, k).wait_recv()
            for j in range(3):
                self.z_copy(l, k, j).start()

        def beside():
            self.z_wait(l, k)
            self.y_copy(l, k, self.place.y).start()

        def across():
            self.y_copy(l, k, 1 - self.place.y).wait_recv()
            if way == ("A" if owner else "G"):
                self.x_all(l, k).start()
            self.d_copy(l, k, self.place.c).start()

        def twin():
            self.x_all(l, k).wait_recv()
            self.d_copy(l, k, self.place.c).start()

        plane = self.place.p == l if owner else self.place.p != l
        pl.when(plane)((start, spread, beside, across, twin)[i])

    def arrived(self, l, k):
        self.d_copy(l, k, 1 - self.place.c).wait_recv()

    def drain(self):
        def finish(l, kind, blocks, ways):
            width = sum(FORWARD_PIECES[k][1] for k, way in enumerate(self.ways[l]) if way in ways)
            if not width:
                return
            if blocks == 8:
                part = self.w.at[l, :, :, 0, :, pl.ds(0, width)]
            else:
                part = self.w.at[l, pl.ds(0, blocks), 0, 0, :, pl.ds(0, width)]
            sent, arrived = self.sent.at[l, kind], self.dr.at[l, 0]
            remote(part, part, sent, arrived, self.place.twin).wait_send()

        for l in range(2):
            finish(l, 4, 8, "FAG")

            @pl.when(self.place.p == l)
            def _():
                finish(l, 0, 3, "FA")
                finish(l, 1, 4, "FA")
                finish(l, 2, 1, "FG")
                finish(l, 3, 8, "A")

            @pl.when(self.place.p != l)
            def _():
                finish(l, 0, 3, "FG")
                finish(l, 1, 4, "FG")
                finish(l, 3, 8, "G")


def gather_sems():
    dma, count = pltpu.SemaphoreType.DMA, len(FORWARD_PIECES)
    return [dma((2, count))] * 4 + [dma((2, 5)), dma((1,))]


BACKWARD_PIECES = (
    [(base + j, STEP) for j in range(0, 2048, STEP) for base in (LD, LU)]
    + [(CO, STEP), (CI, STEP), (CI + 512, STEP), (AO, STEP), (PJ, STEP), (PJ + 512, STEP), (PJ + 1024, STEP)]
    + [(base + j, STEP) for j in range(0, 2048, STEP) for base in (ED, EU)]
    + [(SM, 128)]
)
BACK_INDEX = {column: k for k, (column, _) in enumerate(BACKWARD_PIECES)}
STAGES = 4


class Scatter:
    def __init__(self, place, ways, out, refs, sems):
        self.place, self.ways, self.out = place, ways, out
        self.wide_slot, self.late_slot = scatter_slots(ways)
        self.stage, self.part, self.wide, self.side, self.line, self.late = refs
        self.ds, self.dr, self.sent, self.xr, self.yr, self.zr, self.free = sems
        self.count = 0
        self.slot = {}

    def width(self, k):
        return BACKWARD_PIECES[k][1]

    def cols(self, k):
        return pl.ds(0, self.width(k))

    def d_copy(self, l, k):
        source = self.stage.at[self.slot[l, k], :, :, 1 - self.place.c, :, self.cols(k)]
        target = self.part.at[k, :, :, :, self.cols(k)]
        return remote(source, target, self.ds.at[self.slot[l, k]], self.dr.at[k], self.place.twin)

    def x_wide(self, l, k):
        source = self.part.at[k, :, :, :, self.cols(k)]
        target = self.wide.at[self.wide_slot[l, k], :, :, :, self.cols(k)]
        return remote(source, target, self.sent.at[k], self.xr.at[l, k], self.place.across)

    def x_late(self, l, k):
        source = self.part.at[k, self.place.z, self.place.y, :, self.cols(k)]
        target = self.late.at[self.late_slot[l, k], :, self.cols(k)]
        return remote(source, target, self.sent.at[k], self.xr.at[l, k], self.place.across)

    def y_copy(self, l, k):
        source = self.part.at[k, :, 1 - self.place.y, :, self.cols(k)]
        target = self.side.at[k, :, :, self.cols(k)]
        return remote(source, target, self.sent.at[k], self.yr.at[k], self.place.beside)

    def z_copy(self, l, k, j):
        source = self.part.at[k, (self.place.z + j + 1) % 4, self.place.y, :, self.cols(k)]
        target = self.line.at[k, j, :, self.cols(k)]
        return remote(source, target, self.sent.at[k], self.zr.at[k], self.place.column[j])

    def offer(self, l, column, value):
        k = BACK_INDEX[column]
        width = self.width(k)
        slot = self.count % STAGES
        self.count += 1
        self.slot[l, k] = slot
        self.stage[slot, :, :, :, :, :width] = value.astype(LOW).reshape(4, 2, 2, 32, width)
        if l == 0:
            self.shared(
                k,
                lambda: pl.semaphore_wait(self.free.at[k], 5),
                lambda: pl.semaphore_wait(self.free.at[k], 1),
            )
        self.d_copy(l, k).start()

    def shared(self, k, run, otherwise=lambda: None):
        both = way_planes(self.ways[1][k], 1) & way_planes(self.ways[0][k], 0)
        if len(both) == 2:
            run()
        elif both:
            plane = both.pop()
            pl.when(self.place.p == plane)(run)
            pl.when(self.place.p != plane)(otherwise)
        else:
            otherwise()

    def step(self, i, l, k, owner):
        way, cols = self.ways[l][k], self.cols(k)
        column = pl.ds(BACKWARD_PIECES[k][0], self.width(k))
        place = self.place

        def pair():
            self.d_copy(l, k).wait()
            slot, c = self.slot[l, k], place.c
            stage = self.stage

            total = self.part[k, :, :, :, cols].astype(F32)
            total = total + stage[slot, :, :, c, :, cols].astype(F32)
            self.part[k, :, :, :, cols] = total.astype(LOW)
            if way == "F":
                self.y_copy(l, k).start()
            else:
                plane = place.p == l if way == "G" else place.p != l
                pl.when(plane)(self.x_wide(l, k).start)

        def wide():
            self.x_wide(l, k).wait_recv()
            slot = self.wide_slot[l, k]

            total = self.part[k, :, :, :, cols].astype(F32)
            total = total + self.wide[slot, :, :, :, cols].astype(F32)
            self.part[k, :, :, :, cols] = total.astype(LOW)
            self.y_copy(l, k).start()

        def side():
            self.y_copy(l, k).wait_recv()
            y = place.y

            total = self.part[k, :, y, :, cols].astype(F32)
            total = total + self.side[k, :, :, cols].astype(F32)
            self.part[k, :, y, :, cols] = total.astype(LOW)
            for j in range(3):
                self.z_copy(l, k, j).start()

        def line():
            three = self.line.at[k, :, :, cols]
            remote(three, three, self.sent.at[k], self.zr.at[k], place.twin).wait_recv()
            result = self.part[k, place.z, place.y, :, cols].astype(F32)
            for j in range(3):
                result = result + self.line[k, j, :, cols].astype(F32)
            if owner:
                self.out[:, column] = result
            else:
                self.part[k, place.z, place.y, :, cols] = result.astype(LOW)
                self.x_late(l, k).start()

        def late():
            self.x_late(l, k).wait_recv()
            got = self.late[self.late_slot[l, k], :, cols].astype(F32)
            self.out[:, column] = self.out[:, column] + got if way == "F" else got

        run = (pair, wide, side, line, late)[i - 1]
        if owner is None:
            run()
        else:
            pl.when(place.p == l if owner else place.p != l)(run)

    def release(self, l, k):
        way, place = self.ways[l][k], self.place

        def sent(blocks):
            part = self.late.at[pl.ds(0, blocks), :, self.cols(k)]
            remote(part, part, self.sent.at[k], self.zr.at[k], place.twin).wait_send()

        pl.when(place.p == l)(lambda: sent(8 if way == "G" else 7))
        pl.when(place.p != l)(lambda: sent(8))
        if l == 0:
            return
        pl.semaphore_signal(self.free.at[k], inc=1, device_id=place.twin, device_id_type=MESH)

        def give():
            for device in [place.beside] + place.column:
                pl.semaphore_signal(self.free.at[k], inc=1, device_id=device, device_id_type=MESH)

        self.shared(k, give)


def way_planes(way, l):
    return {"F": {0, 1}, "A": {l}, "G": {1 - l}}[way]


def scatter_slots(ways):
    wide, late, used = {}, {}, [0, 0]
    for l in (1, 0):
        for k, way in enumerate(ways[l]):
            if way in "AG":
                plane = l if way == "A" else 1 - l
                wide[l, k] = used[plane]
                used[plane] += 1
            if way in "FG":
                late[l, k] = sum(1 for item in late if item[0] == l)
    return wide, late


def scatter_refs(ways):
    count = len(BACKWARD_PIECES)
    wide, late = scatter_slots(ways)
    return [
        pltpu.VMEM((STAGES, 4, 2, 2, 32, STEP), LOW),
        pltpu.VMEM((count, 4, 2, 32, STEP), LOW),
        pltpu.VMEM((max(wide.values()) + 1, 4, 2, 32, STEP), LOW),
        pltpu.VMEM((count, 4, 32, STEP), LOW),
        pltpu.VMEM((count, 3, 32, STEP), LOW),
        pltpu.VMEM((max(late.values()) + 1, 32, STEP), LOW),
    ]


def scatter_sems():
    dma, count = pltpu.SemaphoreType.DMA, len(BACKWARD_PIECES)
    each = [dma((count,))]
    return (
        [dma((STAGES,))]
        + each * 2
        + [dma((2, count))]
        + each * 2
        + [pltpu.SemaphoreType.REGULAR((count,))]
    )


GATHER_WAYS = ("AGGAAGGAFAFAFGAFGAFFAGFA", "FGAGFGFAAFGFFFGAAAFGFFFF")
SCATTER_WAYS = ("FAAFFAFGAFFAGFAFGFFGFAGG", "AFGFFAFFGFAFFAFAGFFFGGAG")
FORWARD_ORDER = (
    1, 4, 149, 7, 10, 152, 49, 13, 16, 161, 19, 164, 28, 293, 25, 170, 289, 31, 296, 22, 43, 298, 433, 437, 40,
    185, 64, 37, 34, 578, 723, 308, 176, 209, 73, 301, 442, 76, 305, 440, 52, 58, 316, 194, 445, 313, 46, 452,
    182, 319, 329, 310, 61, 331, 314, 0, 67, 79, 320, 449, 103, 460, 94, 203, 88, 325, 580, 726, 322, 454, 583,
    82, 338, 729, 353, 221, 191, 346, 340, 326, 70, 130, 100, 473, 590, 735, 212, 595, 367, 55, 200, 469, 466,
    118, 587, 334, 347, 218, 349, 484, 245, 85, 463, 470, 759, 599, 109, 97, 464, 335, 355, 592, 738, 457, 497,
    382, 227, 365, 91, 493, 361, 230, 458, 747, 124, 121, 741, 611, 756, 358, 115, 388, 356, 343, 0, 511, 475,
    233, 106, 254, 629, 482, 362, 616, 762, 478, 112, 744, 605, 490, 750, 248, 389, 136, 344, 732, 0, 479, 373,
    753, 640, 491, 780, 502, 236, 406, 371, 620, 133, 0, 397, 487, 139, 509, 260, 526, 374, 638, 0, 488, 777, 127,
    379, 0, 377, 251, 515, 517, 0, 385, 398, 532, 0, 0, 0, 550, 0, 275, 0, 774, 392, 0, 625, 518, 0, 0, 533, 380,
    647, 409, 257, 771, 765, 783, 786, 499, 412, 768, 807, 394, 652, 281, 521, 0, 404, 500, 529, 142, 0, 278, 658,
    798, 505, 0, 400, 656, 523, 0, 395, 541, 0, 792, 506, 795, 419, 424, 524, 789, 671, 542, 664, 536, 401, 0, 0,
    553, 0, 272, 425, 284, 548, 556, 421, 801, 538, 695, 810, 804, 822, 813, 539, 0, 0, 422, 0, 679, 0, 828, 415,
    674, 819, 427, 816, 544, 825, 287, 563, 416, 430, 568, 428, 545, 0, 0, 834, 569, 0, 691, 698, 0, 0, 831, 0,
    431, 0, 0, 837, 0, 565, 0, 559, 840, 566, 571, 560, 0, 701, 0, 706, 572, 0, 574, 846, 843, 852, 575, 858, 861,
    855, 849, 0, 0, 864, 0, 0, 0, 0,
)
BACKWARD_ORDER = (
    0, 0, 222, 219, 0, 225, 228, 0, 231, 0, 0, 0, 234, 237, 0, 243, 514, 515, 240, 0, 0, 509, 508, 517, 518, 246,
    361, 368, 0, 0, 0, 0, 0, 0, 0, 249, 0, 523, 524, 659, 376, 386, 653, 252, 533, 526, 527, 532, 512, 255, 0,
    258, 261, 0, 264, 267, 0, 530, 520, 677, 505, 270, 273, 0, 662, 539, 538, 410, 279, 541, 542, 391, 656, 548,
    547, 400, 276, 0, 649, 939, 282, 652, 796, 942, 0, 671, 556, 557, 668, 559, 560, 674, 285, 799, 945, 288, 658,
    802, 948, 0, 147, 661, 805, 951, 150, 664, 954, 0, 422, 406, 554, 535, 683, 153, 667, 811, 957, 156, 670, 814,
    960, 0, 562, 563, 544, 692, 686, 159, 817, 963, 0, 0, 0, 434, 433, 566, 431, 162, 676, 820, 966, 165, 679,
    969, 0, 425, 550, 427, 704, 168, 682, 826, 972, 0, 0, 0, 0, 0, 442, 443, 575, 707, 698, 445, 446, 701, 292,
    295, 171, 710, 0, 0, 0, 569, 451, 452, 0, 685, 829, 975, 174, 688, 978, 177, 691, 835, 981, 0, 180, 694, 984,
    183, 841, 987, 0, 439, 713, 186, 571, 311, 460, 461, 719, 436, 700, 844, 990, 189, 703, 847, 993, 0, 192, 706,
    850, 996, 195, 853, 999, 0, 578, 464, 463, 473, 472, 207, 590, 455, 304, 201, 313, 326, 198, 856, 1002, 715,
    1005, 0, 204, 862, 1008, 0, 478, 479, 587, 213, 338, 448, 494, 493, 488, 487, 347, 596, 599, 470, 210, 617,
    322, 608, 482, 356, 632, 623, 485, 484, 605, 491, 500, 216, 359, 614, 457, 626, 638, 503, 331, 352, 466, 635,
    577, 721, 629, 583, 873, 589, 733, 879, 475, 580, 870, 867, 496, 586, 730, 876, 595, 739, 885, 644, 647, 616,
    760, 906, 607, 751, 897, 631, 775, 921, 622, 766, 912, 604, 748, 894, 619, 909, 601, 891, 592, 882, 637, 781,
    927, 628, 772, 918, 610, 900, 640, 930, 742, 888, 757, 903, 769, 915, 778, 924, 790, 936, 787, 933,
)


FORWARD_CHUNKS, BACKWARD_CHUNKS, SHARES = 23, 23, 8
MATRICES = ((EU, 2048), (ED, 2048), (PJ, 1536), (AO, 512), (CI, 1024), (CO, 512), (LU, 2048), (LD, 2048))


def swap_halves(columns, back=False):
    parts = []
    for g in range(0, 1024, 256):
        for i in range(8):
            a, b = divmod(i, 2 if back else 4)
            start = g + (b * 128 + a * 32 if back else b * 64 + a * 32)
            parts.append(columns[:, start : start + 32])
    return jnp.concatenate(parts, axis=1)


def fused_kernel(groups, length, flag, span, frames, cotangent, *rest):
    n_acts, act_names, work_names, n = groups
    matrices, small, rest = rest[:8], rest[8:15], rest[15:]
    cos, sin, y_out, dx_out, g_out, w, *rest = rest
    kept, rest = dict(zip(act_names, rest[:n_acts])), rest[n_acts:]
    acts, rest = dict(zip(act_names, rest[:n_acts])), rest[n_acts:]
    work, rest = dict(zip(work_names, rest[: len(work_names)])), rest[len(work_names) :]
    back_refs, rest = rest[:6], rest[6:]
    gather_sem, rest = rest[:6], rest[6:]
    scatter_sem, rest = rest[:7], rest[7:]
    load_sem, keep_sem, given_sem, share_send, share_arrive, shard_sem, shard, proj, rows = rest

    place = Place()
    place.greet()
    p = place.p
    given = [
        pltpu.make_async_copy(source.at[p], work["given"].at[i], given_sem.at[i])
        for i, source in enumerate((frames, cotangent))
    ]
    for copy in given:
        copy.start()
    pieces = []
    for i, (column, width) in enumerate(MATRICES):
        target = proj if column == PJ else shard.at[:, pl.ds(column, width)]
        pieces.append(pltpu.make_async_copy(matrices[i], target, shard_sem.at[i]))
        pieces[-1].start()
    rows[...] = jnp.zeros_like(rows)
    for i, gain in enumerate(small[:6]):
        rows[i : i + 1, :32] = gain[...].astype(F32)
    rows[TAPS : TAPS + KERNEL, :32] = small[6][...].astype(F32)
    shard[:, SM:] = rows[...].astype(LOW)
    for copy in pieces:
        copy.wait()
    gather = Gather(place, GATHER_WAYS, shard, w, gather_sem)
    place.meet()

    count = len(FORWARD_PIECES)
    number = {column: k for k, (column, _) in enumerate(FORWARD_PIECES)}
    waiting = []

    def load(l, k):
        cols = gather.cols(k)
        return pltpu.make_async_copy(
            w.at[l, :, :, :, :, cols], work["w"].at[:, :, :, :, cols], load_sem.at[k]
        )

    def need(l, *columns):
        for column in columns:
            load(l, number[column]).wait()

    def keep(module, back):
        copies = []
        for i, (name, index) in enumerate(MODULE_ACTS[module]):
            near, far = acts[name], kept[name]
            if index is not None:
                near, far = near.at[index], far.at[index]
            source, target = (far, near) if back else (near, far)
            copies.append(pltpu.make_async_copy(source, target, keep_sem.at[module, i]))
        return copies

    scatter = Scatter(place, SCATTER_WAYS, g_out, back_refs, scatter_sem)
    run = Layer({**acts, **work, "cos": cos, "sin": sin}, scatter.offer, need)

    def share(i, l, rows):
        results, out = ((run.result, y_out), (run.result_grad, dx_out))[i]
        source, send, arrive = results.at[l, rows], share_send.at[i, l], share_arrive.at[i]
        own = pltpu.make_async_copy(source, out.at[p, rows], send)
        away = remote(source, out.at[p, rows], send, arrive, place.across)
        expected = remote(source, out.at[1 - p, rows], send, arrive, place.across)
        return own, away, expected

    def share_start(i, l, q):
        own, away, _ = share(i, l, pl.ds(q * (n // SHARES), n // SHARES))
        pl.when(p == l)(own.start)
        pl.when(p != l)(away.start)

    def share_finish(i, l):
        own, away, expected = share(i, l, pl.ds(0, n))
        pl.when(p == l)(own.wait)

        @pl.when(p != l)
        def _():
            away.wait_send()
            expected.wait_recv()

    def forward():
        modules = (
            lambda l: run.feed_forward(l, 0, G_EARLY, 0, EU, ED),
            run.attend_forward,
            run.convolve_forward,
            lambda l: run.feed_forward(l, 3, G_LATE, 3, LU, LD),
        )
        for l in range(2):
            run.small_forward(l)
            yield
            for m, module in enumerate(modules):
                if l == 1:
                    for copy in keep(m, False):
                        copy.wait()
                yield from module(l)
                if l == 0:
                    for copy in keep(m, False):
                        if m < 3:
                            copy.start()
                yield
            run.result[l] = run.finish_forward(l)
            if l == 0:
                for copy in keep(3, False):
                    copy.start()
                run.stream[...] = run.result[0].astype(F32)
                for item in waiting:
                    load(*item).start()
                waiting.clear()
                run.first_done = True
            yield

    def reload(m):
        columns = ((EU, 4096), (PJ, 2048), (CI, 1536), (LU, 4096))
        cols = pl.ds(*columns[m])
        return pltpu.make_async_copy(
            w.at[0, :, :, :, :, cols], work["w"].at[:, :, :, :, cols], load_sem.at[m]
        )

    def backward():
        modules = (
            lambda l: run.feed_backward(l, 0, G_EARLY, 0, EU, ED),
            run.attend_backward,
            run.convolve_backward,
            lambda l: run.feed_backward(l, 3, G_LATE, 3, LU, LD),
        )
        for l in (1, 0):
            if l == 0:
                for copy in keep(3, True):
                    copy.wait()
            start = run.given[1].astype(F32) if l == 1 else run.result_grad[1].astype(F32)
            run.grad[...] = run.leave(l, 4, G_FINAL, start)
            for m in (3, 2, 1, 0):
                if l == 0:
                    if m < 3:
                        for copy in keep(m, True):
                            copy.wait()
                    reload(m).wait()
                yield from modules[m](l)
                if l == 1:
                    for copy in keep(m, True):
                        copy.start()
                    reload(m).start()
                yield
            run.small_backward(l)
            run.result_grad[l] = run.grad[...].astype(LOW)
            yield

    def item(code):
        if code == 0:
            return None, None, None, None
        code, owner = divmod(code - 1, 3)
        code, k = divmod(code, count)
        return code // 2, code % 2, k, (True, False, None)[owner]

    run.first_done = False
    chunks, chunk, prepared, packed, owned = forward(), 0, False, False, False
    for code in FORWARD_ORDER:
        i, l, k, owner = item(code)
        if not packed and (i == 2 or i == 0 and PJ <= FORWARD_PIECES[k][0] < AO):
            shard[:, PJ : PJ + 1024] = swap_halves(proj[:, :1024].astype(F32)).astype(LOW)
            shard[:, PJ + 1024 : AO] = proj[:, 1024:]
            gather.own_start()
            packed = True
        if not owned and i == 2:
            gather.own_wait()
            owned = True
        if not prepared and (code == 0 or i > 0):
            run.prepare(length[p], flag[p], span[p])
            given[0].wait()
            run.stream[...] = run.given[0].astype(F32)
            prepared = True
        if code == 0:
            next(chunks)
            if 0 <= chunk - FORWARD_CHUNKS < SHARES:
                share_start(0, 0, chunk - FORWARD_CHUNKS)
            chunk += 1
            continue
        if i < 5:
            gather.step(i, l, k, owner)
            continue
        gather.arrived(l, k)
        if l == 0 or run.first_done:
            load(l, k).start()
        else:
            waiting.append((l, k))
    given[1].wait()
    chunks, chunk = backward(), 0
    for code in BACKWARD_ORDER:
        if code == 0:
            next(chunks)
            if chunk < SHARES:
                share_start(0, 1, chunk)
            if 0 <= chunk - BACKWARD_CHUNKS < SHARES:
                share_start(1, 1, chunk - BACKWARD_CHUNKS)
            chunk += 1
            if chunk == 2 * BACKWARD_CHUNKS:
                for q in range(SHARES):
                    share_start(1, 0, q)
            continue
        i, l, k, owner = item(code)
        if i < 6:
            scatter.step(i, l, k, owner)
        else:
            scatter.release(l, k)
    gather.drain()
    for i in range(2):
        for l in range(2):
            share_finish(i, l)


def tables(n):
    rates = np.exp(np.arange(32, dtype=np.float64) * (-2.0 * math.log(10000.0) / 64))
    phases = np.arange(n, dtype=np.float64)[:, None] * np.tile(rates, 4)[None, :]
    return np.cos(phases).astype(np.float32), np.sin(phases).astype(np.float32)


def fused(lengths, flags, spans, frames, cotangent, shards):
    n = frames.shape[1]
    acts, work = act_shapes(n), work_shapes(n)
    cosine, sine = tables(n)
    eg, eu, ed, ag, pj, ao, cg, ci, cd, cn, co, lg, lu, ld, fg = shards
    matrices = [eu[0], ed[0].T, pj[0], ao[0], ci[0], co[0], lu[0], ld[0].T]
    small = [eg, ag, cg, cn, lg, fg, cd[0]]
    vmem = pl.BlockSpec(memory_space=pltpu.VMEM)
    hbm = pl.BlockSpec(memory_space=pl.ANY)
    smem = pl.BlockSpec(memory_space=pltpu.SMEM)
    dma, count = pltpu.SemaphoreType.DMA, len(FORWARD_PIECES)
    groups = (len(acts), tuple(acts), tuple(work), n)
    outs = pl.pallas_call(
        functools.partial(fused_kernel, groups),
        out_shape=[
            jax.ShapeDtypeStruct((2, n, 512), LOW),
            jax.ShapeDtypeStruct((2, n, 512), LOW),
            jax.ShapeDtypeStruct((32, COLS), F32),
            jax.ShapeDtypeStruct((2, 4, 2, 2, 32, COLS), LOW),
        ]
        + [jax.ShapeDtypeStruct(shape, kind) for shape, kind in acts.values()],
        in_specs=[smem] * 3 + [hbm] * 10 + [vmem] * 9,
        out_specs=[hbm, hbm, vmem, hbm] + [hbm] * len(acts),
        scratch_shapes=[pltpu.VMEM(shape, kind) for shape, kind in acts.values()]
        + list(work.values())
        + scatter_refs(SCATTER_WAYS)
        + gather_sems()
        + scatter_sems()
        + [dma((count,)), dma((4, 6)), dma((2,)), dma((2, 2)), dma((2,)), dma((8,))]
        + [
            pltpu.VMEM((32, COLS), LOW),
            pltpu.VMEM((32, 1536), LOW),
            pltpu.VMEM((32, 128), F32),
        ],
        compiler_params=pltpu.CompilerParams(
            collective_id=0, has_side_effects=True, vmem_limit_bytes=63 * 2**20
        ),
        cost_estimate=pl.CostEstimate(
            flops=30 * 10**9, bytes_accessed=100 * 2**20, transcendentals=10**7
        ),
    )(lengths[:, 0], flags[:, 0], spans[:, 0], frames, cotangent, *matrices, *small, jnp.asarray(cosine), jnp.asarray(sine))
    return finish(*outs[:3])


def finish_kernel(y, dx, g, y_out, dx_out, *rest):
    outs, (y_here, dx_here, g_here, heads, *small_here), sem = rest[:15], rest[15:-1], rest[-1]
    fetch = [
        pltpu.make_async_copy(source, here, sem.at[i])
        for i, (source, here) in enumerate(((g, g_here), (y, y_here), (dx, dx_here)))
    ]
    for copy in fetch:
        copy.start()
    fetch[0].wait()
    send = []

    def away(source, target):
        send.append(pltpu.make_async_copy(source, target, sem.at[3 + len(send)]))
        send[-1].start()

    for out, (column, width) in zip(outs, MATRICES):
        if column != PJ:
            away(g_here.at[:, pl.ds(column, width)], out)
    heads[:, :1024] = swap_halves(g_here[:, PJ : PJ + 1024], True)
    heads[:, 1024:] = g_here[:, PJ + 1024 : AO]
    away(heads, outs[2])
    for i in range(6):
        small_here[i][...] = g_here[i : i + 1, SM : SM + 32]
    small_here[6][...] = g_here[TAPS : TAPS + KERNEL, SM : SM + 32]
    for here, out in zip(small_here, outs[8:]):
        away(here, out)
    fetch[1].wait()
    away(y_here, y_out)
    fetch[2].wait()
    away(dx_here, dx_out)
    for copy in send:
        copy.wait()


def finish(y, dx, g):
    widths = [(32, width) for _, width in MATRICES] + [(1, 32)] * 6 + [(KERNEL, 32)]
    hbm = pl.BlockSpec(memory_space=pltpu.HBM)
    y, dx, eu, ed, pj, ao, ci, co, lu, ld, eg, ag, cg, cn, lg, fg, cd = pl.pallas_call(
        finish_kernel,
        out_shape=[jax.ShapeDtypeStruct(y.shape, LOW)] * 2
        + [jax.ShapeDtypeStruct(shape, F32) for shape in widths],
        in_specs=[hbm] * 3,
        out_specs=[hbm] * 17,
        scratch_shapes=[
            pltpu.VMEM(y.shape, LOW),
            pltpu.VMEM(y.shape, LOW),
            pltpu.VMEM(g.shape, F32),
            pltpu.VMEM((32, 1536), F32),
        ]
        + [pltpu.VMEM(shape, F32) for shape in widths[8:]]
        + [pltpu.SemaphoreType.DMA((20,))],
        compiler_params=pltpu.CompilerParams(vmem_limit_bytes=62 * 2**20),
    )(y, dx, g)
    return (
        y[None, :, None],
        dx[None, :, None],
        eg,
        eu[None],
        ed.T[None],
        ag,
        pj[None],
        ao[None],
        cg,
        ci[None],
        cd[None],
        cn,
        co[None],
        lg,
        lu[None],
        ld.T[None],
        fg,
    )


def plain_kernel(groups, scalars, w, frames, cotangent, cos, sin, y_out, dx_out, g_out, *rest):
    n_acts, act_names, work_names, n = groups
    kept, rest = dict(zip(act_names, rest[:n_acts])), rest[n_acts:]
    acts, rest = dict(zip(act_names, rest[:n_acts])), rest[n_acts:]
    work, rest = dict(zip(work_names, rest[: len(work_names)])), rest[len(work_names) :]
    stage, sem = rest

    def move(source, target):
        copy = pltpu.make_async_copy(source, target, sem)
        copy.start()
        copy.wait()

    def emit(l, column, value):
        width = value.shape[1]
        stage[:, :width] = value.astype(LOW)
        move(stage.at[:, pl.ds(0, width)], g_out.at[l, :, pl.ds(column, width)])

    run = Layer({**acts, **work, "cos": cos, "sin": sin}, emit, lambda *_: None)

    def whole(*modules):
        for module in modules:
            for _ in module:
                pass

    move(frames, run.given.at[0])
    move(cotangent, run.given.at[1])
    run.prepare(scalars[0], scalars[1], scalars[2])
    run.stream[...] = run.given[0].astype(F32)
    for l in range(2):
        move(w.at[l], work["w"])
        run.small_forward(l)
        whole(
            run.feed_forward(l, 0, G_EARLY, 0, EU, ED),
            run.attend_forward(l),
            run.convolve_forward(l),
            run.feed_forward(l, 3, G_LATE, 3, LU, LD),
        )
        run.result[l] = run.finish_forward(l)
        run.stream[...] = run.result[l].astype(F32)
        if l == 0:
            for name in act_names:
                move(acts[name], kept[name])
    for l in (1, 0):
        if l == 0:
            move(w.at[0], work["w"])
            for name in act_names:
                move(kept[name], acts[name])
        start = run.given[1].astype(F32) if l == 1 else run.result_grad[1].astype(F32)
        run.grad[...] = run.leave(l, 4, G_FINAL, start)
        whole(
            run.feed_backward(l, 3, G_LATE, 3, LU, LD),
            run.convolve_backward(l),
            run.attend_backward(l),
            run.feed_backward(l, 0, G_EARLY, 0, EU, ED),
        )
        run.small_backward(l)
        run.result_grad[l] = run.grad[...].astype(LOW)
    move(run.result, y_out)
    move(run.result_grad, dx_out)


def plain(scalars, weights, frames, cotangent):
    n = frames.shape[0]
    acts, work = act_shapes(n), work_shapes(n)
    cosine, sine = tables(n)
    vmem = pl.BlockSpec(memory_space=pltpu.VMEM)
    hbm = pl.BlockSpec(memory_space=pl.ANY)
    outs = pl.pallas_call(
        functools.partial(plain_kernel, (len(acts), tuple(acts), tuple(work), n)),
        out_shape=[
            jax.ShapeDtypeStruct((2, n, 512), LOW),
            jax.ShapeDtypeStruct((2, n, 512), LOW),
            jax.ShapeDtypeStruct((2, 512, COLS), LOW),
        ]
        + [jax.ShapeDtypeStruct(shape, kind) for shape, kind in acts.values()],
        in_specs=[pl.BlockSpec(memory_space=pltpu.SMEM), hbm, hbm, hbm, vmem, vmem],
        out_specs=[hbm] * (3 + len(acts)),
        scratch_shapes=[pltpu.VMEM(shape, kind) for shape, kind in acts.values()]
        + list(work.values())
        + [pltpu.VMEM((512, STEP), LOW), pltpu.SemaphoreType.DMA],
        compiler_params=pltpu.CompilerParams(vmem_limit_bytes=60 * 2**20),
    )(scalars, weights, frames, cotangent, jnp.asarray(cosine), jnp.asarray(sine))
    return outs[:3]


def pack(shards):
    eg, eu, ed, ag, pj, ao, cg, ci, cd, cn, co, lg, lu, ld, fg = (piece[0] for piece in shards)
    rows = eu.shape[0]
    small = jnp.concatenate(
        [gain[:, None] for gain in (eg, ag, cg, cn, lg, fg)]
        + [cd.T, jnp.zeros((rows, 128 - 6 - KERNEL), LOW)],
        axis=1,
    )
    proj = jnp.concatenate([swap_halves(pj[:, :1024]), pj[:, 1024:]], axis=1)
    return jnp.concatenate([eu, ed.T, proj, ao, ci, co, lu, ld.T, small], axis=1)


def unpack(block):
    proj = block[:, PJ : PJ + 1536]
    proj = jnp.concatenate([swap_halves(proj[:, :1024], True), proj[:, 1024:]], axis=1)
    gains = [block[:, SM + i] for i in range(6)]
    eg, ag, cg, cn, lg, fg = gains
    outs = (
        eg,
        block[:, EU:ED],
        block[:, ED:PJ].T,
        ag,
        proj,
        block[:, AO:CI],
        cg,
        block[:, CI:CO],
        block[:, SM + TAPS : SM + TAPS + KERNEL].T,
        cn,
        block[:, CO:LU],
        lg,
        block[:, LU:LD],
        block[:, LD:SM].T,
        fg,
    )
    return tuple(piece[None] for piece in outs)


def turn_small(block):
    small = block[..., SM : SM + 32].reshape(2, len(OWNERS), 32, 32).swapaxes(2, 3)
    small = jnp.pad(small.reshape(2, 512, 32), ((0, 0), (0, 0), (0, 96)))
    return jnp.concatenate([block[..., :SM], small], axis=2)


def by_collectives(lengths, flags, spans, frames, cotangent, shards):
    section = lax.axis_index("pipe")

    def mine(block):
        return lax.dynamic_index_in_dim(block, section, 0, keepdims=False)

    full = lax.all_gather(pack(shards), ("pipe", "dp"), axis=0, tiled=True)
    full = turn_small(full.reshape(2, 512, COLS)).reshape(2, 4, 2, 2, 32, COLS)
    scalars = jnp.stack([mine(lengths)[0], mine(flags)[0], mine(spans)[0]])
    ys, dxs, grads = plain(scalars, full, mine(frames), mine(cotangent))
    summed = lax.psum_scatter(
        turn_small(grads).reshape(1024, COLS), ("pipe", "dp"), scatter_dimension=0, tiled=True
    ).astype(F32)

    def share(pair):
        own, other = mine(pair), jnp.where(section == 0, pair[1], pair[0])
        got = lax.ppermute(other, "pipe", [(0, 1), (1, 0)])
        pair = jnp.where(section == 0, jnp.stack([own, got]), jnp.stack([got, own]))
        return pair[None, :, None]

    return (share(ys), share(dxs)) + unpack(summed)


def body(frames, cotangent, lengths, stream_flags, span_sizes, *shards):
    run = fused if lax.axis_size("dp") == 16 else by_collectives
    return run(lengths, stream_flags, span_sizes, frames[:, 0], cotangent[:, 0], shards)


def solution(mesh):
    gain, matrix, column = P("pipe", "dp"), P("pipe", "dp", None), P("pipe", None, "dp")
    weights = (gain, matrix, column, gain, matrix, matrix, gain, matrix, column, gain, matrix)
    weights = weights + (gain, matrix, column, gain)
    frames, stacked = P(None, "dp", None, None), P("pipe", None, "dp", None, None)
    return jax.shard_map(
        body,
        mesh=mesh,
        in_specs=(frames, frames) + (P(None, "dp"),) * 3 + weights,
        out_specs=(stacked, stacked) + weights,
        check_vma=False,
    )
```
